32 devices in a mesh: gy: 4 (over y, x), gx: 8 (over z, core).
Axes of the slice: x: 2, y: 2, z: 4, core: 2. Of those that a mesh axis runs over, the one named last changes fastest.
Arguments:
- tokens: bfloat16 [8192, 1152], P(('gy', 'gx')), may hold values from -6 to 6
- text_states: bfloat16 [512, 4096], P(('gy', 'gx')), may hold values from -6 to 6
- pooled_text: float32 [4, 1152], replicated, may hold values from -5 to 5
- timesteps: int32 [4], replicated, may hold values from 0 to 999
- frame_counts: int32 [4], replicated, may hold values from 1 to 3, as said below
- still_clips: int32 [4], replicated, may hold values from 0 to 1, as said below
- text_lengths: int32 [4], replicated, may hold values from 16 to 128, as said below
- w_ada: bfloat16 [1152, 10368], P('gy', 'gx'), may hold values from -0.1875 to 0.1875
- w_sqkv: bfloat16 [1152, 3456], P('gy', 'gx'), may hold values from -0.1875 to 0.1875
- w_sout: bfloat16 [1152, 1152], P('gy', 'gx'), may hold values from -1.5 to 1.5
- w_cq: bfloat16 [1152, 1152], P('gy', 'gx'), may hold values from -0.1875 to 0.1875
- w_ckv: bfloat16 [4096, 2304], P('gy', 'gx'), may hold values from -0.09375 to 0.09375
- w_cout: bfloat16 [1152, 1152], P('gy', 'gx'), may hold values from -0.75 to 0.75
- w_up: bfloat16 [1152, 4608], P('gy', 'gx'), may hold values from -0.1875 to 0.1875
- w_down: bfloat16 [4608, 1152], P('gy', 'gx'), may hold values from -0.09375 to 0.09375
- w_tqkv: bfloat16 [1152, 3456], P('gy', 'gx'), may hold values from -0.1875 to 0.1875
- w_tout: bfloat16 [1152, 1152], P('gy', 'gx'), may hold values from -0.375 to 0.375
- grad_out: bfloat16 [8192, 1152], P(('gy', 'gx')), may hold values from -6 to 6
Outputs:
- mixed: bfloat16 [8192, 1152], P(('gy', 'gx'))
- grad_tokens: bfloat16 [8192, 1152], P(('gy', 'gx'))
- grad_ada: float32 [1152, 10368], P('gy', 'gx')
- grad_sqkv: float32 [1152, 3456], P('gy', 'gx')
- grad_sout: float32 [1152, 1152], P('gy', 'gx')
- grad_cq: float32 [1152, 1152], P('gy', 'gx')
- grad_ckv: float32 [4096, 2304], P('gy', 'gx')
- grad_cout: float32 [1152, 1152], P('gy', 'gx')
- grad_up: float32 [1152, 4608], P('gy', 'gx')
- grad_down: float32 [4608, 1152], P('gy', 'gx')
- grad_tqkv: float32 [1152, 3456], P('gy', 'gx')
- grad_tout: float32 [1152, 1152], P('gy', 'gx')
The draws below stay inside these ranges and needn't reach their ends.
Inputs may be any that keep to these rules, and one draw needn't show every extreme that they name: `frame_counts`: they sum to 8; at least one clip, drawn from the seed, has 3 frames. `still_clips`: exactly two of the 4 clips are marked. `text_lengths`: some clip has all 128 slots live.
All inputs are finite; a program needn't handle non-finite values.
Results may differ from the reference program's by a relative error of at most 0.025.
Values may be sent and summed in bfloat16 or wider, within the bound.
No kernel may reach another device: no remote copies, remote signals or barrier semaphores. Data moves between devices by JAX's collectives and lax.ppermute only.
A program may use at most 384 MiB of HBM per device.

```python
import math
import jax
import jax.numpy as jnp
from jax import lax

D = 1152
HEADS = 16
HEAD_DIM = 72
FF = 4608
TD = 4096
FRAME = 1024
CLIPS = 4
LTEXT = 128
TOKENS = 8192
FRAMES = 8
MOST = 3
TEXT_ROWS = 512


def draw_frame_counts(key, part):
    key = jax.random.fold_in(key, 5)
    key_place, key_fill = jax.random.split(key)
    other_clips = CLIPS - 1

    def add_frame(step, counts):
        order = jax.random.permutation(jax.random.fold_in(key_fill, step), other_clips)
        room = (counts < MOST).astype(jnp.int32)
        chosen = jnp.argmax(room * (other_clips + 1) + order)
        return counts + (jnp.arange(other_clips) == chosen).astype(jnp.int32)
    counts = lax.fori_loop(0, FRAMES - MOST - other_clips, add_frame, jnp.ones((other_clips,), jnp.int32))
    place = jax.random.randint(key_place, (), 0, CLIPS)
    index = jnp.arange(CLIPS)
    source = jnp.clip(jnp.where(index < place, index, index - 1), 0, other_clips - 1)
    return jnp.where(index == place, MOST, counts[source]).astype(jnp.int32)


def draw_still_clips(key, part):
    key = jax.random.fold_in(key, 41)
    shuffled = jax.random.permutation(key, CLIPS)
    return (shuffled < 2).astype(jnp.int32)


def draw_text_lengths(key, part):
    key = jax.random.fold_in(key, 23)
    key_lengths, key_longest = jax.random.split(key)
    drawn = jax.random.randint(key_lengths, (CLIPS,), LTEXT // 8, LTEXT + 1)
    longest = jax.random.randint(key_longest, (), 0, CLIPS)
    return jnp.where(jnp.arange(CLIPS) == longest, LTEXT, drawn).astype(jnp.int32)


def place_ends(entries, stream_key, low, high):
    extent = entries.shape
    spot = [jax.random.randint(jax.random.fold_in(stream_key, axis), (), 0, extent[axis]) for axis in range(len(extent))]
    entries = entries.at[tuple(spot)].set(low)
    longest = extent.index(max(extent))
    spot[longest] = (spot[longest] + 1) % extent[longest]
    return entries.at[tuple(spot)].set(high)


def levels(stream_key, extent, shards, low, top_value):
    def one(axis_at, blocks):
        heights = jax.random.uniform(jax.random.fold_in(jax.random.fold_in(stream_key, 6), axis_at), (blocks,), jnp.float32, low / len(shards), top_value / len(shards))
        return jnp.repeat(jnp.exp(heights), extent[axis_at] // blocks).reshape((-1,) + (1,) * (len(extent) - axis_at - 1))

    factor_of = one(*shards[0])
    for cut in shards[1:]:
        factor_of = factor_of * one(*cut)
    return factor_of


def gaussian(rng, shape, width, bound, cuts=(), kind=jnp.bfloat16):
    values = jax.random.normal(rng, shape, jnp.float32) * width
    if len(cuts) > 0:
        values = levels(rng, shape, cuts, -0.22, 0.18) * values
    return jnp.clip(values, min=-bound, max=bound).astype(kind)


def setup_inputs(seed: int = 0) -> dict:
    streams_of = jax.random.split(jax.random.key(seed), 19)
    return {
        "tokens": gaussian(streams_of[0], (TOKENS, D), 1.0, 6.0, ((0, 32),)),
        "text_states": gaussian(streams_of[1], (TEXT_ROWS, TD), 1.0, 6.0, ((0, 32),)),
        "pooled_text": gaussian(streams_of[2], (CLIPS, D), 1.0, 5.0, (), jnp.float32),
        "timesteps": place_ends(jax.random.randint(streams_of[3], (CLIPS,), 0, 1000), jax.random.fold_in(streams_of[3], 1), 0, 999).astype(jnp.int32),
        "frame_counts": draw_frame_counts(jax.random.fold_in(streams_of[18], 71), 0),
        "still_clips": draw_still_clips(jax.random.fold_in(streams_of[18], 71), 0),
        "text_lengths": draw_text_lengths(jax.random.fold_in(streams_of[18], 71), 0),
        "w_ada": gaussian(streams_of[7], (D, 9 * D), D ** -0.5, 0.1875, ((0, 4), (1, 8))),
        "w_sqkv": gaussian(streams_of[8], (D, 3 * D), D ** -0.5, 0.1875, ((0, 4), (1, 8))),
        "w_sout": gaussian(streams_of[9], (D, D), (max(D // 64, 1)) ** -0.5, 1.5, ((0, 4), (1, 8))),
        "w_cq": gaussian(streams_of[10], (D, D), D ** -0.5, 0.1875, ((0, 4), (1, 8))),
        "w_ckv": gaussian(streams_of[11], (TD, 2 * D), TD ** -0.5, 0.09375, ((0, 4), (1, 8))),
        "w_cout": gaussian(streams_of[12], (D, D), (max(D // 16, 1)) ** -0.5, 0.75, ((0, 4), (1, 8))),
        "w_up": gaussian(streams_of[13], (D, FF), D ** -0.5, 0.1875, ((0, 4), (1, 8))),
        "w_down": gaussian(streams_of[14], (FF, D), FF ** -0.5, 0.09375, ((0, 4), (1, 8))),
        "w_tqkv": gaussian(streams_of[15], (D, 3 * D), D ** -0.5, 0.1875, ((0, 4), (1, 8))),
        "w_tout": gaussian(streams_of[16], (D, D), (max(D // 4, 1)) ** -0.5, 0.375, ((0, 4), (1, 8))),
        "grad_out": gaussian(streams_of[17], (TOKENS, D), 1.0, 6.0, ((0, 32),)),
    }


@jax.custom_vjp
def low(v):
    return lax.optimization_barrier(v.astype(jnp.bfloat16)).astype(jnp.float32)

@jax.custom_vjp
def low_back(v):
    return v

def low_keep(v):
    return (low(v), None)

def low_pass(kept, grad):
    return (grad,)

def back_keep(v):
    return (v, None)

def back_low(kept, grad):
    return (low(grad),)
low.defvjp(low_keep, low_pass)
low_back.defvjp(back_keep, back_low)
norm_eps = 1e-06
masked_score = -1e+30
highest = lax.Precision.HIGHEST

def layer_norm(values):
    centred = values - lax.optimization_barrier(jnp.mean(values, axis=-1, keepdims=True))
    return centred * lax.rsqrt(lax.optimization_barrier(jnp.mean(centred * centred, axis=-1, keepdims=True)) + norm_eps)

def condition(timesteps, pooled_text):
    half_width = D // 2
    frequency = jnp.exp(-math.log(10000.0) * jnp.arange(half_width).astype(jnp.float32) / half_width)
    angles = timesteps.astype(jnp.float32)[:, None] * frequency[None, :]
    embedded = jnp.concatenate([jnp.cos(angles), jnp.sin(angles)], axis=1)
    return jax.nn.silu(embedded + pooled_text)

def split_heads(values):
    return values.reshape(values.shape[:-1] + (HEADS, HEAD_DIM))

def attend(queries, keys, values, key_ok):
    scores = jnp.einsum('qbhd,kbhd->bhqk', split_heads(queries), split_heads(keys), precision=highest)
    scores = low_back(scores * HEAD_DIM ** (-0.5))
    scores = jnp.where(key_ok, scores, masked_score)
    probs = jax.nn.softmax(scores, axis=-1)
    output = jnp.einsum('bhqk,kbhd->qbhd', low(probs), split_heads(values), precision=highest)
    return low(low_back(output.reshape(queries.shape)))

def reference(tokens, text_states, pooled_text, timesteps, frame_counts, still_clips, text_lengths, w_ada, w_sqkv, w_sout, w_cq, w_ckv, w_cout, w_up, w_down, w_tqkv, w_tout, grad_out):
    clip_ends = jnp.cumsum(frame_counts)
    frame_clip = lax.optimization_barrier(jnp.sum((clip_ends[None, :] <= jnp.arange(FRAMES)[:, None]).astype(jnp.int32), axis=1))
    clip_pick = (frame_clip[:, None] == jnp.arange(CLIPS)[None, :]).astype(jnp.float32)
    keep_frame = jnp.dot(clip_pick, (1 - still_clips).astype(jnp.float32), precision=highest)
    row_clip = jnp.arange(TEXT_ROWS) % CLIPS
    row_slot = jnp.arange(TEXT_ROWS) // CLIPS
    row_live = row_slot < text_lengths[row_clip]
    text_ok = (row_clip[None, :] == frame_clip[:, None]) & row_live[None, :]
    time_ok = (frame_clip[:, None] == frame_clip[None, :])[None, None]
    cond = condition(timesteps, pooled_text)
    text_float = text_states.astype(jnp.float32)

    def forward(inputs, weights):
        ada, sqkv, sout, cq, ckv, cout, up_w, down_w, tqkv, tout = weights
        modulation = jnp.dot(cond, ada, precision=highest).reshape(CLIPS, 9, D)
        frame_mod = jnp.einsum('fc,cjd->fjd', clip_pick, modulation, precision=highest)
        text_pairs = low(low_back(jnp.dot(text_float, ckv, precision=highest)))

        def frame_step(packed):
            frame_x, mods, frame_text_ok = packed
            hidden_a = low(layer_norm(frame_x) * (1.0 + mods[1]) + mods[0])
            qkv_a = low(low_back(jnp.dot(hidden_a, sqkv, precision=highest)))
            out_a = attend(qkv_a[:, None, :D], qkv_a[:, None, D:2 * D], qkv_a[:, None, 2 * D:], True)[:, 0]
            after_a = frame_x + mods[2] * low_back(jnp.dot(out_a, sout, precision=highest))
            hidden_b = low(layer_norm(after_a))
            query_b = low(low_back(jnp.dot(hidden_b, cq, precision=highest)))
            out_b = attend(query_b[:, None], text_pairs[:, None, :D], text_pairs[:, None, D:], frame_text_ok[None, None, None, :])[:, 0]
            after_b = after_a + low_back(jnp.dot(out_b, cout, precision=highest))
            hidden_c = low(layer_norm(after_b) * (1.0 + mods[4]) + mods[3])
            pre_act = low_back(jnp.dot(hidden_c, up_w, precision=highest))
            activated = low(jax.nn.gelu(pre_act))
            return after_b + mods[5] * low_back(jnp.dot(activated, down_w, precision=highest))
        after_c = lax.map(jax.checkpoint(frame_step), (inputs.reshape(FRAMES, FRAME, D), frame_mod, text_ok))
        hidden_d = low(low_back(layer_norm(after_c) * (1.0 + frame_mod[:, None, 7]) + frame_mod[:, None, 6]))
        qkv_d = low(low_back(jnp.dot(hidden_d, tqkv, precision=highest)))
        out_d = attend(qkv_d[..., :D], qkv_d[..., D:2 * D], qkv_d[..., 2 * D:], time_ok)
        branch_d = low(low_back(jnp.dot(out_d, tout, precision=highest)))
        result = after_c + keep_frame[:, None, None] * frame_mod[:, None, 8] * branch_d
        return result.reshape(TOKENS, D)
    weights = (w_ada, w_sqkv, w_sout, w_cq, w_ckv, w_cout, w_up, w_down, w_tqkv, w_tout)
    weights = tuple((item.astype(jnp.float32) for item in weights))
    result, pullback = jax.vjp(forward, tokens.astype(jnp.float32), weights)
    grad_inputs, grad_weights = pullback(grad_out.astype(jnp.float32))
    return (result.astype(jnp.bfloat16), grad_inputs.astype(jnp.bfloat16), grad_weights[0], grad_weights[1], grad_weights[2], grad_weights[3], grad_weights[4], grad_weights[5], grad_weights[6], grad_weights[7], grad_weights[8], grad_weights[9])
```

```python
import functools
import math

import jax
import jax.numpy as jnp
from jax import lax
from jax.experimental import pallas as pl
from jax.experimental.pallas import tpu as pltpu
from jax.sharding import PartitionSpec as P

D = 1152
HEADS = 16
HEAD_DIM = 72
FRAME = 1024
CLIPS = 4

norm_eps = 1e-06
masked_score = -1e30
highest = lax.Precision.HIGHEST
f32 = jnp.float32
bf16 = jnp.bfloat16
score_scale = HEAD_DIM ** (-0.5)
log2_scale = score_scale * math.log2(math.e)
row_axes = ("gy", "gx")
col_axes = ("gx", "gy")
nt = (((1,), (1,)), ((), ()))


def vmem():
    return pl.BlockSpec(memory_space=pltpu.VMEM)


def smem():
    return pl.BlockSpec(memory_space=pltpu.SMEM)


def hbm():
    return pl.BlockSpec(memory_space=pl.ANY)


def shape(*size, dtype=f32):
    return jax.ShapeDtypeStruct(size, dtype)


def run(kernel, outs, specs, scratch, args, flops, moved):
    return pl.pallas_call(
        kernel,
        out_shape=outs,
        in_specs=specs,
        out_specs=[vmem() for _ in outs],
        scratch_shapes=scratch,
        compiler_params=pltpu.CompilerParams(vmem_limit_bytes=56 << 20),
        cost_estimate=pl.CostEstimate(flops=flops, bytes_accessed=moved, transcendentals=0),
    )(*args)


class Window:
    def __init__(self, lo, hi):
        self.lo, self.hi = lo, hi
        self.start = lo // 128 * 128
        self.stop = -(-hi // 128) * 128
        self.off = lo - self.start
        self.n = hi - lo
        self.width = self.stop - self.start

    def inside(self, outer):
        return Window(self.lo - outer.start, self.hi - outer.start)


def padded(lanes):
    return -(-lanes // 128) * 128


def block_copies(source, window, buffer, sems, count):
    return [
        pltpu.make_async_copy(
            source.at[i, :, window.start : window.stop], buffer.at[i], sems.at[i]
        )
        for i in range(count)
    ]


def stats(values):
    centred = values - jnp.mean(values, axis=-1, keepdims=True)
    inv_std = lax.rsqrt(jnp.mean(centred * centred, axis=-1, keepdims=True) + norm_eps)
    return centred * inv_std, inv_std


def stats_back(grad_norm, normed, inv_std):
    return inv_std * (
        grad_norm
        - jnp.mean(grad_norm, axis=-1, keepdims=True)
        - normed * jnp.mean(grad_norm * normed, axis=-1, keepdims=True)
    )


def mm(left, right):
    return jnp.dot(left, right, preferred_element_type=f32)


def mm_nt(left, right):
    return lax.dot_general(left, right, nt, preferred_element_type=f32)


def put(dests, start, value):
    base, width = 0, value.shape[1]
    for ref in dests:
        size = ref.shape[1]
        lo, hi = max(start, base), min(start + width, base + size)
        if lo < hi:
            ref[:, lo - base : hi - base] = value[:, lo - start : hi - start].astype(ref.dtype)
        base += size


def take(pad, off, sources, start, width):
    base = 0
    for ref in sources:
        size = ref.shape[1]
        lo, hi = max(start, base), min(start + width, base + size)
        if lo < hi:
            pad[:, off + lo - start : off + hi - start] = ref[:, lo - base : hi - base]
        base += size


def head(h):
    return slice(h * HEAD_DIM, (h + 1) * HEAD_DIM)


def gelu_parts(u):
    c = math.sqrt(2.0 / math.pi)
    square = u * u
    return jnp.tanh(c * u * (1.0 + 0.044715 * square)), square, c


def qkv_kernel(win, nx, x_ref, mod_ref, w_ref, h_ref, q_ref, kv_ref, buf, sems):
    copies = block_copies(w_ref, win, buf, sems, nx)
    for copy in copies:
        copy.start()
    normed, _ = stats(x_ref[...].astype(f32))
    hidden = (normed * (1.0 + mod_ref[1:2, :]) + mod_ref[0:1, :]).astype(bf16)
    h_ref[...] = hidden
    for x in range(nx):
        copies[x].wait()
        block = mm(hidden, buf[x])[:, win.off : win.off + win.n]
        put([q_ref, kv_ref], x * win.n, block)


def stage_heads(dest, row, source, start):
    rows = source.shape[0]
    for h in range(HEADS):
        dest[h, row : row + rows, :HEAD_DIM] = source[
            :, start + h * HEAD_DIM : start + (h + 1) * HEAD_DIM
        ]


def spatial_kernel(pieces, *refs):
    q_ref = refs[0]
    kv_refs = refs[1 : 1 + pieces]
    o_ref, lse_ref, q_t, v_t, k_heads, o_t = refs[1 + pieces :]
    rows = q_ref.shape[0]
    q_t[...] = q_ref[...].astype(f32).T
    for i, kv in enumerate(kv_refs):
        v_t[:, i * rows : (i + 1) * rows] = kv[:, D:].astype(f32).T
        stage_heads(k_heads, i * rows, kv, 0)

    def one_head(h, carry):
        span = pl.ds(pl.multiple_of(h * HEAD_DIM, 8), HEAD_DIM)
        scores = mm(k_heads[h, :, :HEAD_DIM], q_t[span, :].astype(bf16)) * log2_scale
        top = jnp.max(scores, axis=0, keepdims=True)
        weights = jnp.exp2(scores - top)
        total = jnp.sum(weights, axis=0, keepdims=True)
        o_t[span, :] = mm(v_t[span, :].astype(bf16), weights.astype(bf16)) / total
        lse_ref[pl.ds(h, 1), :] = top + jnp.log2(total)
        return carry

    lax.fori_loop(0, HEADS, one_head, 0)
    o_ref[...] = o_t[...].T.astype(bf16)


def text_probs(text_ref, q_t, h, length):
    scores = mm(text_ref[:, head(h)], q_t[head(h), :].astype(bf16)) * score_scale
    slot = lax.broadcasted_iota(jnp.int32, scores.shape, 0)
    scores = jnp.where(slot < length, scores, masked_score)
    weights = jnp.exp(scores - jnp.max(scores, axis=0, keepdims=True))
    return weights / jnp.sum(weights, axis=0, keepdims=True)


def text_kernel(
    outer, w_out, w_cq, w_cout, nx, x_ref, o_ref, mod_ref, w_ref, text_ref, length_ref,
    a1_ref, x1_ref, hc_ref, qc_ref, oc_ref, x2_ref, h3_ref,
    buf, sems, acc, q_t, v_t,
):
    copies = block_copies(w_ref, outer, buf, sems, nx)
    for copy in copies:
        copy.start()

    def product(left, win, dest, wait=False):
        for x in range(nx):
            if wait:
                copies[x].wait()
            block = mm(left, buf[x, :, win.start : win.stop])[:, win.off : win.off + win.n]
            put([dest], x * win.n, block)

    product(o_ref[...], w_out, a1_ref, wait=True)
    after_a = x_ref[...].astype(f32) + mod_ref[2:3, :] * a1_ref[...]
    x1_ref[...] = after_a
    hidden = stats(after_a)[0].astype(bf16)
    hc_ref[...] = hidden
    product(hidden, w_cq, qc_ref)
    q_t[...] = qc_ref[...].astype(f32).T
    v_t[...] = text_ref[:, D:].astype(f32).T
    length = length_ref[0]
    for h in range(HEADS):
        probs = text_probs(text_ref, q_t, h, length).astype(bf16)
        acc[head(h), :] = mm(v_t[head(h), :].astype(bf16), probs)
    oc_ref[...] = acc[...].T.astype(bf16)
    product(oc_ref[...], w_cout, x2_ref)
    after_b = x1_ref[...] + x2_ref[...]
    x2_ref[...] = after_b
    h3_ref[...] = (
        stats(after_b)[0] * (1.0 + mod_ref[4:5, :]) + mod_ref[3:4, :]
    ).astype(bf16)


def ff_kernel(
    win, nx, ny, h_ref, x2_ref, mod_ref, up_ref, down_ref,
    u_ref, g_ref, m_ref, x3_ref, h4_ref, up_buf, down_buf, up_sems, down_sems,
):
    ups = block_copies(up_ref, win, up_buf, up_sems, nx)
    width = down_ref.shape[2]
    downs = block_copies(down_ref, Window(0, width), down_buf, down_sems, ny)
    for copy in ups + downs:
        copy.start()
    hidden = h_ref[...]
    for x in range(nx):
        ups[x].wait()
        u = mm(hidden, up_buf[x])[:, win.off : win.off + win.n]
        put([u_ref], x * win.n, u)
        put([g_ref], x * win.n, 0.5 * u * (1.0 + gelu_parts(u)[0]))
    total = jnp.zeros(m_ref.shape, f32)
    for i in range(ny):
        downs[i].wait()
        total = total + mm_nt(g_ref[:, i * width : (i + 1) * width], down_buf[i])
    m_ref[...] = total
    after_c = x2_ref[...] + mod_ref[5:6, :] * total
    x3_ref[...] = after_c
    h4_ref[...] = (
        stats(after_c)[0] * (1.0 + mod_ref[7:8, :]) + mod_ref[6:7, :]
    ).astype(bf16)


def early_kernel(win, nx, g_ref, mod_ref, keep_ref, w_ref, da_ref, do_ref, buf, pad, sems):
    copies = block_copies(w_ref, win, buf, sems, nx)
    for copy in copies:
        copy.start()
    da_ref[...] = (keep_ref[0] * mod_ref[8:9, :] * g_ref[...].astype(f32)).astype(bf16)
    pad[...] = jnp.zeros(pad.shape, bf16)
    total = jnp.zeros(g_ref.shape, f32)
    for x in range(nx):
        copies[x].wait()
        take(pad, win.off, [da_ref], x * win.n, win.n)
        total = total + mm_nt(pad[...], buf[x])
    do_ref[...] = total.astype(bf16)


def temporal_kernel(
    win, nx, frames, h_ref, do_in, w_ref, row_clip, frame_clip,
    o_ref, dqkv_ref, dh_ref, buf, sems, pad, q_s, k_s, v_s, do_s, o_s, dq_s, dk_s, dv_s, qkv_s,
):
    copies = block_copies(w_ref, win, buf, sems, nx)
    for copy in copies:
        copy.start()
    rows = h_ref.shape[0]
    spots = rows // frames
    hidden = h_ref[...]
    for x in range(nx):
        copies[x].wait()
        block = mm(hidden, buf[x])[:, win.off : win.off + win.n]
        put([qkv_s], x * win.n, block)
    q_s[...] = qkv_s[:, :D].astype(f32)
    k_s[...] = qkv_s[:, D : 2 * D].astype(f32)
    v_s[...] = qkv_s[:, 2 * D :].astype(f32)
    do_s[...] = do_in[...].astype(f32)
    dk_s[...] = jnp.zeros(dk_s.shape, f32)
    dv_s[...] = jnp.zeros(dv_s.shape, f32)

    def one_hot(size, feature, slot):
        first = lax.broadcasted_iota(jnp.int32, size, slot) * HEAD_DIM
        place = lax.broadcasted_iota(jnp.int32, size, feature)
        return jnp.where((place >= first) & (place < first + HEAD_DIM), 1.0, 0.0).astype(bf16)

    gather = one_hot((D, 128), 0, 1)
    spread = one_hot((128, D), 1, 0)

    def per_head(values):
        high = values.astype(bf16)
        low = (values - high.astype(f32)).astype(bf16)
        return mm(high, gather) + mm(low, gather)

    def every_frame(values):
        return jnp.broadcast_to(values[None], (frames, spots, D)).reshape(rows, D)

    def over_frames(values):
        return jnp.sum(values.reshape(frames, spots, values.shape[-1]), axis=0)

    def one_frame(f, carry):
        span = pl.ds(pl.multiple_of(f * spots, 8), spots)
        queries = every_frame(q_s[span, :])
        grads = every_frame(do_s[span, :])
        scores = per_head(queries * k_s[...]) * score_scale
        scores = jnp.where(row_clip[...] == frame_clip[f], scores, masked_score)
        scores = scores.reshape(frames, spots, 128)
        weights = jnp.exp(scores - jnp.max(scores, axis=0, keepdims=True))
        probs = weights / jnp.sum(weights, axis=0, keepdims=True)
        grad_probs = per_head(grads * v_s[...]).reshape(frames, spots, 128)
        inner = jnp.sum(probs * grad_probs, axis=0, keepdims=True)
        grad_scores = (probs * (grad_probs - inner)).reshape(rows, 128).astype(bf16)
        probs_wide = mm(probs.reshape(rows, 128).astype(bf16), spread)
        grads_wide = mm(grad_scores, spread)
        o_s[span, :] = over_frames(probs_wide * v_s[...])
        dq_s[span, :] = over_frames(grads_wide * k_s[...]) * score_scale
        dk_s[...] += grads_wide * queries
        dv_s[...] += probs_wide * grads
        return carry

    lax.fori_loop(0, frames, one_frame, 0)
    o_ref[...] = o_s[...].astype(bf16)
    dqkv_ref[:, :D] = dq_s[...].astype(bf16)
    dqkv_ref[:, D : 2 * D] = (dk_s[...] * score_scale).astype(bf16)
    dqkv_ref[:, 2 * D :] = dv_s[...].astype(bf16)
    pad[...] = jnp.zeros(pad.shape, bf16)
    total = jnp.zeros(dh_ref.shape, f32)
    for x in range(nx):
        take(pad, win.off, [dqkv_ref], x * win.n, win.n)
        total = total + mm_nt(pad[...], buf[x])
    dh_ref[...] = total.astype(bf16)


def mixed_kernel(
    win, nx, o_ref, x3_ref, g_ref, mod_ref, keep_ref, w_ref, y_ref, gate_ref, buf, sems, acc
):
    copies = block_copies(w_ref, win, buf, sems, nx)
    for copy in copies:
        copy.start()
    for x in range(nx):
        copies[x].wait()
        put([acc], x * win.n, mm(o_ref[...], buf[x])[:, win.off : win.off + win.n])
    branch = acc[...].astype(bf16).astype(f32)
    keep = keep_ref[0]
    y_ref[...] = (x3_ref[...] + keep * mod_ref[8:9, :] * branch).astype(bf16)
    gate_ref[...] = jnp.sum(keep * g_ref[...].astype(f32) * branch, axis=0, keepdims=True)


def column_sum(values):
    return jnp.sum(values, axis=0, keepdims=True)


def ff_back_kernel(
    win, nx, ny, g_ref, dh4_ref, x3_ref, x2_ref, u_ref, m_ref, mod_ref, up_ref, down_ref,
    dm_ref, du_ref, dx2_ref, sum_ref, up_buf, down_buf, up_sems, down_sems, du_s, pad,
):
    width = down_ref.shape[2]
    downs = block_copies(down_ref, Window(0, width), down_buf, down_sems, ny)
    ups = block_copies(up_ref, win, up_buf, up_sems, nx)
    for copy in downs + ups:
        copy.start()
    dh4 = dh4_ref[...].astype(f32)
    normed, inv_std = stats(x3_ref[...])
    dx3 = g_ref[...].astype(f32) + stats_back(dh4 * (1.0 + mod_ref[7:8, :]), normed, inv_std)
    sum_ref[0:1, :] = column_sum(dh4)
    sum_ref[1:2, :] = column_sum(dh4 * normed)
    sum_ref[2:3, :] = column_sum(dx3 * m_ref[...])
    dm = (mod_ref[5:6, :] * dx3).astype(bf16)
    dm_ref[...] = dm
    for i in range(ny):
        downs[i].wait()
        grad = mm(dm, down_buf[i])
        u = u_ref[:, i * width : (i + 1) * width]
        tanh, square, c = gelu_parts(u)
        slope = 0.5 * (1.0 + tanh) + 0.5 * u * (1.0 - tanh * tanh) * (
            c * (1.0 + 3.0 * 0.044715 * square)
        )
        du_s[:, i * width : (i + 1) * width] = (grad * slope).astype(bf16)
    pad[...] = jnp.zeros(pad.shape, bf16)
    total = jnp.zeros(dx2_ref.shape, f32)
    for x in range(nx):
        ups[x].wait()
        take(pad, win.off, [du_s], x * win.n, win.n)
        du_ref[x] = pad[:, win.off : win.off + win.n]
        total = total + mm_nt(pad[...], up_buf[x])
    normed, inv_std = stats(x2_ref[...])
    sum_ref[3:4, :] = column_sum(total)
    sum_ref[4:5, :] = column_sum(total * normed)
    sum_ref[5:8, :] = jnp.zeros((3, D), f32)
    dx2_ref[...] = dx3 + stats_back(total * (1.0 + mod_ref[4:5, :]), normed, inv_std)


def text_back_kernel(
    outer, w_out, w_cq, w_cout, nx, dx2_ref, x1_ref, a1_ref, mod_ref, w_ref, qc_ref, text_ref,
    length_ref, dac_ref, dqc_ref, dx1_ref, da1_ref, do1_ref, dtext_ref, gate_ref,
    buf, sems, pad, acc, q_t, do_t, k_t, do_s, dtext_s,
):
    copies = block_copies(w_ref, outer, buf, sems, nx)
    for copy in copies:
        copy.start()

    def product(source, win, wait=False):
        pad[...] = jnp.zeros(pad.shape, bf16)
        total = jnp.zeros(dx2_ref.shape, f32)
        for x in range(nx):
            if wait:
                copies[x].wait()
            take(pad, win.off, [source], x * win.n, win.n)
            total = total + mm_nt(pad[:, : win.width], buf[x, :, win.start : win.stop])
        return total

    dx2 = dx2_ref[...]
    dac_ref[...] = dx2.astype(bf16)
    grad_o = product(dac_ref, w_cout, wait=True).astype(bf16)
    do_s[...] = grad_o
    do_t[...] = grad_o.astype(f32).T
    q_t[...] = qc_ref[...].astype(f32).T
    k_t[...] = text_ref[:, :D].astype(f32).T
    length = length_ref[0]
    for h in range(HEADS):
        probs = text_probs(text_ref, q_t, h, length)
        values = text_ref[:, D + h * HEAD_DIM : D + (h + 1) * HEAD_DIM]
        grad_probs = mm(values, do_t[head(h), :].astype(bf16))
        inner = jnp.sum(probs * grad_probs, axis=0, keepdims=True)
        grad_scores = (probs * (grad_probs - inner)).astype(bf16)
        dtext_s[:, head(h)] = mm(grad_scores, qc_ref[:, head(h)]) * score_scale
        dtext_s[:, D + h * HEAD_DIM : D + (h + 1) * HEAD_DIM] = mm(
            probs.astype(bf16), do_s[:, head(h)]
        )
        acc[head(h), :] = mm(k_t[head(h), :].astype(bf16), grad_scores) * score_scale
    width = dtext_ref.shape[2]
    for x in range(nx):
        dtext_ref[x] = dtext_s[:, x * width : (x + 1) * width].astype(bf16)
    dqc_ref[...] = acc[...].T.astype(bf16)
    normed, inv_std = stats(x1_ref[...])
    dx1 = dx2 + stats_back(product(dqc_ref, w_cq), normed, inv_std)
    dx1_ref[...] = dx1
    gate_ref[...] = column_sum(dx1 * a1_ref[...])
    da1_ref[...] = (mod_ref[2:3, :] * dx1).astype(bf16)
    do1_ref[...] = product(da1_ref, w_out).astype(bf16)


def spatial_back_kernel(pieces, *refs):
    q_ref, do_ref, o_ref, lse_ref = refs[:4]
    kv_refs = refs[4 : 4 + pieces]
    (
        dq_ref, dkv_ref,
        q_t, do_t, o_t, k_t, dq_t, q_heads, do_heads, k_heads, v_heads, dk_heads, dv_heads,
    ) = refs[4 + pieces :]
    rows = q_ref.shape[0]
    q_t[...] = q_ref[...].astype(f32).T
    do_t[...] = do_ref[...].astype(f32).T
    o_t[...] = o_ref[...].astype(f32).T
    stage_heads(q_heads, 0, q_ref, 0)
    stage_heads(do_heads, 0, do_ref, 0)
    for i, kv in enumerate(kv_refs):
        k_t[:, i * rows : (i + 1) * rows] = kv[:, :D].astype(f32).T
        stage_heads(k_heads, i * rows, kv, 0)
        stage_heads(v_heads, i * rows, kv, D)

    def one_head(h, carry):
        span = pl.ds(pl.multiple_of(h * HEAD_DIM, 8), HEAD_DIM)
        grad_o = do_t[span, :]
        inner = jnp.sum(grad_o * o_t[span, :], axis=0, keepdims=True)
        scores = mm(k_heads[h, :, :HEAD_DIM], q_t[span, :].astype(bf16)) * log2_scale
        probs = jnp.exp2(scores - lse_ref[pl.ds(h, 1), :])
        grad_probs = mm(v_heads[h, :, :HEAD_DIM], grad_o.astype(bf16))
        grad_scores = (probs * (grad_probs - inner)).astype(bf16)
        dv_heads[h, :, :HEAD_DIM] = mm(probs.astype(bf16), do_heads[h, :, :HEAD_DIM]).astype(bf16)
        dk_heads[h, :, :HEAD_DIM] = (
            mm(grad_scores, q_heads[h, :, :HEAD_DIM]) * score_scale
        ).astype(bf16)
        dq_t[span, :] = mm(k_t[span, :].astype(bf16), grad_scores) * score_scale
        return carry

    lax.fori_loop(0, HEADS, one_head, 0)
    dq_ref[...] = dq_t[...].T.astype(bf16)
    for i in range(pieces):
        span = slice(i * rows, (i + 1) * rows)
        for h in range(HEADS):
            dkv_ref[i, :, head(h)] = dk_heads[h, span, :HEAD_DIM]
            dkv_ref[i, :, D + h * HEAD_DIM : D + (h + 1) * HEAD_DIM] = dv_heads[
                h, span, :HEAD_DIM
            ]


def qkv_back_kernel(
    win, nx, dq_ref, own_ref, come_ref, x_ref, mod_ref, dx1_ref, w_ref,
    dkv_ref, gx_ref, sum_ref, buf, sems, pad,
):
    copies = block_copies(w_ref, win, buf, sems, nx)
    for copy in copies:
        copy.start()
    dkv_ref[...] = (own_ref[...].astype(f32) + come_ref[...].astype(f32)).astype(bf16)
    pad[...] = jnp.zeros(pad.shape, bf16)
    total = jnp.zeros(dx1_ref.shape, f32)
    for x in range(nx):
        copies[x].wait()
        take(pad, win.off, [dq_ref, dkv_ref], x * win.n, win.n)
        total = total + mm_nt(pad[...], buf[x])
    normed, inv_std = stats(x_ref[...].astype(f32))
    sum_ref[0:1, :] = column_sum(total)
    sum_ref[1:2, :] = column_sum(total * normed)
    gx_ref[...] = (
        dx1_ref[...] + stats_back(total * (1.0 + mod_ref[1:2, :]), normed, inv_std)
    ).astype(bf16)


def weight_kernel(nx, lanes, counts, *refs):
    lefts, k = [], 0
    for count in counts:
        lefts.append((refs[k], refs[k + 1 : k + 1 + count]))
        k += 1 + count
    out_ref, pads, turned = refs[k], refs[k + 1 :: 2], refs[k + 2 :: 2]
    x = pl.program_id(0)

    @pl.when(x == 0)
    def _():
        for (left, _), turn in zip(lefts, turned):
            turn[...] = left[...].astype(f32).T.astype(bf16)

    at = 0
    for (_, rights), pad, turn in zip(lefts, pads, turned):
        n = pad.shape[1]
        for i in range(nx):

            @pl.when(x == i)
            def _():
                take(pad, 0, rights, i * n, n)

        out_ref[0, :, at : at + n] = mm(turn[...], pad[...]).astype(bf16)
        at += n
    if at < lanes:
        out_ref[0, :, at:] = jnp.zeros((out_ref.shape[1], lanes - at), bf16)


def weight_grads(nx, pairs):
    widths = [sum(r.shape[1] for r in rights) // nx for _, rights in pairs]
    lanes = padded(sum(widths))
    rows = pairs[0][0].shape[0]
    args, specs, scratch = [], [], []
    for (left, rights), width in zip(pairs, widths):
        args += [left, *rights]
        specs += [vmem() for _ in range(1 + len(rights))]
        scratch += [pltpu.VMEM((rows, width), bf16), pltpu.VMEM((D, rows), bf16)]
    return pl.pallas_call(
        functools.partial(weight_kernel, nx, lanes, [len(r) for _, r in pairs]),
        out_shape=shape(nx, D, lanes, dtype=bf16),
        grid=(nx,),
        in_specs=specs,
        out_specs=pl.BlockSpec((1, D, lanes), lambda x: (x, 0, 0)),
        scratch_shapes=scratch,
        compiler_params=pltpu.CompilerParams(vmem_limit_bytes=56 << 20),
        cost_estimate=pl.CostEstimate(
            flops=4 * rows * D * nx * lanes, bytes_accessed=2 * nx * D * lanes, transcendentals=0
        ),
    )(*args)


def ff_grads(h3, du, dm, g):
    nx, rows, n = du.shape
    lanes = padded(n)

    def up_kernel(h_ref, du_ref, out_ref, turn):
        @pl.when(pl.program_id(0) == 0)
        def _():
            turn[...] = h_ref[...].astype(f32).T.astype(bf16)

        out_ref[0, :, :n] = mm(turn[...], du_ref[0]).astype(bf16)
        if n < lanes:
            out_ref[0, :, n:] = jnp.zeros((D, lanes - n), bf16)

    d_up = pl.pallas_call(
        up_kernel,
        out_shape=shape(nx, D, lanes, dtype=bf16),
        grid=(nx,),
        in_specs=[vmem(), pl.BlockSpec((1, rows, n), lambda x: (x, 0, 0))],
        out_specs=pl.BlockSpec((1, D, lanes), lambda x: (x, 0, 0)),
        scratch_shapes=[pltpu.VMEM((D, rows), bf16)],
        compiler_params=pltpu.CompilerParams(vmem_limit_bytes=56 << 20),
        cost_estimate=pl.CostEstimate(
            flops=4 * rows * D * nx * n, bytes_accessed=2 * nx * D * n, transcendentals=0
        ),
    )(h3, du)
    ny = lax.axis_size("gy")
    width = g.shape[1] // ny

    def down_kernel(dm_ref, g_ref, out_ref, turn):
        @pl.when(pl.program_id(0) == 0)
        def _():
            turn[...] = dm_ref[...].astype(f32).T.astype(bf16)

        out_ref[0] = mm(turn[...], g_ref[...]).astype(bf16)

    d_down = pl.pallas_call(
        down_kernel,
        out_shape=shape(ny, D, width, dtype=bf16),
        grid=(ny,),
        in_specs=[vmem(), pl.BlockSpec((rows, width), lambda i: (0, i))],
        out_specs=pl.BlockSpec((1, D, width), lambda i: (i, 0, 0)),
        scratch_shapes=[pltpu.VMEM((D, rows), bf16)],
        compiler_params=pltpu.CompilerParams(vmem_limit_bytes=56 << 20),
        cost_estimate=pl.CostEstimate(
            flops=4 * rows * D * ny * width, bytes_accessed=2 * ny * D * width, transcendentals=0
        ),
    )(dm, g)
    return d_up, d_down


def gather_columns(shard):
    nx = lax.axis_size("gx")
    whole = lax.all_gather(shard, col_axes, axis=0, tiled=True)
    return whole.reshape(nx, -1, shard.shape[1])


def gather_rows(shard):
    ny = lax.axis_size("gy")
    whole = lax.all_gather(shard, row_axes, axis=0, tiled=True)
    return whole.reshape(ny, -1, shard.shape[1])


def scatter(blocks, axes):
    flat = blocks.reshape(-1, blocks.shape[-1])
    return lax.psum_scatter(flat, axes, scatter_dimension=0, tiled=True).astype(f32)


def swap(values, axis, mask):
    return lax.ppermute(values, axis, [(i, i ^ mask) for i in range(lax.axis_size(axis))])


def reorder(values):
    devices = lax.axis_size(row_axes)
    return lax.all_to_all(
        values.reshape(devices, values.shape[0] // devices, values.shape[1]),
        row_axes,
        split_axis=0,
        concat_axis=0,
        tiled=True,
    ).reshape(values.shape)


def pad_lanes(values):
    return jnp.pad(values, ((0, 0), (0, padded(values.shape[1]) - values.shape[1])))


def condition(timesteps, pooled_text):
    half_width = D // 2
    frequency = jnp.exp(
        -math.log(10000.0) * jnp.arange(half_width).astype(jnp.float32) / half_width
    )
    angles = timesteps.astype(jnp.float32)[:, None] * frequency[None, :]
    embedded = jnp.concatenate([jnp.cos(angles), jnp.sin(angles)], axis=1)
    return jax.nn.silu(embedded + pooled_text)


def local(
    tokens,
    text_states,
    pooled_text,
    timesteps,
    frame_counts,
    still_clips,
    text_lengths,
    w_ada,
    w_sqkv,
    w_sout,
    w_cq,
    w_ckv,
    w_cout,
    w_up,
    w_down,
    w_tqkv,
    w_tout,
    grad_out,
):
    nx, ny = lax.axis_size("gx"), lax.axis_size("gy")
    gx, gy = lax.axis_index("gx"), lax.axis_index("gy")
    devices = nx * ny
    device = gy * nx + gx
    rows = tokens.shape[0]
    frame_devs = FRAME // rows
    frames = rows * devices // FRAME
    k_rows = w_ada.shape[0]
    clip_ends = jnp.cumsum(frame_counts)
    clip_here = jnp.sum((clip_ends <= device // frame_devs).astype(jnp.int32))
    clip_mark = jnp.arange(CLIPS) == clip_here
    clip_pick = clip_mark.astype(f32)
    keep_here = (1.0 - jnp.sum(clip_pick * still_clips.astype(f32))).reshape(1)
    length_here = jnp.sum(jnp.where(clip_mark, text_lengths, 0)).reshape(1)
    frame_clip = jnp.sum(
        (clip_ends[None, :] <= jnp.arange(frames)[:, None]).astype(jnp.int32), axis=1
    ).astype(f32)
    row_clip = jnp.repeat(frame_clip, rows // frames)[:, None]

    n_sqkv, n_one, n_up = w_sqkv.shape[1], w_sout.shape[1], w_up.shape[1]
    full_a = gather_columns(pad_lanes(jnp.concatenate([w_sqkv, w_sout, w_cq, w_cout], axis=1)))
    full_b = gather_columns(pad_lanes(jnp.concatenate([w_up, w_tqkv, w_tout], axis=1)))
    full_down = gather_rows(w_down.T)
    ff_width = full_down.shape[2]
    ff = ff_width * ny
    win_sqkv = Window(0, n_sqkv)
    at = n_sqkv
    win_rest = Window(at, at + 3 * n_one)
    win_sout, win_cq, win_cout = [
        Window(at + i * n_one, at + (i + 1) * n_one).inside(win_rest) for i in range(3)
    ]
    win_up = Window(0, n_up)
    win_tqkv = Window(n_up, n_up + n_sqkv)
    win_tout = Window(n_up + n_sqkv, n_up + n_sqkv + n_one)

    cond_all = condition(timesteps, pooled_text)
    cond_rows = lax.dynamic_slice_in_dim(cond_all, gy * k_rows, k_rows, axis=1)
    mod_part = jnp.dot(cond_rows, w_ada.astype(f32), precision=highest)
    mod_all = lax.all_gather(lax.psum(mod_part, "gy"), "gx", axis=1, tiled=True)
    mod = jnp.dot(clip_pick, mod_all, precision=highest).reshape(9, D)

    own = text_states.shape[0]
    depth = w_ckv.shape[0]
    pieces = text_states.reshape(own // CLIPS, CLIPS, ny, depth).transpose(2, 1, 0, 3)
    pieces = lax.all_to_all(
        pieces.reshape(ny, own, depth), "gy", split_axis=0, concat_axis=0, tiled=True
    )
    text_block = lax.all_gather(pieces, "gx", axis=0)
    text_block = (
        text_block.reshape(nx, ny, CLIPS, own // CLIPS, depth)
        .transpose(2, 1, 0, 3, 4)
        .reshape(own * devices, depth)
    )
    text_part = jnp.dot(text_block, w_ckv, preferred_element_type=f32)
    text_sum = lax.psum_scatter(text_part, "gy", scatter_dimension=0, tiled=True).astype(bf16)
    text_all = lax.all_gather(text_sum, row_axes, axis=0)
    slots = own * devices // CLIPS
    text_all = text_all.reshape(ny, nx, -1, w_ckv.shape[1]).transpose(0, 2, 1, 3)
    text_all = text_all.reshape(CLIPS, slots, 2 * D)
    text_pairs = lax.dynamic_index_in_dim(text_all, clip_here, axis=0, keepdims=False)

    win = win_sqkv
    hidden_a, query_a, pair_a = run(
        functools.partial(qkv_kernel, win, nx),
        [
            shape(rows, D, dtype=bf16),
            shape(rows, D, dtype=bf16),
            shape(rows, 2 * D, dtype=bf16),
        ],
        [vmem(), vmem(), hbm()],
        [pltpu.VMEM((nx, D, win.width), bf16), pltpu.SemaphoreType.DMA((nx,))],
        (tokens, mod, full_a),
        4 * rows * D * 3 * D,
        2 * D * 3 * D,
    )
    pairs = [pair_a]
    bit = frame_devs // 2
    while bit:
        pairs = pairs + [swap(p, "gx", bit) for p in pairs]
        bit //= 2
    count = len(pairs)
    keys = count * rows
    out_a, lse_a = run(
        functools.partial(spatial_kernel, count),
        [shape(rows, D, dtype=bf16), shape(HEADS, rows)],
        [vmem() for _ in range(1 + count)],
        [
            pltpu.VMEM((D, rows), f32),
            pltpu.VMEM((D, keys), f32),
            pltpu.VMEM((HEADS, keys, 128), bf16),
            pltpu.VMEM((D, rows), f32),
        ],
        (query_a, *pairs),
        16 * rows * keys * HEADS * 128,
        4 * keys * D,
    )

    branch_a, after_a, hidden_b, query_b, out_b, after_b, hidden_c = run(
        functools.partial(text_kernel, win_rest, win_sout, win_cq, win_cout, nx),
        [
            shape(rows, D),
            shape(rows, D),
            shape(rows, D, dtype=bf16),
            shape(rows, D, dtype=bf16),
            shape(rows, D, dtype=bf16),
            shape(rows, D),
            shape(rows, D, dtype=bf16),
        ],
        [vmem(), vmem(), vmem(), hbm(), vmem(), smem()],
        [
            pltpu.VMEM((nx, D, win_rest.width), bf16),
            pltpu.SemaphoreType.DMA((nx,)),
            pltpu.VMEM((D, rows), f32),
            pltpu.VMEM((D, rows), f32),
            pltpu.VMEM((D, slots), f32),
        ],
        (tokens, out_a, mod, full_a, text_pairs, length_here),
        8 * rows * D * 3 * D,
        2 * D * 4 * D,
    )

    pre_act, activated, branch_c, after_c, hidden_d = run(
        functools.partial(ff_kernel, win_up, nx, ny),
        [
            shape(rows, ff),
            shape(rows, ff, dtype=bf16),
            shape(rows, D),
            shape(rows, D),
            shape(rows, D, dtype=bf16),
        ],
        [vmem(), vmem(), vmem(), hbm(), hbm()],
        [
            pltpu.VMEM((nx, D, win_up.width), bf16),
            pltpu.VMEM((ny, D, ff_width), bf16),
            pltpu.SemaphoreType.DMA((nx,)),
            pltpu.SemaphoreType.DMA((ny,)),
        ],
        (hidden_c, after_b, mod, full_b, full_down),
        8 * rows * D * ff,
        4 * D * ff,
    )

    win = win_tout
    grad_branch_d, grad_out_d = run(
        functools.partial(early_kernel, win, nx),
        [shape(rows, D, dtype=bf16), shape(rows, D, dtype=bf16)],
        [vmem(), vmem(), smem(), hbm()],
        [
            pltpu.VMEM((nx, D, win.width), bf16),
            pltpu.VMEM((rows, win.width), bf16),
            pltpu.SemaphoreType.DMA((nx,)),
        ],
        (grad_out, mod, keep_here, full_b),
        4 * rows * D * D,
        2 * D * D,
    )
    grad_out_moved = reorder(grad_out_d)
    moved_d = reorder(hidden_d)
    win = win_tqkv
    out_moved, grad_qkv_d, grad_hidden_moved = run(
        functools.partial(temporal_kernel, win, nx, frames),
        [
            shape(rows, D, dtype=bf16),
            shape(rows, 3 * D, dtype=bf16),
            shape(rows, D, dtype=bf16),
        ],
        [vmem(), vmem(), hbm(), vmem(), smem()],
        [
            pltpu.VMEM((nx, D, win.width), bf16),
            pltpu.SemaphoreType.DMA((nx,)),
            pltpu.VMEM((rows, win.width), bf16),
        ]
        + [pltpu.VMEM((rows, D), f32)] * 8
        + [pltpu.VMEM((rows, 3 * D), bf16)],
        (moved_d, grad_out_moved, full_b, row_clip, frame_clip),
        16 * rows * D * 3 * D,
        2 * D * 3 * D,
    )
    grad_hidden_d = reorder(grad_hidden_moved)
    out_d = reorder(out_moved)
    win = win_tout
    mixed, d_gate3 = run(
        functools.partial(mixed_kernel, win, nx),
        [shape(rows, D, dtype=bf16), shape(1, D)],
        [vmem(), vmem(), vmem(), vmem(), smem(), hbm()],
        [
            pltpu.VMEM((nx, D, win.width), bf16),
            pltpu.SemaphoreType.DMA((nx,)),
            pltpu.VMEM((rows, D), f32),
        ],
        (out_d, after_c, grad_out, mod, keep_here, full_b),
        4 * rows * D * D,
        2 * D * D,
    )
    late = scatter(
        weight_grads(nx, [(moved_d, [grad_qkv_d]), (out_d, [grad_branch_d])]), col_axes
    )
    d_tqkv, d_tout = late[:, :n_sqkv], late[:, n_sqkv : n_sqkv + n_one]

    grad_branch_c, grad_pre, grad_b, sums_c = run(
        functools.partial(ff_back_kernel, win_up, nx, ny),
        [
            shape(rows, D, dtype=bf16),
            shape(nx, rows, n_up, dtype=bf16),
            shape(rows, D),
            shape(8, D),
        ],
        [vmem()] * 7 + [hbm(), hbm()],
        [
            pltpu.VMEM((nx, D, win_up.width), bf16),
            pltpu.VMEM((ny, D, ff_width), bf16),
            pltpu.SemaphoreType.DMA((nx,)),
            pltpu.SemaphoreType.DMA((ny,)),
            pltpu.VMEM((rows, ff), bf16),
            pltpu.VMEM((rows, win_up.width), bf16),
        ],
        (grad_out, grad_hidden_d, after_c, after_b, pre_act, branch_c, mod, full_b, full_down),
        8 * rows * D * ff,
        4 * D * ff,
    )
    up_terms, down_terms = ff_grads(hidden_c, grad_pre, grad_branch_c, activated)
    d_up = scatter(up_terms, col_axes)[:, :n_up]
    d_down = scatter(down_terms, row_axes).T

    kv_width = w_ckv.shape[1]
    grad_cout_rows, grad_query_b, grad_a, grad_branch_a, grad_out_a, text_terms, d_gate1 = run(
        functools.partial(text_back_kernel, win_rest, win_sout, win_cq, win_cout, nx),
        [
            shape(rows, D, dtype=bf16),
            shape(rows, D, dtype=bf16),
            shape(rows, D),
            shape(rows, D, dtype=bf16),
            shape(rows, D, dtype=bf16),
            shape(nx, slots, kv_width, dtype=bf16),
            shape(1, D),
        ],
        [vmem()] * 4 + [hbm(), vmem(), vmem(), smem()],
        [
            pltpu.VMEM((nx, D, win_rest.width), bf16),
            pltpu.SemaphoreType.DMA((nx,)),
            pltpu.VMEM((rows, max(w.width for w in (win_sout, win_cq, win_cout))), bf16),
            pltpu.VMEM((D, rows), f32),
            pltpu.VMEM((D, rows), f32),
            pltpu.VMEM((D, rows), f32),
            pltpu.VMEM((D, slots), f32),
            pltpu.VMEM((rows, D), bf16),
            pltpu.VMEM((slots, 2 * D), f32),
        ],
        (grad_b, after_a, branch_a, mod, full_a, query_b, text_pairs, length_here),
        8 * rows * D * 3 * D,
        2 * D * 4 * D,
    )
    text_terms = jnp.where(clip_mark[None, :, None, None], text_terms[:, None], 0)
    text_terms = lax.psum_scatter(
        text_terms.reshape(nx, -1, kv_width), "gx", scatter_dimension=0, tiled=True
    )
    text_grad = lax.psum(text_terms[0].astype(f32), "gy").astype(bf16)
    d_ckv = jnp.einsum("rd,re->de", text_block, text_grad, preferred_element_type=f32)

    grad_query_a, grad_pairs = run(
        functools.partial(spatial_back_kernel, count),
        [shape(rows, D, dtype=bf16), shape(count, rows, 2 * D, dtype=bf16)],
        [vmem() for _ in range(4 + count)],
        [pltpu.VMEM((D, rows), f32)] * 3
        + [pltpu.VMEM((D, keys), f32), pltpu.VMEM((D, rows), f32)]
        + [pltpu.VMEM((HEADS, rows, 128), bf16)] * 2
        + [pltpu.VMEM((HEADS, keys, 128), bf16)] * 4,
        (query_a, grad_out_a, out_a, lse_a, *pairs),
        40 * rows * keys * HEADS * 128,
        8 * keys * D,
    )
    bit = 1
    while bit < frame_devs // 2:
        half = grad_pairs.shape[0] // 2
        come = swap(grad_pairs[half:], "gx", bit)
        grad_pairs = (grad_pairs[:half].astype(f32) + come.astype(f32)).astype(bf16)
        bit *= 2
    come = swap(grad_pairs[1], "gx", bit)
    win = win_sqkv
    grad_pair_a, grad_tokens, sums_a = run(
        functools.partial(qkv_back_kernel, win, nx),
        [shape(rows, 2 * D, dtype=bf16), shape(rows, D, dtype=bf16), shape(2, D)],
        [vmem()] * 6 + [hbm()],
        [
            pltpu.VMEM((nx, D, win.width), bf16),
            pltpu.SemaphoreType.DMA((nx,)),
            pltpu.VMEM((rows, win.width), bf16),
        ],
        (grad_query_a, grad_pairs[0], come, tokens, mod, grad_a, full_a),
        4 * rows * D * 3 * D,
        2 * D * 3 * D,
    )
    early = scatter(
        weight_grads(
            nx,
            [
                (hidden_a, [grad_query_a, grad_pair_a]),
                (out_a, [grad_branch_a]),
                (hidden_b, [grad_query_b]),
                (out_b, [grad_cout_rows]),
            ],
        ),
        col_axes,
    )
    d_sqkv = early[:, :n_sqkv]
    d_sout, d_cq, d_cout = [
        early[:, n_sqkv + i * n_one : n_sqkv + (i + 1) * n_one] for i in range(3)
    ]

    grad_mod = jnp.concatenate(
        [sums_a, d_gate1, sums_c[3:5], sums_c[2:3], sums_c[0:2], d_gate3]
    ).reshape(-1)
    grad_mod = jnp.where(clip_mark[:, None], grad_mod[None, :], 0.0)
    grad_mod = lax.psum_scatter(grad_mod, "gx", scatter_dimension=1, tiled=True)
    grad_mod = lax.psum(grad_mod, "gy")
    d_ada = lax.dot_general(
        cond_rows, grad_mod, (((0,), (0,)), ((), ())), precision=highest
    )
    return (
        mixed,
        grad_tokens,
        d_ada,
        d_sqkv,
        d_sout,
        d_cq,
        d_ckv,
        d_cout,
        d_up,
        d_down,
        d_tqkv,
        d_tout,
    )


def solution(mesh):
    rows = P(("gy", "gx"), None)
    both = P("gy", "gx")
    return jax.shard_map(
        local,
        mesh=mesh,
        in_specs=(rows, rows, P(), P(), P(), P(), P()) + (both,) * 10 + (rows,),
        out_specs=(rows, rows) + (both,) * 10,
        check_vma=False,
    )
```

```python
import functools
import math

import jax
import jax.numpy as jnp
from jax import lax
from jax.experimental import pallas as pl
from jax.experimental.pallas import tpu as pltpu
from jax.sharding import PartitionSpec as P

D = 1152
HEADS = 16
HEAD_DIM = 72
FRAME = 1024
CLIPS = 4

norm_eps = 1e-06
masked_score = -1e30
highest = lax.Precision.HIGHEST
f32 = jnp.float32
bf16 = jnp.bfloat16
score_scale = HEAD_DIM ** (-0.5)
log2_scale = score_scale * math.log2(math.e)
row_axes = ("gy", "gx")
nt = (((1,), (1,)), ((), ()))


def vmem():
    return pl.BlockSpec(memory_space=pltpu.VMEM)


def smem():
    return pl.BlockSpec(memory_space=pltpu.SMEM)


def hbm():
    return pl.BlockSpec(memory_space=pl.ANY)


def shape(*size, dtype=f32):
    return jax.ShapeDtypeStruct(size, dtype)


def cost(micros):
    return pl.CostEstimate(flops=micros * 20000000, bytes_accessed=0, transcendentals=0)


def run(kernel, outs, specs, scratch, args, micros):
    flat, tree = jax.tree.flatten(tuple(args))
    flat_specs = []
    for arg, spec in zip(args, specs):
        flat_specs += [spec] * len(jax.tree.leaves(arg))

    def grouped(*refs):
        kernel(*jax.tree.unflatten(tree, refs[: len(flat)]), *refs[len(flat) :])

    return pl.pallas_call(
        grouped,
        out_shape=outs,
        in_specs=flat_specs,
        out_specs=[vmem() for _ in outs],
        scratch_shapes=scratch,
        compiler_params=pltpu.CompilerParams(vmem_limit_bytes=56 << 20),
        cost_estimate=cost(micros),
    )(*flat)


class Window:
    def __init__(self, lo, hi):
        self.lo, self.hi = lo, hi
        self.start = lo // 128 * 128
        self.stop = -(-hi // 128) * 128
        self.off = lo - self.start
        self.n = hi - lo
        self.width = self.stop - self.start

    def inside(self, outer):
        return Window(self.lo - outer.start, self.hi - outer.start)


def padded(lanes):
    return -(-lanes // 128) * 128


def piece_places(nx):
    half = nx // 4
    for core in range(2):
        for k, (first, last, low) in enumerate(((1, 0, 0), (1, 2, 0), (2, 0, half), (2, 1, half))):
            for i in range(2):
                for j in range(half):
                    yield core * 4 + k, i, j, (2 * (low + j)) ^ core, (first * i) ^ last


class Pieces:
    def __init__(self, sources, me, window, buffer, sems, nx):
        rows = sources[0].shape[2]
        columns = slice(window.start, window.stop)
        for k, i, j, far_x, far_y in piece_places(nx):
            x, y = me[0] ^ far_x, me[1] ^ far_y
            pltpu.make_async_copy(
                sources[k].at[i, j, :, columns],
                buffer.at[x, pl.ds(pl.multiple_of(y * rows, 16), rows), :],
                sems.at[x],
            ).start()
        self.buffer, self.sems = buffer, sems

    def wait(self, x):
        pltpu.make_async_copy(self.buffer.at[x], self.buffer.at[x], self.sems.at[x]).wait()


class Blocks:
    def __init__(self, source, buffer, sems):
        self.copies = [
            pltpu.make_async_copy(source.at[i], buffer.at[i], sems.at[i])
            for i in range(source.shape[0])
        ]
        for copy in self.copies:
            copy.start()

    def wait(self, i):
        self.copies[i].wait()


class Folded:
    def __init__(self, sources, me, start, buffer, sems, nx):
        rows = sources[0].shape[2] // 2
        width = buffer.shape[2]
        fold = fold_width(width)
        for k, i, j, far_x, far_y in piece_places(nx):
            x, y = me[0] ^ far_x, me[1] ^ far_y
            place = pl.ds(pl.multiple_of(x * rows, 16), rows)
            for top, columns in ((0, slice(0, fold)), (rows, slice(fold, width))):
                lanes = slice(start, start + columns.stop - columns.start)
                pltpu.make_async_copy(
                    sources[k].at[i, j, top : top + rows, lanes],
                    buffer.at[y, place, columns],
                    sems.at[y],
                ).start()
        self.buffer, self.sems = buffer, sems

    def wait(self, y):
        pltpu.make_async_copy(self.buffer.at[y], self.buffer.at[y], self.sems.at[y]).wait()


def fold_width(width):
    return padded(width // 2)


def down_blocks(up_refs, down_ref, me_ref, start, buf, sems, nx):
    if down_ref is None:
        return Folded(up_refs, me_ref, start, buf, sems, nx)
    return Blocks(down_ref, buf, sems)


def stats(values):
    centred = values - jnp.mean(values, axis=-1, keepdims=True)
    inv_std = lax.rsqrt(jnp.mean(centred * centred, axis=-1, keepdims=True) + norm_eps)
    return centred * inv_std, inv_std


def stats_back(grad_norm, normed, inv_std):
    return inv_std * (
        grad_norm
        - jnp.mean(grad_norm, axis=-1, keepdims=True)
        - normed * jnp.mean(grad_norm * normed, axis=-1, keepdims=True)
    )


def mm(left, right):
    return jnp.dot(left, right, preferred_element_type=f32)


def mm_nt(left, right):
    return lax.dot_general(left, right, nt, preferred_element_type=f32)


def put(dests, start, value):
    base, width = 0, value.shape[1]
    for ref in dests:
        size = ref.shape[1]
        lo, hi = max(start, base), min(start + width, base + size)
        if lo < hi:
            ref[:, lo - base : hi - base] = value[:, lo - start : hi - start].astype(ref.dtype)
        base += size


def take(pad, off, sources, start, width):
    base = 0
    for ref in sources:
        size = ref.shape[1]
        lo, hi = max(start, base), min(start + width, base + size)
        if lo < hi:
            pad[:, off + lo - start : off + hi - start] = ref[:, lo - base : hi - base]
        base += size


def head(h):
    return slice(h * HEAD_DIM, (h + 1) * HEAD_DIM)


def gelu_parts(u):
    c = math.sqrt(2.0 / math.pi)
    square = u * u
    return jnp.tanh(c * u * (1.0 + 0.044715 * square)), square, c


def qkv_kernel(win, nx, me_ref, x_ref, mod_ref, w_refs, h_ref, q_ref, kv_ref, buf, sems):
    pieces = Pieces(w_refs, me_ref, win, buf, sems, nx)
    normed, _ = stats(x_ref[...].astype(f32))
    hidden = (normed * (1.0 + mod_ref[1:2, :]) + mod_ref[0:1, :]).astype(bf16)
    h_ref[...] = hidden
    for x in range(nx):
        pieces.wait(x)
        block = mm(hidden, buf[x])[:, win.off : win.off + win.n]
        put([q_ref, kv_ref], x * win.n, block)


def stage_heads(dest, row, source, start):
    rows = source.shape[0]
    for h in range(HEADS):
        dest[h, row : row + rows, :HEAD_DIM] = source[
            :, start + h * HEAD_DIM : start + (h + 1) * HEAD_DIM
        ]


def spatial_kernel(pieces, *refs):
    q_ref = refs[0]
    kv_refs = refs[1 : 1 + pieces]
    o_ref, lse_ref, q_t, v_t, k_heads, o_t = refs[1 + pieces :]
    rows = q_ref.shape[0]
    q_t[...] = q_ref[...].astype(f32).T
    for i, kv in enumerate(kv_refs):
        v_t[:, i * rows : (i + 1) * rows] = kv[:, D:].astype(f32).T
        stage_heads(k_heads, i * rows, kv, 0)

    def one_head(h, carry):
        span = pl.ds(pl.multiple_of(h * HEAD_DIM, 8), HEAD_DIM)
        scores = mm(k_heads[h, :, :HEAD_DIM], q_t[span, :].astype(bf16)) * log2_scale
        top = jnp.max(scores, axis=0, keepdims=True)
        weights = jnp.exp2(scores - top)
        total = jnp.sum(weights, axis=0, keepdims=True)
        o_t[span, :] = mm(v_t[span, :].astype(bf16), weights.astype(bf16)) / total
        lse_ref[pl.ds(h, 1), :] = top + jnp.log2(total)
        return carry

    lax.fori_loop(0, HEADS, one_head, 0)
    o_ref[...] = o_t[...].T.astype(bf16)


def text_probs(text_ref, q_t, h, length):
    scores = mm(text_ref[:, head(h)], q_t[head(h), :].astype(bf16)) * score_scale
    slot = lax.broadcasted_iota(jnp.int32, scores.shape, 0)
    scores = jnp.where(slot < length, scores, masked_score)
    weights = jnp.exp(scores - jnp.max(scores, axis=0, keepdims=True))
    return weights / jnp.sum(weights, axis=0, keepdims=True)


def text_kernel(
    outer, w_out, w_cq, w_cout, nx, me_ref, x_ref, o_ref, mod_ref, w_refs, text_ref, length_ref,
    a1_ref, x1_ref, hc_ref, qc_ref, oc_ref, x2_ref, h3_ref,
    buf, sems, acc, q_t, v_t,
):
    pieces = Pieces(w_refs, me_ref, outer, buf, sems, nx)

    def product(left, win, dest, wait=False):
        for x in range(nx):
            if wait:
                pieces.wait(x)
            block = mm(left, buf[x, :, win.start : win.stop])[:, win.off : win.off + win.n]
            put([dest], x * win.n, block)

    product(o_ref[...], w_out, a1_ref, wait=True)
    after_a = x_ref[...].astype(f32) + mod_ref[2:3, :] * a1_ref[...]
    x1_ref[...] = after_a
    hidden = stats(after_a)[0].astype(bf16)
    hc_ref[...] = hidden
    product(hidden, w_cq, qc_ref)
    q_t[...] = qc_ref[...].astype(f32).T
    v_t[...] = text_ref[:, D:].astype(f32).T
    length = length_ref[0]
    for h in range(HEADS):
        probs = text_probs(text_ref, q_t, h, length).astype(bf16)
        acc[head(h), :] = mm(v_t[head(h), :].astype(bf16), probs)
    oc_ref[...] = acc[...].T.astype(bf16)
    product(oc_ref[...], w_cout, x2_ref)
    after_b = x1_ref[...] + x2_ref[...]
    x2_ref[...] = after_b
    h3_ref[...] = (
        stats(after_b)[0] * (1.0 + mod_ref[4:5, :]) + mod_ref[3:4, :]
    ).astype(bf16)


def ff_kernel(
    win, nx, ny, me_ref, h_ref, x2_ref, mod_ref, up_refs, down_ref,
    u_ref, g_ref, m_ref, x3_ref, h4_ref, up_buf, down_buf, up_sems, down_sems,
):
    ups = Pieces(up_refs, me_ref, win, up_buf, up_sems, nx)
    width = down_buf.shape[2]
    downs = down_blocks(up_refs, down_ref, me_ref, win.stop, down_buf, down_sems, nx)
    hidden = h_ref[...]
    for x in range(nx):
        ups.wait(x)
        u = mm(hidden, up_buf[x])[:, win.off : win.off + win.n]
        put([u_ref], x * win.n, u)
        put([g_ref], x * win.n, 0.5 * u * (1.0 + gelu_parts(u)[0]))
    total = jnp.zeros(m_ref.shape, f32)
    for i in range(ny):
        downs.wait(i)
        total = total + mm_nt(g_ref[:, i * width : (i + 1) * width], down_buf[i])
    m_ref[...] = total
    after_c = x2_ref[...] + mod_ref[5:6, :] * total
    x3_ref[...] = after_c
    h4_ref[...] = (
        stats(after_c)[0] * (1.0 + mod_ref[7:8, :]) + mod_ref[6:7, :]
    ).astype(bf16)


def temporal_kernel(
    win_all, win, w_out, nx, frames, me_ref, h_ref, da_ref, w_refs, row_clip, frame_clip,
    o_ref, at_ref, dqkv_ref, dh_ref, buf, sems, pad, q_s, k_s, v_s, do_s, o_s, dq_s, dk_s, dv_s, qkv_s,
):
    pieces = Pieces(w_refs, me_ref, win_all, buf, sems, nx)
    rows = h_ref.shape[0]
    spots = rows // frames
    hidden = h_ref[...]
    out_cols = slice(w_out.start, w_out.stop)
    pad[...] = jnp.zeros(pad.shape, bf16)
    total = jnp.zeros(h_ref.shape, f32)
    for x in range(nx):
        pieces.wait(x)
        block = mm(hidden, buf[x, :, win.start : win.stop])[:, win.off : win.off + win.n]
        put([qkv_s], x * win.n, block)
        take(pad, w_out.off, [da_ref], x * w_out.n, w_out.n)
        total = total + mm_nt(pad[:, : w_out.width], buf[x, :, out_cols])
    do_s[...] = total.astype(bf16).astype(f32)
    q_s[...] = qkv_s[:, :D].astype(f32)
    k_s[...] = qkv_s[:, D : 2 * D].astype(f32)
    v_s[...] = qkv_s[:, 2 * D :].astype(f32)
    dk_s[...] = jnp.zeros(dk_s.shape, f32)
    dv_s[...] = jnp.zeros(dv_s.shape, f32)

    def one_hot(size, feature, slot):
        first = lax.broadcasted_iota(jnp.int32, size, slot) * HEAD_DIM
        place = lax.broadcasted_iota(jnp.int32, size, feature)
        return jnp.where((place >= first) & (place < first + HEAD_DIM), 1.0, 0.0).astype(bf16)

    gather = one_hot((D, 128), 0, 1)
    spread = one_hot((128, D), 1, 0)

    def per_head(values):
        high = values.astype(bf16)
        low = (values - high.astype(f32)).astype(bf16)
        return mm(high, gather) + mm(low, gather)

    def every_frame(values):
        return jnp.broadcast_to(values[None], (frames, spots, D)).reshape(rows, D)

    def over_frames(values):
        return jnp.sum(values.reshape(frames, spots, values.shape[-1]), axis=0)

    def one_frame(f, carry):
        span = pl.ds(pl.multiple_of(f * spots, 8), spots)
        queries = every_frame(q_s[span, :])
        grads = every_frame(do_s[span, :])
        scores = per_head(queries * k_s[...]) * score_scale
        scores = jnp.where(row_clip[...] == frame_clip[f], scores, masked_score)
        scores = scores.reshape(frames, spots, 128)
        weights = jnp.exp(scores - jnp.max(scores, axis=0, keepdims=True))
        probs = weights / jnp.sum(weights, axis=0, keepdims=True)
        grad_probs = per_head(grads * v_s[...]).reshape(frames, spots, 128)
        inner = jnp.sum(probs * grad_probs, axis=0, keepdims=True)
        grad_scores = (probs * (grad_probs - inner)).reshape(rows, 128).astype(bf16)
        probs_wide = mm(probs.reshape(rows, 128).astype(bf16), spread)
        grads_wide = mm(grad_scores, spread)
        o_s[span, :] = over_frames(probs_wide * v_s[...])
        dq_s[span, :] = over_frames(grads_wide * k_s[...]) * score_scale
        dk_s[...] += grads_wide * queries
        dv_s[...] += probs_wide * grads
        return carry

    lax.fori_loop(0, frames, one_frame, 0)
    o_ref[...] = o_s[...].astype(bf16)
    for x in range(nx):
        block = mm(o_ref[...], buf[x, :, out_cols])[:, w_out.off : w_out.off + w_out.n]
        put([at_ref], x * w_out.n, block)
    dqkv_ref[:, :D] = dq_s[...].astype(bf16)
    dqkv_ref[:, D : 2 * D] = (dk_s[...] * score_scale).astype(bf16)
    dqkv_ref[:, 2 * D :] = dv_s[...].astype(bf16)
    pad[...] = jnp.zeros(pad.shape, bf16)
    total = jnp.zeros(dh_ref.shape, f32)
    for x in range(nx):
        take(pad, win.off, [dqkv_ref], x * win.n, win.n)
        total = total + mm_nt(pad[:, : win.width], buf[x, :, win.start : win.stop])
    dh_ref[...] = total.astype(bf16)


def mixed_kernel(at_ref, x3_ref, g_ref, mod_ref, keep_ref, y_ref, gate_ref):
    branch = at_ref[...].astype(f32)
    keep = keep_ref[0]
    y_ref[...] = (x3_ref[...] + keep * mod_ref[8:9, :] * branch).astype(bf16)
    gate_ref[...] = jnp.sum(keep * g_ref[...].astype(f32) * branch, axis=0, keepdims=True)


def column_sum(values):
    return jnp.sum(values, axis=0, keepdims=True)


def ff_back_kernel(
    win, nx, ny, me_ref, g_ref, dh4_ref, x3_ref, x2_ref, u_ref, m_ref, mod_ref, up_refs, down_ref,
    dm_ref, du_ref, dx2_ref, sum_ref, up_buf, down_buf, up_sems, down_sems, du_s, pad,
):
    width = down_buf.shape[2]
    downs = down_blocks(up_refs, down_ref, me_ref, win.stop, down_buf, down_sems, nx)
    ups = Pieces(up_refs, me_ref, win, up_buf, up_sems, nx)
    dh4 = dh4_ref[...].astype(f32)
    normed, inv_std = stats(x3_ref[...])
    dx3 = g_ref[...].astype(f32) + stats_back(dh4 * (1.0 + mod_ref[7:8, :]), normed, inv_std)
    sum_ref[0:1, :] = column_sum(dh4)
    sum_ref[1:2, :] = column_sum(dh4 * normed)
    sum_ref[2:3, :] = column_sum(dx3 * m_ref[...])
    dm = (mod_ref[5:6, :] * dx3).astype(bf16)
    dm_ref[...] = dm
    for i in range(ny):
        downs.wait(i)
        grad = mm(dm, down_buf[i])
        u = u_ref[:, i * width : (i + 1) * width]
        tanh, square, c = gelu_parts(u)
        slope = 0.5 * (1.0 + tanh) + 0.5 * u * (1.0 - tanh * tanh) * (
            c * (1.0 + 3.0 * 0.044715 * square)
        )
        du_s[:, i * width : (i + 1) * width] = (grad * slope).astype(bf16)
    pad[...] = jnp.zeros(pad.shape, bf16)
    total = jnp.zeros(dx2_ref.shape, f32)
    for x in range(nx):
        ups.wait(x)
        take(pad, win.off, [du_s], x * win.n, win.n)
        du_ref[x] = pad[:, win.off : win.off + win.n]
        total = total + mm_nt(pad[...], up_buf[x])
    normed, inv_std = stats(x2_ref[...])
    sum_ref[3:4, :] = column_sum(total)
    sum_ref[4:5, :] = column_sum(total * normed)
    sum_ref[5:8, :] = jnp.zeros((3, D), f32)
    dx2_ref[...] = dx3 + stats_back(total * (1.0 + mod_ref[4:5, :]), normed, inv_std)


def text_back_kernel(
    outer, w_out, w_cq, w_cout, nx, me_ref, dx2_ref, x1_ref, a1_ref, mod_ref, w_refs, qc_ref, text_ref,
    length_ref, dac_ref, dqc_ref, dx1_ref, da1_ref, do1_ref, dtext_ref, gate_ref,
    buf, sems, pad, acc, q_t, do_t, k_t, do_s, dtext_s,
):
    pieces = Pieces(w_refs, me_ref, outer, buf, sems, nx)

    def product(source, win, wait=False):
        pad[...] = jnp.zeros(pad.shape, bf16)
        total = jnp.zeros(dx2_ref.shape, f32)
        for x in range(nx):
            if wait:
                pieces.wait(x)
            take(pad, win.off, [source], x * win.n, win.n)
            total = total + mm_nt(pad[:, : win.width], buf[x, :, win.start : win.stop])
        return total

    dx2 = dx2_ref[...]
    dac_ref[...] = dx2.astype(bf16)
    grad_o = product(dac_ref, w_cout, wait=True).astype(bf16)
    do_s[...] = grad_o
    do_t[...] = grad_o.astype(f32).T
    q_t[...] = qc_ref[...].astype(f32).T
    k_t[...] = text_ref[:, :D].astype(f32).T
    length = length_ref[0]
    for h in range(HEADS):
        probs = text_probs(text_ref, q_t, h, length)
        values = text_ref[:, D + h * HEAD_DIM : D + (h + 1) * HEAD_DIM]
        grad_probs = mm(values, do_t[head(h), :].astype(bf16))
        inner = jnp.sum(probs * grad_probs, axis=0, keepdims=True)
        grad_scores = (probs * (grad_probs - inner)).astype(bf16)
        dtext_s[:, head(h)] = mm(grad_scores, qc_ref[:, head(h)]) * score_scale
        dtext_s[:, D + h * HEAD_DIM : D + (h + 1) * HEAD_DIM] = mm(
            probs.astype(bf16), do_s[:, head(h)]
        )
        acc[head(h), :] = mm(k_t[head(h), :].astype(bf16), grad_scores) * score_scale
    width = dtext_ref.shape[2]
    for x in range(nx):
        dtext_ref[x] = dtext_s[:, x * width : (x + 1) * width].astype(bf16)
    dqc_ref[...] = acc[...].T.astype(bf16)
    normed, inv_std = stats(x1_ref[...])
    dx1 = dx2 + stats_back(product(dqc_ref, w_cq), normed, inv_std)
    dx1_ref[...] = dx1
    gate_ref[...] = column_sum(dx1 * a1_ref[...])
    da1_ref[...] = (mod_ref[2:3, :] * dx1).astype(bf16)
    do1_ref[...] = product(da1_ref, w_out).astype(bf16)


def spatial_back_kernel(pieces, *refs):
    q_ref, do_ref, o_ref, lse_ref = refs[:4]
    kv_refs = refs[4 : 4 + pieces]
    (
        dq_ref, dkv_ref,
        q_t, do_t, o_t, k_t, dq_t, q_heads, do_heads, k_heads, v_heads, dk_heads, dv_heads,
    ) = refs[4 + pieces :]
    rows = q_ref.shape[0]
    q_t[...] = q_ref[...].astype(f32).T
    do_t[...] = do_ref[...].astype(f32).T
    o_t[...] = o_ref[...].astype(f32).T
    stage_heads(q_heads, 0, q_ref, 0)
    stage_heads(do_heads, 0, do_ref, 0)
    for i, kv in enumerate(kv_refs):
        k_t[:, i * rows : (i + 1) * rows] = kv[:, :D].astype(f32).T
        stage_heads(k_heads, i * rows, kv, 0)
        stage_heads(v_heads, i * rows, kv, D)

    def one_head(h, carry):
        span = pl.ds(pl.multiple_of(h * HEAD_DIM, 8), HEAD_DIM)
        grad_o = do_t[span, :]
        inner = jnp.sum(grad_o * o_t[span, :], axis=0, keepdims=True)
        scores = mm(k_heads[h, :, :HEAD_DIM], q_t[span, :].astype(bf16)) * log2_scale
        probs = jnp.exp2(scores - lse_ref[pl.ds(h, 1), :])
        grad_probs = mm(v_heads[h, :, :HEAD_DIM], grad_o.astype(bf16))
        grad_scores = (probs * (grad_probs - inner)).astype(bf16)
        dv_heads[h, :, :HEAD_DIM] = mm(probs.astype(bf16), do_heads[h, :, :HEAD_DIM]).astype(bf16)
        dk_heads[h, :, :HEAD_DIM] = (
            mm(grad_scores, q_heads[h, :, :HEAD_DIM]) * score_scale
        ).astype(bf16)
        dq_t[span, :] = mm(k_t[span, :].astype(bf16), grad_scores) * score_scale
        return carry

    lax.fori_loop(0, HEADS, one_head, 0)
    dq_ref[...] = dq_t[...].T.astype(bf16)
    for i in range(pieces):
        span = slice(i * rows, (i + 1) * rows)
        for h in range(HEADS):
            dkv_ref[i, :, head(h)] = dk_heads[h, span, :HEAD_DIM]
            dkv_ref[i, :, D + h * HEAD_DIM : D + (h + 1) * HEAD_DIM] = dv_heads[
                h, span, :HEAD_DIM
            ]


def qkv_back_kernel(
    win, nx, me_ref, dq_ref, own_ref, come_ref, x_ref, mod_ref, dx1_ref, w_refs,
    dkv_ref, gx_ref, sum_ref, buf, sems, pad,
):
    pieces = Pieces(w_refs, me_ref, win, buf, sems, nx)
    dkv_ref[...] = (own_ref[...].astype(f32) + come_ref[...].astype(f32)).astype(bf16)
    pad[...] = jnp.zeros(pad.shape, bf16)
    total = jnp.zeros(dx1_ref.shape, f32)
    for x in range(nx):
        pieces.wait(x)
        take(pad, win.off, [dq_ref, dkv_ref], x * win.n, win.n)
        total = total + mm_nt(pad[...], buf[x])
    normed, inv_std = stats(x_ref[...].astype(f32))
    sum_ref[0:1, :] = column_sum(total)
    sum_ref[1:2, :] = column_sum(total * normed)
    gx_ref[...] = (
        dx1_ref[...] + stats_back(total * (1.0 + mod_ref[1:2, :]), normed, inv_std)
    ).astype(bf16)


def step_block(step, me_x, nx):
    half = nx // 2
    return me_x ^ (2 * lax.rem(step, half) + (1 - step // half))


def turn_rows(turn, value, me_y, ny):
    rows = turn.shape[0] // ny
    flipped = value.astype(f32).T.astype(bf16)
    for y in range(ny):
        turn[pl.ds(pl.multiple_of((y ^ me_y) * rows, 16), rows), :] = flipped[
            y * rows : (y + 1) * rows
        ]


def weight_kernel(nx, ny, lanes, counts, me_ref, *refs):
    lefts, k = [], 0
    for count in counts:
        lefts.append((refs[k], refs[k + 1 : k + 1 + count]))
        k += 1 + count
    send_ref, keep_ref = refs[k : k + 2]
    pads, turned = refs[k + 2 :: 2], refs[k + 3 :: 2]
    step = pl.program_id(0)
    x = step_block(step, me_ref[0], nx)

    @pl.when(step == 0)
    def _():
        for (left, _), turn in zip(lefts, turned):
            turn_rows(turn, left[...], me_ref[1], ny)

    for (_, rights), pad in zip(lefts, pads):
        n = pad.shape[1]
        for i in range(nx):

            @pl.when(x == i)
            def _():
                take(pad, 0, rights, i * n, n)

    def fill(out_ref):
        at = 0
        for pad, turn in zip(pads, turned):
            n = pad.shape[1]
            out_ref[0, :, at : at + n] = mm(turn[...], pad[...]).astype(bf16)
            at += n
        if at < lanes:
            out_ref[0, :, at:] = jnp.zeros((out_ref.shape[1], lanes - at), bf16)

    @pl.when(step < nx // 2)
    def _():
        fill(send_ref)

    @pl.when(step >= nx // 2)
    def _():
        fill(keep_ref)


def weight_grads(nx, me, pairs):
    widths = [sum(r.shape[1] for r in rights) // nx for _, rights in pairs]
    lanes = padded(sum(widths))
    rows = pairs[0][0].shape[0]
    half = nx // 2
    args, specs, scratch = [], [], []
    for (left, rights), width in zip(pairs, widths):
        args += [left, *rights]
        specs += [vmem() for _ in range(1 + len(rights))]
        scratch += [pltpu.VMEM((rows, width), bf16), pltpu.VMEM((D, rows), bf16)]
    send, keep = pl.pallas_call(
        functools.partial(
            weight_kernel, nx, lax.axis_size("gy"), lanes, [len(r) for _, r in pairs]
        ),
        out_shape=[shape(half, D, lanes, dtype=bf16)] * 2,
        grid_spec=pltpu.PrefetchScalarGridSpec(
            num_scalar_prefetch=1,
            grid=(nx,),
            in_specs=specs,
            out_specs=[
                pl.BlockSpec((1, D, lanes), lambda t, me: (jnp.minimum(t, half - 1), 0, 0)),
                pl.BlockSpec((1, D, lanes), lambda t, me: (jnp.maximum(t - half, 0), 0, 0)),
            ],
            scratch_shapes=scratch,
        ),
        compiler_params=pltpu.CompilerParams(vmem_limit_bytes=56 << 20),
        cost_estimate=cost(12),
    )(me, *args)
    return keep, send


def up_grads(me, h3, du, dm, g):
    nx, rows, n = du.shape
    ny = lax.axis_size("gy")
    start = padded(n)
    width = g.shape[1] // ny
    fold = fold_width(width)
    lanes = start if dm is None else start + fold
    half = nx // 2
    each = D // nx
    args = (h3, du) if dm is None else (h3, du, dm, g)

    def kernel(me_ref, h_ref, du_ref, *refs):
        if dm is None:
            send_ref, keep_ref, turn = refs
        else:
            dm_ref, g_ref, send_ref, keep_ref, turn, down_turn = refs
        step = pl.program_id(0)

        @pl.when(step == 0)
        def _():
            turn_rows(turn, h_ref[...], me_ref[1], ny)
            if dm is not None:
                down_turn[...] = dm_ref[...].astype(f32).T.astype(bf16)

        def fill(out_ref):
            out_ref[0, :, :n] = mm(turn[...], du_ref[0]).astype(bf16)
            if n < lanes:
                out_ref[0, :, n:] = jnp.zeros((D, lanes - n), bf16)
            if dm is None:
                return
            x = step_block(step, me_ref[0], nx)
            left = down_turn[pl.ds(pl.multiple_of(x * each, 16), each), :]
            for y in range(ny):
                block = mm(left, g_ref[:, y * width : (y + 1) * width]).astype(bf16)
                top = pl.multiple_of((y ^ me_ref[1]) * 2 * each, 16)
                out_ref[0, pl.ds(top, each), start:] = block[:, :fold]
                low = pl.multiple_of((y ^ me_ref[1]) * 2 * each + each, 16)
                out_ref[0, pl.ds(low, each), start : start + width - fold] = block[:, fold:]

        @pl.when(step < half)
        def _():
            fill(send_ref)

        @pl.when(step >= half)
        def _():
            fill(keep_ref)

    send, keep = pl.pallas_call(
        kernel,
        out_shape=[shape(half, D, lanes, dtype=bf16)] * 2,
        grid_spec=pltpu.PrefetchScalarGridSpec(
            num_scalar_prefetch=1,
            grid=(nx,),
            in_specs=[
                vmem(),
                pl.BlockSpec((1, rows, n), lambda t, me: (step_block(t, me[0], nx), 0, 0)),
            ]
            + [vmem()] * (len(args) - 2),
            out_specs=[
                pl.BlockSpec((1, D, lanes), lambda t, me: (jnp.minimum(t, half - 1), 0, 0)),
                pl.BlockSpec((1, D, lanes), lambda t, me: (jnp.maximum(t - half, 0), 0, 0)),
            ],
            scratch_shapes=[pltpu.VMEM((D, rows), bf16)] * (len(args) // 2),
        ),
        compiler_params=pltpu.CompilerParams(vmem_limit_bytes=56 << 20),
        cost_estimate=cost(20),
    )(me, *args)
    return keep, send


def down_grads(dm, g):
    rows = g.shape[0]
    ny = lax.axis_size("gy")
    width = g.shape[1] // ny

    def kernel(dm_ref, g_ref, out_ref, turn):
        @pl.when(pl.program_id(0) == 0)
        def _():
            turn[...] = dm_ref[...].astype(f32).T.astype(bf16)

        out_ref[0] = mm(turn[...], g_ref[...]).astype(bf16)

    return pl.pallas_call(
        kernel,
        out_shape=shape(ny, D, width, dtype=bf16),
        grid=(ny,),
        in_specs=[vmem(), pl.BlockSpec((rows, width), lambda i: (0, i))],
        out_specs=pl.BlockSpec((1, D, width), lambda i: (i, 0, 0)),
        scratch_shapes=[pltpu.VMEM((D, rows), bf16)],
        compiler_params=pltpu.CompilerParams(vmem_limit_bytes=56 << 20),
        cost_estimate=cost(12),
    )(dm, g)


def after(value, *others):
    return lax.optimization_barrier((value, others))[0]


class Gather:
    def __init__(self, shard):
        self.line = [shard]

    def along(self, fars, *others):
        shard = after(self.line[0], *others)
        new = [swap(shard, "gx", 2 * far) for far in fars]
        self.line = self.line + new
        return new

    def first(self, *others):
        line = after(self.line, *others)
        half = len(line) // 2
        some, rest = jnp.stack(line[:half]), jnp.stack(line[half:])
        self.near = (some, rest)
        self.far = [swap(some, "gy", 1), swap(rest, "gy", 2)]
        return self.far

    def second(self, *others):
        far = after(self.far, *others)
        some, rest = [jnp.stack(pair) for pair in zip(self.near, far)]
        arrays = [swap(some, "gy", 2), swap(rest, "gy", 1)]
        self.arrays = [some, arrays[0], rest, arrays[1]]
        return arrays

    def last(self, *others):
        arrays = after(self.arrays, *others)
        return tuple(arrays + [swap(array, "gx", 1) for array in arrays])


def gather_rows(shard):
    ny = lax.axis_size("gy")
    whole = lax.all_gather(shard, row_axes, axis=0, tiled=True)
    return whole.reshape(ny, -1, shard.shape[1])


def total(*terms):
    return sum(term.astype(f32) for term in terms).astype(bf16)


class Scatter:
    def __init__(self, keep, send, *others):
        nz, depth, lanes = keep.shape
        ny = lax.axis_size("gy")
        self.half = nz // 2
        self.keep = keep.reshape(nz, ny, depth // ny, lanes)
        self.come = swap(after(send, *others), "gx", 1).reshape(self.keep.shape)

    def first(self, *others):
        keep, half = self.keep, self.half
        come = self.come = after(self.come, *others)
        some = swap(total(keep[:half, 2:], come[:half, 2:]), "gy", 2)
        self.some_come = some.reshape(half, 2, *some.shape[-2:])
        self.rest_come = [
            swap(total(keep[half:, y], come[half:, y]), "gy", 1) for y in (1, 3)
        ]
        return [self.some_come, *self.rest_come]

    def second(self, *others):
        keep, come, half = self.keep, self.come, self.half
        some_come, rest_come = after((self.some_come, self.rest_come), *others)
        some_end = swap(total(keep[:half, 1], come[:half, 1], some_come[:, 1]), "gy", 1)
        rest_end = swap(total(keep[half:, 2], come[half:, 2], rest_come[1]), "gy", 2)
        self.parts = (some_come, rest_come, some_end, rest_end)
        return [some_end, rest_end]

    def line(self, *others):
        keep, come, half = self.keep, self.come, self.half
        some_come, rest_come, some_end, rest_end = after(self.parts, *others)
        some = total(keep[:half, 0], come[:half, 0], some_come[:, 0], some_end)
        rest = total(keep[half:, 0], come[half:, 0], rest_come[0], rest_end)
        self.ends = [some[i] for i in range(half)] + [rest[i] for i in range(half)]
        self.got = []

    def along(self, fars, *others):
        new = [swap(after(self.ends[far], *others), "gx", 2 * far) for far in fars]
        self.got = self.got + new
        return new

    def result(self):
        return sum([term.astype(f32) for term in self.got], self.ends[0].astype(f32))


def scatter(blocks, axes):
    flat = blocks.reshape(-1, blocks.shape[-1])
    return lax.psum_scatter(flat, axes, scatter_dimension=0, tiled=True).astype(f32)


def swap(values, axis, mask):
    return lax.ppermute(values, axis, [(i, i ^ mask) for i in range(lax.axis_size(axis))])


def reorder(values):
    devices = lax.axis_size(row_axes)
    return lax.all_to_all(
        values.reshape(devices, values.shape[0] // devices, values.shape[1]),
        row_axes,
        split_axis=0,
        concat_axis=0,
        tiled=True,
    ).reshape(values.shape)


def pad_lanes(values):
    return jnp.pad(values, ((0, 0), (0, padded(values.shape[1]) - values.shape[1])))


def condition(timesteps, pooled_text):
    half_width = D // 2
    frequency = jnp.exp(
        -math.log(10000.0) * jnp.arange(half_width).astype(jnp.float32) / half_width
    )
    angles = timesteps.astype(jnp.float32)[:, None] * frequency[None, :]
    embedded = jnp.concatenate([jnp.cos(angles), jnp.sin(angles)], axis=1)
    return jax.nn.silu(embedded + pooled_text)


def local(
    tokens,
    text_states,
    pooled_text,
    timesteps,
    frame_counts,
    still_clips,
    text_lengths,
    w_ada,
    w_sqkv,
    w_sout,
    w_cq,
    w_ckv,
    w_cout,
    w_up,
    w_down,
    w_tqkv,
    w_tout,
    grad_out,
):
    nx, ny = lax.axis_size("gx"), lax.axis_size("gy")
    gx, gy = lax.axis_index("gx"), lax.axis_index("gy")
    devices = nx * ny
    me = jnp.stack([gx, gy]).astype(jnp.int32)
    device = gy * nx + gx
    rows = tokens.shape[0]
    frame_devs = FRAME // rows
    frames = rows * devices // FRAME
    k_rows = w_ada.shape[0]
    clip_ends = jnp.cumsum(frame_counts)
    clip_here = jnp.sum((clip_ends <= device // frame_devs).astype(jnp.int32))
    clip_mark = jnp.arange(CLIPS) == clip_here
    clip_pick = clip_mark.astype(f32)
    keep_here = (1.0 - jnp.sum(clip_pick * still_clips.astype(f32))).reshape(1)
    length_here = jnp.sum(jnp.where(clip_mark, text_lengths, 0)).reshape(1)
    frame_clip = jnp.sum(
        (clip_ends[None, :] <= jnp.arange(frames)[:, None]).astype(jnp.int32), axis=1
    ).astype(f32)
    row_clip = jnp.repeat(frame_clip, rows // frames)[:, None]

    n_sqkv, n_one, n_up = w_sqkv.shape[1], w_sout.shape[1], w_up.shape[1]
    shard_a = pad_lanes(jnp.concatenate([w_sqkv, w_sout, w_cq, w_cout], axis=1))
    shard_d = pad_lanes(jnp.concatenate([w_tqkv, w_tout], axis=1))
    shard_up = pad_lanes(w_up)
    trees = w_down.shape[1] % 16 == 0 and 2 * w_down.shape[1] == k_rows
    if trees:
        turned = w_down.T
        fold = fold_width(turned.shape[1])
        rest = jnp.pad(turned[:, fold:], ((0, 0), (0, 2 * fold - turned.shape[1])))
        folded = jnp.concatenate([turned[:, :fold], rest])
        shard_up = jnp.concatenate([shard_up, folded], axis=1)
    fars = range(1, nx // 2)
    get_a, get_up, get_d = Gather(shard_a), Gather(shard_up), Gather(shard_d)
    get_a.along(fars)
    cond_all = condition(timesteps, pooled_text)
    cond_rows = lax.dynamic_slice_in_dim(cond_all, gy * k_rows, k_rows, axis=1)
    mod_part = jnp.dot(cond_rows, w_ada.astype(f32), precision=highest)
    mod_part = mod_part + swap(mod_part, "gy", 1)
    mod_all = (mod_part + swap(mod_part, "gy", 2))[None]
    bit = 1
    while bit < nx:
        come = swap(mod_all, "gx", bit)
        mod_all = jnp.where(
            gx & bit != 0,
            jnp.concatenate([come, mod_all]),
            jnp.concatenate([mod_all, come]),
        )
        bit *= 2
    mod = lax.dynamic_index_in_dim(mod_all, clip_here, axis=1, keepdims=False).reshape(9, D)
    done = [*get_a.line, mod_all]
    done = get_a.first(*done) + get_up.along(fars[:1], *done)
    done = get_a.second(*done) + get_up.along(fars[1:], *done)
    full_a = get_a.last(*done)
    held = done
    done = get_up.first(*held) + get_d.along(fars, *held)
    ff_width = w_down.shape[0]
    ff = ff_width * ny
    win_sqkv = Window(0, n_sqkv)
    at = n_sqkv
    win_rest = Window(at, at + 3 * n_one)
    win_sout, win_cq, win_cout = [
        Window(at + i * n_one, at + (i + 1) * n_one).inside(win_rest) for i in range(3)
    ]
    win_up = Window(0, n_up)
    win_d = Window(0, n_sqkv + n_one)
    win_tqkv = Window(0, n_sqkv)
    win_tout = Window(n_sqkv, n_sqkv + n_one)

    own = text_states.shape[0]
    depth = w_ckv.shape[0]
    text_rows = text_states.reshape(own // CLIPS, CLIPS, -1).transpose(1, 0, 2)
    text_rows = lax.all_gather(text_rows.reshape(own, -1), row_axes, axis=0)
    text_rows = after(text_rows, *held)
    text_block = lax.dynamic_slice_in_dim(text_rows, gy * depth, depth, axis=2)
    text_block = (
        text_block.reshape(devices, CLIPS, own // CLIPS, depth)
        .transpose(1, 0, 2, 3)
        .reshape(own * devices, depth)
    )
    text_part = jnp.dot(text_block, w_ckv, preferred_element_type=f32)
    text_sum = lax.psum_scatter(text_part, "gy", scatter_dimension=0, tiled=True).astype(bf16)

    win = win_sqkv
    hidden_a, query_a, pair_a = run(
        functools.partial(qkv_kernel, win, nx),
        [
            shape(rows, D, dtype=bf16),
            shape(rows, D, dtype=bf16),
            shape(rows, 2 * D, dtype=bf16),
        ],
        [smem()] + [vmem(), vmem(), hbm()],
        [pltpu.VMEM((nx, D, win.width), bf16), pltpu.SemaphoreType.DMA((nx,))],
        (me, tokens, mod, full_a),
        9,
    )
    done = done + [pair_a]
    near_up = get_up.second(*done)
    text_all = lax.all_gather(after(text_sum, *done), row_axes, axis=0)
    grad_branch_d = (keep_here[0] * mod[8] * grad_out.astype(f32)).astype(bf16)
    grad_branch_moved = reorder(after(grad_branch_d, *done))
    slots = own * devices // CLIPS
    text_all = text_all.reshape(ny, nx, -1, w_ckv.shape[1]).transpose(0, 2, 1, 3)
    text_all = text_all.reshape(CLIPS, slots, 2 * D)
    text_pairs = lax.dynamic_index_in_dim(text_all, clip_here, axis=0, keepdims=False)
    pairs = [after(pair_a, *done)]
    bit = frame_devs // 2
    while bit:
        pairs = pairs + [swap(p, "gx", bit) for p in pairs]
        bit //= 2
    count = len(pairs)
    keys = count * rows
    out_a, lse_a = run(
        functools.partial(spatial_kernel, count),
        [shape(rows, D, dtype=bf16), shape(HEADS, rows)],
        [vmem() for _ in range(1 + count)],
        [
            pltpu.VMEM((D, rows), f32),
            pltpu.VMEM((D, keys), f32),
            pltpu.VMEM((HEADS, keys, 128), bf16),
            pltpu.VMEM((D, rows), f32),
        ],
        (query_a, *pairs),
        18,
    )

    done = near_up + [out_a, text_pairs, grad_branch_moved]
    full_up = get_up.last(*done)
    full_down = None if trees else gather_rows(after(w_down.T, *done))
    far_d = get_d.first(*done)
    out_a = after(out_a, *done)
    branch_a, after_a, hidden_b, query_b, out_b, after_b, hidden_c = run(
        functools.partial(text_kernel, win_rest, win_sout, win_cq, win_cout, nx),
        [
            shape(rows, D),
            shape(rows, D),
            shape(rows, D, dtype=bf16),
            shape(rows, D, dtype=bf16),
            shape(rows, D, dtype=bf16),
            shape(rows, D),
            shape(rows, D, dtype=bf16),
        ],
        [smem()] + [vmem(), vmem(), vmem(), hbm(), vmem(), smem()],
        [
            pltpu.VMEM((nx, D, win_rest.width), bf16),
            pltpu.SemaphoreType.DMA((nx,)),
            pltpu.VMEM((D, rows), f32),
            pltpu.VMEM((D, rows), f32),
            pltpu.VMEM((D, slots), f32),
        ],
        (me, tokens, out_a, mod, full_a, text_pairs, length_here),
        18,
    )

    near_d = get_d.second(hidden_c, *far_d)
    pre_act, activated, branch_c, after_c, hidden_d = run(
        functools.partial(ff_kernel, win_up, nx, ny),
        [
            shape(rows, ff),
            shape(rows, ff, dtype=bf16),
            shape(rows, D),
            shape(rows, D),
            shape(rows, D, dtype=bf16),
        ],
        [smem()] + [vmem(), vmem(), vmem(), hbm(), hbm()],
        [
            pltpu.VMEM((nx, D, win_up.width), bf16),
            pltpu.VMEM((ny, D, ff_width), bf16),
            pltpu.SemaphoreType.DMA((nx,)),
            pltpu.SemaphoreType.DMA((ny,)),
        ],
        (me, hidden_c, after_b, mod, full_up, full_down),
        20,
    )

    done = [*near_d, hidden_d]
    full_d = get_d.last(*done)
    moved_d = reorder(after(hidden_d, *done))
    pad_width = max(win_tqkv.width, win_tout.width)
    out_moved, branch_moved, grad_qkv_d, grad_hidden_moved = run(
        functools.partial(temporal_kernel, win_d, win_tqkv, win_tout, nx, frames),
        [
            shape(rows, D, dtype=bf16),
            shape(rows, D, dtype=bf16),
            shape(rows, 3 * D, dtype=bf16),
            shape(rows, D, dtype=bf16),
        ],
        [smem()] + [vmem(), vmem(), hbm(), vmem(), smem()],
        [
            pltpu.VMEM((nx, D, win_d.width), bf16),
            pltpu.SemaphoreType.DMA((nx,)),
            pltpu.VMEM((rows, pad_width), bf16),
        ]
        + [pltpu.VMEM((rows, D), f32)] * 8
        + [pltpu.VMEM((rows, 3 * D), bf16)],
        (me, moved_d, grad_branch_moved, full_d, row_clip, frame_clip),
        25,
    )
    grad_hidden_d = reorder(grad_hidden_moved)
    late_terms = weight_grads(
        nx, me, [(moved_d, [grad_qkv_d]), (out_moved, [grad_branch_moved])]
    )
    done = [*late_terms, grad_hidden_d]
    late = Scatter(*late_terms, *done)
    grad_hidden_d = after(grad_hidden_d, *done)
    branch_d = reorder(after(branch_moved, *done))
    mixed, d_gate3 = run(
        mixed_kernel,
        [shape(rows, D, dtype=bf16), shape(1, D)],
        [vmem(), vmem(), vmem(), vmem(), smem()],
        [],
        (branch_d, after_c, grad_out, mod, keep_here),
        3,
    )

    grad_branch_c, grad_pre, grad_b, sums_c = run(
        functools.partial(ff_back_kernel, win_up, nx, ny),
        [
            shape(rows, D, dtype=bf16),
            shape(nx, rows, n_up, dtype=bf16),
            shape(rows, D),
            shape(8, D),
        ],
        [smem()] + [vmem()] * 7 + [hbm(), hbm()],
        [
            pltpu.VMEM((nx, D, win_up.width), bf16),
            pltpu.VMEM((ny, D, ff_width), bf16),
            pltpu.SemaphoreType.DMA((nx,)),
            pltpu.SemaphoreType.DMA((ny,)),
            pltpu.VMEM((rows, ff), bf16),
            pltpu.VMEM((rows, win_up.width), bf16),
        ],
        (me, grad_out, grad_hidden_d, after_c, after_b, pre_act, branch_c, mod, full_up, full_down),
        22,
    )
    done = [late.come, grad_b, branch_d]
    late_first = late.first(*done)
    grad_pre = after(grad_pre, *done)
    if trees:
        up_terms = up_grads(me, hidden_c, grad_pre, grad_branch_c, activated)
    else:
        up_terms = up_grads(me, hidden_c, grad_pre, None, activated)
        d_down = scatter(down_grads(grad_branch_c, activated), row_axes).T
    done = [*late_first, *up_terms]
    late_second = late.second(*done)
    up_sums = Scatter(*up_terms, *done)
    grad_b = after(grad_b, *done)

    kv_width = w_ckv.shape[1]
    grad_cout_rows, grad_query_b, grad_a, grad_branch_a, grad_out_a, text_terms, d_gate1 = run(
        functools.partial(text_back_kernel, win_rest, win_sout, win_cq, win_cout, nx),
        [
            shape(rows, D, dtype=bf16),
            shape(rows, D, dtype=bf16),
            shape(rows, D),
            shape(rows, D, dtype=bf16),
            shape(rows, D, dtype=bf16),
            shape(nx, slots, kv_width, dtype=bf16),
            shape(1, D),
        ],
        [smem()] + [vmem()] * 4 + [hbm(), vmem(), vmem(), smem()],
        [
            pltpu.VMEM((nx, D, win_rest.width), bf16),
            pltpu.SemaphoreType.DMA((nx,)),
            pltpu.VMEM((rows, max(w.width for w in (win_sout, win_cq, win_cout))), bf16),
            pltpu.VMEM((D, rows), f32),
            pltpu.VMEM((D, rows), f32),
            pltpu.VMEM((D, rows), f32),
            pltpu.VMEM((D, slots), f32),
            pltpu.VMEM((rows, D), bf16),
            pltpu.VMEM((slots, 2 * D), f32),
        ],
        (me, grad_b, after_a, branch_a, mod, full_a, query_b, text_pairs, length_here),
        20,
    )
    text_terms = jnp.where(clip_mark[None, :, None, None], text_terms[:, None], 0)
    text_terms = lax.psum_scatter(
        text_terms.reshape(nx, -1, kv_width), "gx", scatter_dimension=0, tiled=True
    )
    text_terms = text_terms[0].astype(f32)
    text_terms = text_terms + swap(text_terms.astype(bf16), "gy", 1).astype(f32)
    text_terms = text_terms + swap(text_terms.astype(bf16), "gy", 2).astype(f32)
    text_grad = text_terms.astype(bf16)
    d_ckv = jnp.einsum("rd,re->de", text_block, text_grad, preferred_element_type=f32)

    cross_terms = weight_grads(
        nx, me, [(hidden_b, [grad_query_b]), (out_b, [grad_cout_rows])]
    )
    done = [*late_second, up_sums.come, *cross_terms, grad_out_a]
    late.line(*done)
    late_done = late.along(fars, *done)
    up_first = up_sums.first(*done)
    cross = Scatter(*cross_terms, *done)
    grad_out_a = after(grad_out_a, *done)

    grad_query_a, grad_pairs = run(
        functools.partial(spatial_back_kernel, count),
        [shape(rows, D, dtype=bf16), shape(count, rows, 2 * D, dtype=bf16)],
        [vmem() for _ in range(4 + count)],
        [pltpu.VMEM((D, rows), f32)] * 3
        + [pltpu.VMEM((D, keys), f32), pltpu.VMEM((D, rows), f32)]
        + [pltpu.VMEM((HEADS, rows, 128), bf16)] * 2
        + [pltpu.VMEM((HEADS, keys, 128), bf16)] * 4,
        (query_a, grad_out_a, out_a, lse_a, *pairs),
        28,
    )
    late = late.result()
    d_tqkv, d_tout = late[:, :n_sqkv], late[:, n_sqkv : n_sqkv + n_one]
    done = [*late_done, *up_first, cross.come, grad_pairs]
    up_second = up_sums.second(*done)
    grad_pairs = after(grad_pairs, *done)
    bit = 1
    while bit < frame_devs // 2:
        half = grad_pairs.shape[0] // 2
        come = swap(grad_pairs[half:], "gx", bit)
        grad_pairs = (grad_pairs[:half].astype(f32) + come.astype(f32)).astype(bf16)
        bit *= 2
    come = swap(grad_pairs[1], "gx", bit)
    win = win_sqkv
    grad_pair_a, grad_tokens, sums_a = run(
        functools.partial(qkv_back_kernel, win, nx),
        [shape(rows, 2 * D, dtype=bf16), shape(rows, D, dtype=bf16), shape(2, D)],
        [smem()] + [vmem()] * 6 + [hbm()],
        [
            pltpu.VMEM((nx, D, win.width), bf16),
            pltpu.SemaphoreType.DMA((nx,)),
            pltpu.VMEM((rows, win.width), bf16),
        ],
        (me, grad_query_a, grad_pairs[0], come, tokens, mod, grad_a, full_a),
        11,
    )
    early_terms = weight_grads(
        nx,
        me,
        [(hidden_a, [grad_query_a, grad_pair_a]), (out_a, [grad_branch_a])],
    )
    done = [*up_second, *early_terms]
    early = Scatter(*early_terms, *done)
    up_sums.line(*done)
    done = up_sums.along(fars[:1], *done) + cross.first(*done) + [early.come]
    done = up_sums.along(fars[1:2], *done) + cross.second(*done) + early.first(*done)
    cross.line(*done)
    done = (
        up_sums.along(fars[2:], *done) + cross.along(fars, *done) + early.second(*done)
    )
    early.line(*done)
    early.along(fars)
    up, cross, early = up_sums.result(), cross.result(), early.result()
    d_up = up[:, :n_up]
    if trees:
        start, each = win_up.stop, w_down.shape[1]
        d_down = jnp.concatenate(
            [up[:each, start:], up[each:, start : start + ff_width - fold]], axis=1
        ).T
    d_cq, d_cout = cross[:, :n_one], cross[:, n_one : 2 * n_one]
    d_sqkv, d_sout = early[:, :n_sqkv], early[:, n_sqkv : n_sqkv + n_one]

    grad_mod = jnp.concatenate(
        [sums_a, d_gate1, sums_c[3:5], sums_c[2:3], sums_c[0:2], d_gate3]
    ).reshape(-1)
    grad_mod = lax.all_gather(grad_mod, row_axes, axis=0)
    width = w_ada.shape[1]
    grad_mod = lax.dynamic_slice_in_dim(grad_mod, gx * width, width, axis=1)
    device_clip = jnp.sum(
        (clip_ends[None, :] <= (jnp.arange(devices) // frame_devs)[:, None]).astype(jnp.int32),
        axis=1,
    )
    device_pick = (jnp.arange(CLIPS)[:, None] == device_clip[None, :]).astype(f32)
    grad_mod = jnp.dot(device_pick, grad_mod, precision=highest)
    d_ada = lax.dot_general(
        cond_rows, grad_mod, (((0,), (0,)), ((), ())), precision=highest
    )
    return (
        mixed,
        grad_tokens,
        d_ada,
        d_sqkv,
        d_sout,
        d_cq,
        d_ckv,
        d_cout,
        d_up,
        d_down,
        d_tqkv,
        d_tout,
    )


def solution(mesh):
    rows = P(("gy", "gx"), None)
    both = P("gy", "gx")
    return jax.shard_map(
        local,
        mesh=mesh,
        in_specs=(rows, rows, P(), P(), P(), P(), P()) + (both,) * 10 + (rows,),
        out_specs=(rows, rows) + (both,) * 10,
        check_vma=False,
    )
```

```python
import functools
import math

import jax
import jax.numpy as jnp
from jax import lax
from jax.experimental import pallas as pl
from jax.experimental.pallas import tpu as pltpu
from jax.sharding import PartitionSpec as P

D = 1152
HEADS = 16
HEAD_DIM = 72
FRAME = 1024
CLIPS = 4

norm_eps = 1e-06
masked_score = -1e30
highest = lax.Precision.HIGHEST
f32 = jnp.float32
bf16 = jnp.bfloat16
score_scale = HEAD_DIM ** (-0.5)
log2_scale = score_scale * math.log2(math.e)
row_axes = ("gy", "gx")
nt = (((1,), (1,)), ((), ()))


def vmem():
    return pl.BlockSpec(memory_space=pltpu.VMEM)


def smem():
    return pl.BlockSpec(memory_space=pltpu.SMEM)


def hbm():
    return pl.BlockSpec(memory_space=pl.ANY)


def shape(*size, dtype=f32):
    return jax.ShapeDtypeStruct(size, dtype)


def cost(micros):
    return pl.CostEstimate(flops=micros * 20000000, bytes_accessed=0, transcendentals=0)


def run(kernel, outs, specs, scratch, args, micros):
    flat, tree = jax.tree.flatten(tuple(args))
    flat_specs = []
    for arg, spec in zip(args, specs):
        flat_specs += [spec] * len(jax.tree.leaves(arg))

    def grouped(*refs):
        kernel(*jax.tree.unflatten(tree, refs[: len(flat)]), *refs[len(flat) :])

    return pl.pallas_call(
        grouped,
        out_shape=outs,
        in_specs=flat_specs,
        out_specs=[vmem() for _ in outs],
        scratch_shapes=scratch,
        compiler_params=pltpu.CompilerParams(vmem_limit_bytes=56 << 20),
        cost_estimate=cost(micros),
    )(*flat)


class Window:
    def __init__(self, lo, hi):
        self.lo, self.hi = lo, hi
        self.start = lo // 128 * 128
        self.stop = -(-hi // 128) * 128
        self.off = lo - self.start
        self.n = hi - lo
        self.width = self.stop - self.start

    def inside(self, outer):
        return Window(self.lo - outer.start, self.hi - outer.start)


def padded(lanes):
    return -(-lanes // 128) * 128


def piece_places(nx):
    half = nx // 4
    for core in range(2):
        for k, (first, last, low) in enumerate(((1, 0, 0), (1, 2, 0), (2, 0, half), (2, 1, half))):
            for i in range(2):
                for j in range(half):
                    yield core * 4 + k, i, j, (2 * (low + j)) ^ core, (first * i) ^ last


class Pieces:
    def __init__(self, sources, me, window, buffer, sems, nx):
        rows = buffer.shape[1] // 4
        columns = slice(window.start, window.stop)
        for k, i, j, far_x, far_y in piece_places(nx):
            x, y = me[0] ^ far_x, me[1] ^ far_y
            pltpu.make_async_copy(
                sources[k].at[i, j, :rows, columns],
                buffer.at[x, pl.ds(pl.multiple_of(y * rows, 16), rows), :],
                sems.at[x],
            ).start()
        self.buffer, self.sems = buffer, sems

    def wait(self, x):
        pltpu.make_async_copy(self.buffer.at[x], self.buffer.at[x], self.sems.at[x]).wait()


class Blocks:
    def __init__(self, source, buffer, sems):
        self.copies = [
            pltpu.make_async_copy(source.at[i], buffer.at[i], sems.at[i])
            for i in range(source.shape[0])
        ]
        for copy in self.copies:
            copy.start()

    def wait(self, i):
        self.copies[i].wait()


class Folded:
    def __init__(self, sources, me, buffer, sems, nx):
        rows = buffer.shape[1] // nx
        base = sources[0].shape[2] - 2 * rows
        width = buffer.shape[2]
        fold = fold_width(width)
        for k, i, j, far_x, far_y in piece_places(nx):
            x, y = me[0] ^ far_x, me[1] ^ far_y
            place = pl.ds(pl.multiple_of(x * rows, 16), rows)
            for top, columns in ((base, slice(0, fold)), (base + rows, slice(fold, width))):
                pltpu.make_async_copy(
                    sources[k].at[i, j, top : top + rows, : columns.stop - columns.start],
                    buffer.at[y, place, columns],
                    sems.at[y],
                ).start()
        self.buffer, self.sems = buffer, sems

    def wait(self, y):
        pltpu.make_async_copy(self.buffer.at[y], self.buffer.at[y], self.sems.at[y]).wait()


def fold_width(width):
    return padded(width // 2)


def down_blocks(up_refs, down_ref, me_ref, buf, sems, nx):
    if down_ref is None:
        return Folded(up_refs, me_ref, buf, sems, nx)
    return Blocks(down_ref, buf, sems)


def stats(values):
    centred = values - jnp.mean(values, axis=-1, keepdims=True)
    inv_std = lax.rsqrt(jnp.mean(centred * centred, axis=-1, keepdims=True) + norm_eps)
    return centred * inv_std, inv_std


def stats_back(grad_norm, normed, inv_std):
    return inv_std * (
        grad_norm
        - jnp.mean(grad_norm, axis=-1, keepdims=True)
        - normed * jnp.mean(grad_norm * normed, axis=-1, keepdims=True)
    )


def mm(left, right):
    return jnp.dot(left, right, preferred_element_type=f32)


def mm_nt(left, right):
    return lax.dot_general(left, right, nt, preferred_element_type=f32)


def put(dests, start, value):
    base, width = 0, value.shape[1]
    for ref in dests:
        size = ref.shape[1]
        lo, hi = max(start, base), min(start + width, base + size)
        if lo < hi:
            ref[:, lo - base : hi - base] = value[:, lo - start : hi - start].astype(ref.dtype)
        base += size


def take(pad, off, sources, start, width):
    base = 0
    for ref in sources:
        size = ref.shape[1]
        lo, hi = max(start, base), min(start + width, base + size)
        if lo < hi:
            pad[:, off + lo - start : off + hi - start] = ref[:, lo - base : hi - base]
        base += size


def head(h):
    return slice(h * HEAD_DIM, (h + 1) * HEAD_DIM)


def gelu_parts(u):
    c = math.sqrt(2.0 / math.pi)
    square = u * u
    return jnp.tanh(c * u * (1.0 + 0.044715 * square)), square, c


def qkv_kernel(win, nx, me_ref, x_ref, mod_ref, w_refs, h_ref, q_ref, kv_ref, buf, sems):
    pieces = Pieces(w_refs, me_ref, win, buf, sems, nx)
    normed, _ = stats(x_ref[...].astype(f32))
    hidden = (normed * (1.0 + mod_ref[1:2, :]) + mod_ref[0:1, :]).astype(bf16)
    h_ref[...] = hidden
    for x in range(nx):
        pieces.wait(x)
        block = mm(hidden, buf[x])[:, win.off : win.off + win.n]
        put([q_ref, kv_ref], x * win.n, block)


def stage_heads(dest, row, source, start):
    rows = source.shape[0]
    for h in range(HEADS):
        dest[h, row : row + rows, :HEAD_DIM] = source[
            :, start + h * HEAD_DIM : start + (h + 1) * HEAD_DIM
        ]


def spatial_kernel(pieces, *refs):
    q_ref = refs[0]
    kv_refs = refs[1 : 1 + pieces]
    o_ref, lse_ref, q_t, v_t, k_heads, o_t = refs[1 + pieces :]
    rows = q_ref.shape[0]
    q_t[...] = q_ref[...].astype(f32).T
    for i, kv in enumerate(kv_refs):
        v_t[:, i * rows : (i + 1) * rows] = kv[:, D:].astype(f32).T
        stage_heads(k_heads, i * rows, kv, 0)

    def one_head(h, carry):
        span = pl.ds(pl.multiple_of(h * HEAD_DIM, 8), HEAD_DIM)
        scores = mm(k_heads[h, :, :HEAD_DIM], q_t[span, :].astype(bf16)) * log2_scale
        top = jnp.max(scores, axis=0, keepdims=True)
        weights = jnp.exp2(scores - top)
        total = jnp.sum(weights, axis=0, keepdims=True)
        o_t[span, :] = mm(v_t[span, :].astype(bf16), weights.astype(bf16)) / total
        lse_ref[pl.ds(h, 1), :] = top + jnp.log2(total)
        return carry

    lax.fori_loop(0, HEADS, one_head, 0)
    o_ref[...] = o_t[...].T.astype(bf16)


def text_probs(text_ref, q_t, h, length):
    scores = mm(text_ref[:, head(h)], q_t[head(h), :].astype(bf16)) * score_scale
    slot = lax.broadcasted_iota(jnp.int32, scores.shape, 0)
    scores = jnp.where(slot < length, scores, masked_score)
    weights = jnp.exp(scores - jnp.max(scores, axis=0, keepdims=True))
    return weights / jnp.sum(weights, axis=0, keepdims=True)


def text_kernel(
    outer, w_out, w_cq, w_cout, nx, me_ref, x_ref, o_ref, mod_ref, w_refs, text_ref, length_ref,
    a1_ref, x1_ref, hc_ref, qc_ref, oc_ref, x2_ref, h3_ref,
    buf, sems, acc, q_t, v_t,
):
    pieces = Pieces(w_refs, me_ref, outer, buf, sems, nx)

    def product(left, win, dest, wait=False):
        for x in range(nx):
            if wait:
                pieces.wait(x)
            block = mm(left, buf[x, :, win.start : win.stop])[:, win.off : win.off + win.n]
            put([dest], x * win.n, block)

    product(o_ref[...], w_out, a1_ref, wait=True)
    after_a = x_ref[...].astype(f32) + mod_ref[2:3, :] * a1_ref[...]
    x1_ref[...] = after_a
    hidden = stats(after_a)[0].astype(bf16)
    hc_ref[...] = hidden
    product(hidden, w_cq, qc_ref)
    q_t[...] = qc_ref[...].astype(f32).T
    v_t[...] = text_ref[:, D:].astype(f32).T
    length = length_ref[0]
    for h in range(HEADS):
        probs = text_probs(text_ref, q_t, h, length).astype(bf16)
        acc[head(h), :] = mm(v_t[head(h), :].astype(bf16), probs)
    oc_ref[...] = acc[...].T.astype(bf16)
    product(oc_ref[...], w_cout, x2_ref)
    after_b = x1_ref[...] + x2_ref[...]
    x2_ref[...] = after_b
    h3_ref[...] = (
        stats(after_b)[0] * (1.0 + mod_ref[4:5, :]) + mod_ref[3:4, :]
    ).astype(bf16)


def ff_kernel(
    win, nx, ny, me_ref, h_ref, x2_ref, mod_ref, up_refs, down_ref,
    u_ref, g_ref, m_ref, x3_ref, h4_ref, up_buf, down_buf, up_sems, down_sems,
):
    ups = Pieces(up_refs, me_ref, win, up_buf, up_sems, nx)
    width = down_buf.shape[2]
    downs = down_blocks(up_refs, down_ref, me_ref, down_buf, down_sems, nx)
    hidden = h_ref[...]
    for x in range(nx):
        ups.wait(x)
        u = mm(hidden, up_buf[x])[:, win.off : win.off + win.n]
        put([u_ref], x * win.n, u)
        put([g_ref], x * win.n, 0.5 * u * (1.0 + gelu_parts(u)[0]))
    total = jnp.zeros(m_ref.shape, f32)
    for i in range(ny):
        downs.wait(i)
        total = total + mm_nt(g_ref[:, i * width : (i + 1) * width], down_buf[i])
    m_ref[...] = total
    after_c = x2_ref[...] + mod_ref[5:6, :] * total
    x3_ref[...] = after_c
    h4_ref[...] = (
        stats(after_c)[0] * (1.0 + mod_ref[7:8, :]) + mod_ref[6:7, :]
    ).astype(bf16)


def temporal_kernel(
    win, w_out, nx, frames, h_ref, da_ref, w_ref, row_clip, frame_clip,
    grad_ref, at_ref, dh_ref, buf, sems, pad, q_s, k_s, v_s, do_s, o_s, dq_s, dk_s, dv_s, qkv_s,
):
    pieces = Blocks(w_ref, buf, sems)
    o_ref, dqkv_ref = grad_ref.at[:, :D], grad_ref.at[:, D:]
    rows = h_ref.shape[0]
    spots = rows // frames
    hidden = h_ref[...]
    out_cols = slice(w_out.start, w_out.stop)
    pad[...] = jnp.zeros(pad.shape, bf16)
    total = jnp.zeros(h_ref.shape, f32)
    for x in range(nx):
        pieces.wait(x)
        block = mm(hidden, buf[x, :, win.start : win.stop])[:, win.off : win.off + win.n]
        put([qkv_s], x * win.n, block)
        take(pad, w_out.off, [da_ref], x * w_out.n, w_out.n)
        total = total + mm_nt(pad[:, : w_out.width], buf[x, :, out_cols])
    do_s[...] = total.astype(bf16).astype(f32)
    q_s[...] = qkv_s[:, :D].astype(f32)
    k_s[...] = qkv_s[:, D : 2 * D].astype(f32)
    v_s[...] = qkv_s[:, 2 * D :].astype(f32)
    dk_s[...] = jnp.zeros(dk_s.shape, f32)
    dv_s[...] = jnp.zeros(dv_s.shape, f32)

    def one_hot(size, feature, slot):
        first = lax.broadcasted_iota(jnp.int32, size, slot) * HEAD_DIM
        place = lax.broadcasted_iota(jnp.int32, size, feature)
        return jnp.where((place >= first) & (place < first + HEAD_DIM), 1.0, 0.0).astype(bf16)

    gather = one_hot((D, 128), 0, 1)
    spread = one_hot((128, D), 1, 0)

    def per_head(values):
        high = values.astype(bf16)
        low = (values - high.astype(f32)).astype(bf16)
        return mm(high, gather) + mm(low, gather)

    def every_frame(values):
        return jnp.broadcast_to(values[None], (frames, spots, D)).reshape(rows, D)

    def over_frames(values):
        return jnp.sum(values.reshape(frames, spots, values.shape[-1]), axis=0)

    def one_frame(f, carry):
        span = pl.ds(pl.multiple_of(f * spots, 8), spots)
        queries = every_frame(q_s[span, :])
        grads = every_frame(do_s[span, :])
        scores = per_head(queries * k_s[...]) * score_scale
        scores = jnp.where(row_clip[...] == frame_clip[f], scores, masked_score)
        scores = scores.reshape(frames, spots, 128)
        weights = jnp.exp(scores - jnp.max(scores, axis=0, keepdims=True))
        probs = weights / jnp.sum(weights, axis=0, keepdims=True)
        grad_probs = per_head(grads * v_s[...]).reshape(frames, spots, 128)
        inner = jnp.sum(probs * grad_probs, axis=0, keepdims=True)
        grad_scores = (probs * (grad_probs - inner)).reshape(rows, 128).astype(bf16)
        probs_wide = mm(probs.reshape(rows, 128).astype(bf16), spread)
        grads_wide = mm(grad_scores, spread)
        o_s[span, :] = over_frames(probs_wide * v_s[...])
        dq_s[span, :] = over_frames(grads_wide * k_s[...]) * score_scale
        dk_s[...] += grads_wide * queries
        dv_s[...] += probs_wide * grads
        return carry

    lax.fori_loop(0, frames, one_frame, 0)
    o_ref[...] = o_s[...].astype(bf16)
    for x in range(nx):
        block = mm(o_ref[...], buf[x, :, out_cols])[:, w_out.off : w_out.off + w_out.n]
        put([at_ref], x * w_out.n, block)
    dqkv_ref[:, :D] = dq_s[...].astype(bf16)
    dqkv_ref[:, D : 2 * D] = (dk_s[...] * score_scale).astype(bf16)
    dqkv_ref[:, 2 * D :] = dv_s[...].astype(bf16)
    pad[...] = jnp.zeros(pad.shape, bf16)
    total = jnp.zeros(dh_ref.shape, f32)
    for x in range(nx):
        take(pad, win.off, [dqkv_ref], x * win.n, win.n)
        total = total + mm_nt(pad[:, : win.width], buf[x, :, win.start : win.stop])
    dh_ref[...] = total.astype(bf16)


def mixed_kernel(at_ref, x3_ref, g_ref, mod_ref, keep_ref, y_ref, gate_ref):
    branch = at_ref[...].astype(f32)
    keep = keep_ref[0]
    y_ref[...] = (x3_ref[...] + keep * mod_ref[8:9, :] * branch).astype(bf16)
    gate_ref[...] = jnp.sum(keep * g_ref[...].astype(f32) * branch, axis=0, keepdims=True)


def column_sum(values):
    return jnp.sum(values, axis=0, keepdims=True)


def ff_back_kernel(
    win, nx, ny, me_ref, g_ref, dh4_ref, x3_ref, x2_ref, u_ref, m_ref, mod_ref, up_refs, down_ref,
    grad_ref, dx2_ref, sum_ref, up_buf, down_buf, up_sems, down_sems, pad,
):
    ff = u_ref.shape[1]
    du_s, dm_ref = grad_ref.at[:, :ff], grad_ref.at[:, ff:]
    width = down_buf.shape[2]
    downs = down_blocks(up_refs, down_ref, me_ref, down_buf, down_sems, nx)
    ups = Pieces(up_refs, me_ref, win, up_buf, up_sems, nx)
    dh4 = dh4_ref[...].astype(f32)
    normed, inv_std = stats(x3_ref[...])
    dx3 = g_ref[...].astype(f32) + stats_back(dh4 * (1.0 + mod_ref[7:8, :]), normed, inv_std)
    sum_ref[0:1, :] = column_sum(dh4)
    sum_ref[1:2, :] = column_sum(dh4 * normed)
    sum_ref[2:3, :] = column_sum(dx3 * m_ref[...])
    dm = (mod_ref[5:6, :] * dx3).astype(bf16)
    dm_ref[...] = dm
    for i in range(ny):
        downs.wait(i)
        grad = mm(dm, down_buf[i])
        u = u_ref[:, i * width : (i + 1) * width]
        tanh, square, c = gelu_parts(u)
        slope = 0.5 * (1.0 + tanh) + 0.5 * u * (1.0 - tanh * tanh) * (
            c * (1.0 + 3.0 * 0.044715 * square)
        )
        du_s[:, i * width : (i + 1) * width] = (grad * slope).astype(bf16)
    pad[...] = jnp.zeros(pad.shape, bf16)
    total = jnp.zeros(dx2_ref.shape, f32)
    for x in range(nx):
        ups.wait(x)
        take(pad, win.off, [du_s], x * win.n, win.n)
        total = total + mm_nt(pad[...], up_buf[x])
    normed, inv_std = stats(x2_ref[...])
    sum_ref[3:4, :] = column_sum(total)
    sum_ref[4:5, :] = column_sum(total * normed)
    sum_ref[5:8, :] = jnp.zeros((3, D), f32)
    dx2_ref[...] = dx3 + stats_back(total * (1.0 + mod_ref[4:5, :]), normed, inv_std)


def text_back_kernel(
    outer, w_out, w_cq, w_cout, nx, me_ref, dx2_ref, x1_ref, a1_ref, mod_ref, w_refs, qc_ref, text_ref,
    length_ref, grad_ref, dx1_ref, do1_ref, dtext_ref, gate_ref,
    buf, sems, pad, acc, q_t, do_t, k_t, do_s, dtext_s,
):
    dac_ref, dqc_ref, da1_ref = [grad_ref.at[:, i * D : (i + 1) * D] for i in range(3)]
    pieces = Pieces(w_refs, me_ref, outer, buf, sems, nx)

    def product(source, win, wait=False):
        pad[...] = jnp.zeros(pad.shape, bf16)
        total = jnp.zeros(dx2_ref.shape, f32)
        for x in range(nx):
            if wait:
                pieces.wait(x)
            take(pad, win.off, [source], x * win.n, win.n)
            total = total + mm_nt(pad[:, : win.width], buf[x, :, win.start : win.stop])
        return total

    dx2 = dx2_ref[...]
    dac_ref[...] = dx2.astype(bf16)
    grad_o = product(dac_ref, w_cout, wait=True).astype(bf16)
    do_s[...] = grad_o
    do_t[...] = grad_o.astype(f32).T
    q_t[...] = qc_ref[...].astype(f32).T
    k_t[...] = text_ref[:, :D].astype(f32).T
    length = length_ref[0]
    for h in range(HEADS):
        probs = text_probs(text_ref, q_t, h, length)
        values = text_ref[:, D + h * HEAD_DIM : D + (h + 1) * HEAD_DIM]
        grad_probs = mm(values, do_t[head(h), :].astype(bf16))
        inner = jnp.sum(probs * grad_probs, axis=0, keepdims=True)
        grad_scores = (probs * (grad_probs - inner)).astype(bf16)
        dtext_s[:, head(h)] = mm(grad_scores, qc_ref[:, head(h)]) * score_scale
        dtext_s[:, D + h * HEAD_DIM : D + (h + 1) * HEAD_DIM] = mm(
            probs.astype(bf16), do_s[:, head(h)]
        )
        acc[head(h), :] = mm(k_t[head(h), :].astype(bf16), grad_scores) * score_scale
    width = dtext_ref.shape[2]
    for x in range(nx):
        dtext_ref[x] = dtext_s[:, x * width : (x + 1) * width].astype(bf16)
    dqc_ref[...] = acc[...].T.astype(bf16)
    normed, inv_std = stats(x1_ref[...])
    dx1 = dx2 + stats_back(product(dqc_ref, w_cq), normed, inv_std)
    dx1_ref[...] = dx1
    gate_ref[...] = column_sum(dx1 * a1_ref[...])
    da1_ref[...] = (mod_ref[2:3, :] * dx1).astype(bf16)
    do1_ref[...] = product(da1_ref, w_out).astype(bf16)


def spatial_back_kernel(pieces, *refs):
    q_ref, do_ref, o_ref, lse_ref = refs[:4]
    kv_refs = refs[4 : 4 + pieces]
    (
        dq_ref, dkv_ref,
        q_t, do_t, o_t, k_t, dq_t, q_heads, do_heads, k_heads, v_heads, dk_heads, dv_heads,
    ) = refs[4 + pieces :]
    rows = q_ref.shape[0]
    q_t[...] = q_ref[...].astype(f32).T
    do_t[...] = do_ref[...].astype(f32).T
    o_t[...] = o_ref[...].astype(f32).T
    stage_heads(q_heads, 0, q_ref, 0)
    stage_heads(do_heads, 0, do_ref, 0)
    for i, kv in enumerate(kv_refs):
        k_t[:, i * rows : (i + 1) * rows] = kv[:, :D].astype(f32).T
        stage_heads(k_heads, i * rows, kv, 0)
        stage_heads(v_heads, i * rows, kv, D)

    def one_head(h, carry):
        span = pl.ds(pl.multiple_of(h * HEAD_DIM, 8), HEAD_DIM)
        grad_o = do_t[span, :]
        inner = jnp.sum(grad_o * o_t[span, :], axis=0, keepdims=True)
        scores = mm(k_heads[h, :, :HEAD_DIM], q_t[span, :].astype(bf16)) * log2_scale
        probs = jnp.exp2(scores - lse_ref[pl.ds(h, 1), :])
        grad_probs = mm(v_heads[h, :, :HEAD_DIM], grad_o.astype(bf16))
        grad_scores = (probs * (grad_probs - inner)).astype(bf16)
        dv_heads[h, :, :HEAD_DIM] = mm(probs.astype(bf16), do_heads[h, :, :HEAD_DIM]).astype(bf16)
        dk_heads[h, :, :HEAD_DIM] = (
            mm(grad_scores, q_heads[h, :, :HEAD_DIM]) * score_scale
        ).astype(bf16)
        dq_t[span, :] = mm(k_t[span, :].astype(bf16), grad_scores) * score_scale
        return carry

    lax.fori_loop(0, HEADS, one_head, 0)
    dq_ref[...] = dq_t[...].T.astype(bf16)
    for i in range(pieces):
        span = slice(i * rows, (i + 1) * rows)
        for h in range(HEADS):
            dkv_ref[i, :, head(h)] = dk_heads[h, span, :HEAD_DIM]
            dkv_ref[i, :, D + h * HEAD_DIM : D + (h + 1) * HEAD_DIM] = dv_heads[
                h, span, :HEAD_DIM
            ]


def qkv_back_kernel(
    win, nx, me_ref, dq_ref, own_ref, come_ref, x_ref, mod_ref, dx1_ref, w_refs,
    grad_ref, gx_ref, sum_ref, buf, sems, pad,
):
    dkv_ref = grad_ref.at[:, D:]
    grad_ref[:, :D] = dq_ref[...]
    pieces = Pieces(w_refs, me_ref, win, buf, sems, nx)
    dkv_ref[...] = (own_ref[...].astype(f32) + come_ref[...].astype(f32)).astype(bf16)
    pad[...] = jnp.zeros(pad.shape, bf16)
    total = jnp.zeros(dx1_ref.shape, f32)
    for x in range(nx):
        pieces.wait(x)
        take(pad, win.off, [grad_ref], x * win.n, win.n)
        total = total + mm_nt(pad[...], buf[x])
    normed, inv_std = stats(x_ref[...].astype(f32))
    sum_ref[0:1, :] = column_sum(total)
    sum_ref[1:2, :] = column_sum(total * normed)
    gx_ref[...] = (
        dx1_ref[...] + stats_back(total * (1.0 + mod_ref[1:2, :]), normed, inv_std)
    ).astype(bf16)


def turn_rows(turn, at, value, me_y, ny):
    rows = turn.shape[0] // ny
    flipped = value.astype(f32).T.astype(bf16)
    for y in range(ny):
        place = pl.ds(pl.multiple_of((y ^ me_y) * rows, 16), rows)
        turn[place, at : at + value.shape[0]] = flipped[y * rows : (y + 1) * rows]


def write_blocks(outs, half, columns, block, first=0):
    some_send, rest_send, some_keep, rest_keep = outs
    rows, each = block.shape[0] // 4, some_keep.shape[1] // 2
    step = pl.program_id(0)

    def write(ref, at, y):
        start = at * each + first
        ref[0, start : start + rows, columns] = block[y * rows : (y + 1) * rows]

    @pl.when(step < half)
    def _():
        for at in range(2):
            write(some_keep, at, at)
            write(some_send, at, 2 + at)

    @pl.when(step >= half)
    def _():
        for at in range(2):
            write(rest_keep, at, 2 * at)
            write(rest_send, at, 2 * at + 1)


def block_outs(nx, depth, lanes):
    half = nx // 4
    size = (1, depth // 2, lanes)
    some = pl.BlockSpec(size, lambda t, me: (jnp.minimum(t, half - 1), 0, 0))
    rest = pl.BlockSpec(size, lambda t, me: (jnp.maximum(t - half, 0), 0, 0))
    return [shape(half, depth // 2, lanes, dtype=bf16)] * 4, [some, rest, some, rest]


def view(refs, place):
    k, first, last = place
    return refs[k].at[:, first:last]


def weight_kernel(nx, ny, lanes, count, pairs, me_ref, *refs):
    sides, outs = (refs[:count], refs[count : 2 * count]), refs[2 * count : 2 * count + 4]
    pads, turned = refs[2 * count + 4 :: 2], refs[2 * count + 5 :: 2]
    step = pl.program_id(0)
    x = me_ref[0] ^ (2 * step)
    rows = refs[0].shape[0]

    @pl.when(step == 0)
    def _():
        for (left, _), turn in zip(pairs, turned):
            for i, side in enumerate(sides):
                turn_rows(turn, i * rows, view(side, left)[...], me_ref[1], ny)

    at = 0
    for (_, right), pad, turn in zip(pairs, pads, turned):
        n = pad.shape[1]
        for i in range(nx):

            @pl.when(x == i)
            def _():
                for k, side in enumerate(sides):
                    take(pad.at[k * rows : (k + 1) * rows], 0, [view(side, right)], i * n, n)

        block = mm(turn[...], pad[...]).astype(bf16)
        write_blocks(outs, nx // 4, slice(at, at + n), block)
        at += n
    if at < lanes:
        write_blocks(outs, nx // 4, slice(at, lanes), jnp.zeros((D, lanes - at), bf16))


def weight_grads(nx, me, own, other, pairs):
    widths = [(last - first) // nx for _, (_, first, last) in pairs]
    lanes = padded(sum(widths))
    rows = own[0].shape[0]
    scratch = []
    for width in widths:
        scratch += [pltpu.VMEM((2 * rows, width), bf16), pltpu.VMEM((D, 2 * rows), bf16)]
    outs, out_specs = block_outs(nx, D, lanes)
    return pl.pallas_call(
        functools.partial(weight_kernel, nx, lax.axis_size("gy"), lanes, len(own), pairs),
        out_shape=outs,
        grid_spec=pltpu.PrefetchScalarGridSpec(
            num_scalar_prefetch=1,
            grid=(nx // 2,),
            in_specs=[vmem() for _ in range(2 * len(own))],
            out_specs=out_specs,
            scratch_shapes=scratch,
        ),
        compiler_params=pltpu.CompilerParams(vmem_limit_bytes=56 << 20),
        cost_estimate=cost(9),
    )(me, *own, *other)


def whole_kernel(nx, lanes, pairs, *refs):
    count = 1 + max(k for pair in pairs for k, _, _ in pair)
    ins, out_ref = refs[:count], refs[count]
    pads, turned = refs[count + 1 :: 2], refs[count + 2 :: 2]
    x = pl.program_id(0)

    @pl.when(x == 0)
    def _():
        for (left, _), turn in zip(pairs, turned):
            turn[...] = view(ins, left)[...].astype(f32).T.astype(bf16)

    at = 0
    for (_, right), pad, turn in zip(pairs, pads, turned):
        n = pad.shape[1]
        for i in range(nx):

            @pl.when(x == i)
            def _():
                take(pad, 0, [view(ins, right)], i * n, n)

        out_ref[0, :, at : at + n] = mm(turn[...], pad[...]).astype(bf16)
        at += n
    if at < lanes:
        out_ref[0, :, at:] = jnp.zeros((D, lanes - at), bf16)


def whole_grads(nx, arrays, pairs):
    widths = [(last - first) // nx for _, (_, first, last) in pairs]
    lanes = padded(sum(widths))
    rows = arrays[0].shape[0]
    scratch = []
    for width in widths:
        scratch += [pltpu.VMEM((rows, width), bf16), pltpu.VMEM((D, rows), bf16)]
    return pl.pallas_call(
        functools.partial(whole_kernel, nx, lanes, pairs),
        out_shape=shape(nx, D, lanes, dtype=bf16),
        grid=(nx,),
        in_specs=[vmem() for _ in arrays],
        out_specs=pl.BlockSpec((1, D, lanes), lambda x: (x, 0, 0)),
        scratch_shapes=scratch,
        compiler_params=pltpu.CompilerParams(vmem_limit_bytes=56 << 20),
        cost_estimate=cost(13),
    )(*arrays)


def up_grads(nx, me, own, other, folding):
    rows, ff = own[2].shape
    n = ff // nx
    ny = lax.axis_size("gy")
    start = padded(n)
    width = ff // ny
    fold = fold_width(width)
    each = D // nx

    def kernel(me_ref, *refs):
        sides, outs = (refs[:3], refs[3:6]), refs[6:10]
        turn, pad, down_turn, down_pad = refs[-4:]
        step = pl.program_id(0)
        x = me_ref[0] ^ (2 * step)

        @pl.when(step == 0)
        def _():
            for k, (h_ref, grad_ref, _) in enumerate(sides):
                turn_rows(turn, k * rows, h_ref[...], me_ref[1], ny)
                if folding:
                    down_turn[:, k * rows : (k + 1) * rows] = (
                        grad_ref[:, ff:].astype(f32).T.astype(bf16)
                    )

        for i in range(nx):

            @pl.when(x == i)
            def _():
                for k, (_, grad_ref, _) in enumerate(sides):
                    pad[k * rows : (k + 1) * rows] = grad_ref[:, i * n : (i + 1) * n]

        write_blocks(outs, nx // 4, slice(0, n), mm(turn[...], pad[...]).astype(bf16))
        if n < start:
            write_blocks(outs, nx // 4, slice(n, start), jnp.zeros((D, start - n), bf16))
        if not folding:
            return
        left = down_turn[pl.ds(pl.multiple_of(x * each, 16), each), :]
        for y in range(ny):
            columns = slice(y * width, (y + 1) * width)
            block = mm(left[:, :rows], sides[0][2][:, columns])
            block = (block + mm(left[:, rows:], sides[1][2][:, columns])).astype(bf16)
            top = (y ^ me_ref[1]) * 2 * each
            down_pad[pl.ds(pl.multiple_of(top, 16), each), :] = block[:, :fold]
            low = pl.multiple_of(top + each, 16)
            down_pad[pl.ds(low, each), : width - fold] = block[:, fold:]
            down_pad[pl.ds(low, each), width - fold :] = jnp.zeros((each, 2 * fold - width), bf16)
        write_blocks(outs, nx // 4, slice(0, fold), down_pad[...], D // ny)

    outs, out_specs = block_outs(nx, 2 * D if folding else D, start)
    return pl.pallas_call(
        kernel,
        out_shape=outs,
        grid_spec=pltpu.PrefetchScalarGridSpec(
            num_scalar_prefetch=1,
            grid=(nx // 2,),
            in_specs=[vmem()] * 6,
            out_specs=out_specs,
            scratch_shapes=[
                pltpu.VMEM((D, 2 * rows), bf16),
                pltpu.VMEM((2 * rows, n), bf16),
                pltpu.VMEM((D, 2 * rows), bf16),
                pltpu.VMEM((D, fold), bf16),
            ],
        ),
        compiler_params=pltpu.CompilerParams(vmem_limit_bytes=56 << 20),
        cost_estimate=cost(16),
    )(me, *own, *other)


def down_grads(dm, g):
    rows = g.shape[0]
    ny = lax.axis_size("gy")
    width = g.shape[1] // ny

    def kernel(dm_ref, g_ref, out_ref, turn):
        @pl.when(pl.program_id(0) == 0)
        def _():
            turn[...] = dm_ref[...].astype(f32).T.astype(bf16)

        out_ref[0] = mm(turn[...], g_ref[...]).astype(bf16)

    return pl.pallas_call(
        kernel,
        out_shape=shape(ny, D, width, dtype=bf16),
        grid=(ny,),
        in_specs=[vmem(), pl.BlockSpec((rows, width), lambda i: (0, i))],
        out_specs=pl.BlockSpec((1, D, width), lambda i: (i, 0, 0)),
        scratch_shapes=[pltpu.VMEM((D, rows), bf16)],
        compiler_params=pltpu.CompilerParams(vmem_limit_bytes=56 << 20),
        cost_estimate=cost(12),
    )(dm, g)


def after(value, *others):
    return lax.optimization_barrier((value, others))[0]


class Gather:
    def __init__(self, shard):
        self.line = [shard]

    def along(self, fars, *others):
        shard = after(self.line[0], *others)
        new = [swap(shard, "gx", 2 * far) for far in fars]
        self.line = self.line + new
        return new

    def first(self, *others):
        line = after(self.line, *others)
        half = len(line) // 2
        some, rest = jnp.stack(line[:half]), jnp.stack(line[half:])
        self.near = (some, rest)
        self.far = [swap(some, "gy", 1), swap(rest, "gy", 2)]
        return self.far

    def second(self, *others):
        far = after(self.far, *others)
        self.own = [jnp.stack(pair) for pair in zip(self.near, far)]
        self.new = [swap(self.own[0], "gy", 2), swap(self.own[1], "gy", 1)]
        return self.new

    def own_core(self, *others):
        self.own_other = [swap(array, "gx", 1) for array in after(self.own, *others)]
        return self.own_other

    def new_core(self, *others):
        self.new_other = [swap(array, "gx", 1) for array in after(self.new, *others)]
        return self.new_other

    def arrays(self):
        pairs = ((self.own, self.new), (self.own_other, self.new_other))
        return tuple(side[i] for own, new in pairs for i in range(2) for side in (own, new))


def gather_rows(shard):
    ny = lax.axis_size("gy")
    whole = lax.all_gather(shard, row_axes, axis=0, tiled=True)
    return whole.reshape(ny, -1, shard.shape[1])


def total(*terms):
    return sum(term.astype(f32) for term in terms).astype(bf16)


class Scatter:
    def __init__(self, some_send, rest_send, some_keep, rest_keep):
        self.sent = [some_send, rest_send]
        self.kept = [some_keep, rest_keep]
        half, depth, lanes = some_keep.shape
        self.half, self.size = half, (half, 2, depth // 2, lanes)

    def first(self, *others):
        some, rest = after(self.sent, *others)
        self.come = [swap(some, "gy", 2), swap(rest, "gy", 1)]
        return self.come

    def second(self, *others):
        kept = [array.reshape(self.size) for array in self.kept]
        come = [array.reshape(self.size) for array in after(self.come, *others)]
        self.near = list(zip(kept, come))
        self.sent = [total(mine[:, 1], theirs[:, 1]) for mine, theirs in self.near]
        self.come = [swap(self.sent[0], "gy", 1), swap(self.sent[1], "gy", 2)]
        return self.come

    def line(self, *others):
        come = after(self.come, *others)
        some, rest = [
            total(mine[:, 0], theirs[:, 0], last)
            for (mine, theirs), last in zip(self.near, come)
        ]
        self.ends = [some[i] for i in range(self.half)] + [rest[i] for i in range(self.half)]
        self.got = []

    def along(self, fars, *others):
        new = [swap(after(self.ends[far], *others), "gx", 2 * far) for far in fars]
        self.got = self.got + new
        return new

    def result(self):
        return sum([term.astype(f32) for term in self.got], self.ends[0].astype(f32))


def scatter(blocks, axes):
    flat = blocks.reshape(-1, blocks.shape[-1])
    return lax.psum_scatter(flat, axes, scatter_dimension=0, tiled=True).astype(f32)


def swap(values, axis, mask):
    return lax.ppermute(values, axis, [(i, i ^ mask) for i in range(lax.axis_size(axis))])


def reorder(values):
    devices = lax.axis_size(row_axes)
    return lax.all_to_all(
        values.reshape(devices, values.shape[0] // devices, values.shape[1]),
        row_axes,
        split_axis=0,
        concat_axis=0,
        tiled=True,
    ).reshape(values.shape)


def pad_lanes(values):
    return jnp.pad(values, ((0, 0), (0, padded(values.shape[1]) - values.shape[1])))


def condition(timesteps, pooled_text):
    half_width = D // 2
    frequency = jnp.exp(
        -math.log(10000.0) * jnp.arange(half_width).astype(jnp.float32) / half_width
    )
    angles = timesteps.astype(jnp.float32)[:, None] * frequency[None, :]
    embedded = jnp.concatenate([jnp.cos(angles), jnp.sin(angles)], axis=1)
    return jax.nn.silu(embedded + pooled_text)


def local(
    tokens,
    text_states,
    pooled_text,
    timesteps,
    frame_counts,
    still_clips,
    text_lengths,
    w_ada,
    w_sqkv,
    w_sout,
    w_cq,
    w_ckv,
    w_cout,
    w_up,
    w_down,
    w_tqkv,
    w_tout,
    grad_out,
):
    nx, ny = lax.axis_size("gx"), lax.axis_size("gy")
    gx, gy = lax.axis_index("gx"), lax.axis_index("gy")
    devices = nx * ny
    me = jnp.stack([gx, gy]).astype(jnp.int32)
    device = gy * nx + gx
    rows = tokens.shape[0]
    frame_devs = FRAME // rows
    frames = rows * devices // FRAME
    k_rows = w_ada.shape[0]
    clip_ends = jnp.cumsum(frame_counts)
    clip_here = jnp.sum((clip_ends <= device // frame_devs).astype(jnp.int32))
    clip_mark = jnp.arange(CLIPS) == clip_here
    clip_pick = clip_mark.astype(f32)
    keep_here = (1.0 - jnp.sum(clip_pick * still_clips.astype(f32))).reshape(1)
    length_here = jnp.sum(jnp.where(clip_mark, text_lengths, 0)).reshape(1)
    frame_clip = jnp.sum(
        (clip_ends[None, :] <= jnp.arange(frames)[:, None]).astype(jnp.int32), axis=1
    ).astype(f32)
    row_clip = jnp.repeat(frame_clip, rows // frames)[:, None]

    n_sqkv, n_one, n_up = w_sqkv.shape[1], w_sout.shape[1], w_up.shape[1]
    shard_a = pad_lanes(jnp.concatenate([w_sqkv, w_sout, w_cq, w_cout], axis=1))
    shard_d = pad_lanes(jnp.concatenate([w_tqkv, w_tout], axis=1))
    shard_up = pad_lanes(w_up)
    each = w_down.shape[1]
    fold = fold_width(w_down.shape[0])
    trees = each % 16 == 0 and 2 * each == k_rows and fold == padded(n_up)
    if trees:
        turned = w_down.T
        rest = jnp.pad(turned[:, fold:], ((0, 0), (0, 2 * fold - turned.shape[1])))
        shard_up = jnp.concatenate([shard_up, turned[:, :fold], rest])
    fars = range(1, nx // 2)
    get_a, get_up = Gather(shard_a), Gather(shard_up)
    get_a.along(fars)
    cond_all = condition(timesteps, pooled_text)
    cond_rows = lax.dynamic_slice_in_dim(cond_all, gy * k_rows, k_rows, axis=1)
    mod_part = jnp.dot(cond_rows, w_ada.astype(f32), precision=highest)
    mod_part = mod_part + swap(mod_part, "gy", 1)
    mod_all = (mod_part + swap(mod_part, "gy", 2))[None]
    mod_first = mod_all
    own_text = text_states.shape[0]
    text_rows = text_states.reshape(own_text // CLIPS, CLIPS, -1).transpose(1, 0, 2)
    depth = w_ckv.shape[0]
    text_rows = after(text_rows.reshape(own_text, ny, depth).transpose(1, 0, 2), mod_first)
    text_rows = lax.all_to_all(text_rows, "gy", split_axis=0, concat_axis=0, tiled=True)
    text_rows = lax.all_gather(text_rows, "gx", axis=0)
    bit = 1
    while bit < nx:
        if 2 * bit == nx:
            mod_all = after(mod_all, text_rows, *get_a.line)
        come = swap(mod_all, "gx", bit)
        mod_all = jnp.where(
            gx & bit != 0,
            jnp.concatenate([come, mod_all]),
            jnp.concatenate([mod_all, come]),
        )
        bit *= 2
    mod = lax.dynamic_index_in_dim(mod_all, clip_here, axis=1, keepdims=False).reshape(9, D)
    done = [mod_all]
    held = done
    done = get_a.first(*held) + get_up.along(fars[:2], *held)
    text_block = (
        after(text_rows, *held)
        .reshape(nx, ny, CLIPS, own_text // CLIPS, depth)
        .transpose(2, 1, 0, 3, 4)
        .reshape(own_text * devices, depth)
    )
    text_part = jnp.dot(text_block, w_ckv, preferred_element_type=f32)
    done += [text_part]
    grad_branch_d = (keep_here[0] * mod[8] * grad_out.astype(f32)).astype(bf16)
    held = done
    done = get_a.second(*held) + get_a.own_core()
    done += get_up.along(fars[2:], *held, *get_a.own_other)
    text_sum = lax.psum_scatter(
        after(text_part, *held), "gy", scatter_dimension=0, tiled=True
    )
    done += [text_sum]
    held = done
    up_far = get_up.first(*held)
    done = get_a.new_core(*held, *get_up.near)
    full_a = get_a.arrays()
    ff_width = w_down.shape[0]
    ff = ff_width * ny
    win_sqkv = Window(0, n_sqkv)
    at = n_sqkv
    win_rest = Window(at, at + 3 * n_one)
    win_sout, win_cq, win_cout = [
        Window(at + i * n_one, at + (i + 1) * n_one).inside(win_rest) for i in range(3)
    ]
    win_up = Window(0, n_up)
    win_d = Window(0, n_sqkv + n_one)
    win_tqkv = Window(0, n_sqkv)
    win_tout = Window(n_sqkv, n_sqkv + n_one)


    win = win_sqkv
    hidden_a, query_a, pair_a = run(
        functools.partial(qkv_kernel, win, nx),
        [
            shape(rows, D, dtype=bf16),
            shape(rows, D, dtype=bf16),
            shape(rows, 2 * D, dtype=bf16),
        ],
        [smem()] + [vmem(), vmem(), hbm()],
        [pltpu.VMEM((nx, D, win.width), bf16), pltpu.SemaphoreType.DMA((nx,))],
        (me, tokens, after(mod, *done), full_a),
        9,
    )
    up_near = get_up.second(*up_far, pair_a)
    up_own = get_up.own_core()
    pairs = [after(pair_a, *up_far)]
    bit = frame_devs // 2
    while bit:
        pairs = pairs + [swap(p, "gx", bit) for p in pairs]
        bit //= 2
    text_all = lax.all_gather(after(text_sum, *held).astype(bf16), row_axes, axis=0)
    full_d = lax.all_gather(after(shard_d, text_all), ("gx", "gy"), axis=0, tiled=True)
    full_d = full_d.reshape(nx, D, -1)
    slots = own_text * devices // CLIPS
    text_all = text_all.reshape(ny, nx, -1, w_ckv.shape[1]).transpose(0, 2, 1, 3)
    text_all = text_all.reshape(CLIPS, slots, 2 * D)
    text_pairs = lax.dynamic_index_in_dim(text_all, clip_here, axis=0, keepdims=False)
    done = [*pairs, *up_own]
    query_a = after(query_a, *done)
    grad_branch_moved = reorder(after(grad_branch_d, *done))
    count = len(pairs)
    keys = count * rows
    out_a, lse_a = run(
        functools.partial(spatial_kernel, count),
        [shape(rows, D, dtype=bf16), shape(HEADS, rows)],
        [vmem() for _ in range(1 + count)],
        [
            pltpu.VMEM((D, rows), f32),
            pltpu.VMEM((D, keys), f32),
            pltpu.VMEM((HEADS, keys, 128), bf16),
            pltpu.VMEM((D, rows), f32),
        ],
        (query_a, *pairs),
        18,
    )

    done = [out_a, text_pairs, grad_branch_moved]
    out_a = after(out_a, *done)
    branch_a, after_a, hidden_b, query_b, out_b, after_b, hidden_c = run(
        functools.partial(text_kernel, win_rest, win_sout, win_cq, win_cout, nx),
        [
            shape(rows, D),
            shape(rows, D),
            shape(rows, D, dtype=bf16),
            shape(rows, D, dtype=bf16),
            shape(rows, D, dtype=bf16),
            shape(rows, D),
            shape(rows, D, dtype=bf16),
        ],
        [smem()] + [vmem(), vmem(), vmem(), hbm(), vmem(), smem()],
        [
            pltpu.VMEM((nx, D, win_rest.width), bf16),
            pltpu.SemaphoreType.DMA((nx,)),
            pltpu.VMEM((D, rows), f32),
            pltpu.VMEM((D, rows), f32),
            pltpu.VMEM((D, slots), f32),
        ],
        (me, tokens, out_a, mod, full_a, text_pairs, length_here),
        18,
    )

    done = [hidden_c, *up_near]
    done = get_up.new_core(*done)
    full_up = get_up.arrays()
    full_down = None if trees else gather_rows(after(w_down.T, *up_near))
    hidden_c = after(hidden_c, *done)
    pre_act, activated, branch_c, after_c, hidden_d = run(
        functools.partial(ff_kernel, win_up, nx, ny),
        [
            shape(rows, ff),
            shape(rows, ff, dtype=bf16),
            shape(rows, D),
            shape(rows, D),
            shape(rows, D, dtype=bf16),
        ],
        [smem()] + [vmem(), vmem(), vmem(), hbm(), hbm()],
        [
            pltpu.VMEM((nx, D, win_up.width), bf16),
            pltpu.VMEM((ny, D, ff_width), bf16),
            pltpu.SemaphoreType.DMA((nx,)),
            pltpu.SemaphoreType.DMA((ny,)),
        ],
        (me, hidden_c, after_b, mod, full_up, full_down),
        20,
    )

    rows_own = [hidden_a, out_a, hidden_b, out_b, hidden_c]
    rows_other = swap(after(jnp.stack(rows_own), hidden_d), "gx", 1)
    g_other = swap(after(activated, hidden_d), "gx", 1)
    moved_d = reorder(hidden_d)
    moved_d = after(moved_d, rows_other, g_other, grad_branch_moved)
    pad_width = max(win_tqkv.width, win_tout.width)
    grads_d, branch_moved, grad_hidden_moved = run(
        functools.partial(temporal_kernel, win_tqkv, win_tout, nx, frames),
        [
            shape(rows, 4 * D, dtype=bf16),
            shape(rows, D, dtype=bf16),
            shape(rows, D, dtype=bf16),
        ],
        [vmem(), vmem(), hbm(), vmem(), smem()],
        [
            pltpu.VMEM((nx, D, win_d.width), bf16),
            pltpu.SemaphoreType.DMA((nx,)),
            pltpu.VMEM((rows, pad_width), bf16),
        ]
        + [pltpu.VMEM((rows, D), f32)] * 8
        + [pltpu.VMEM((rows, 3 * D), bf16)],
        (moved_d, grad_branch_moved, full_d, row_clip, frame_clip),
        25,
    )
    grad_hidden_d = reorder(grad_hidden_moved)
    late = whole_grads(
        nx, [moved_d, grad_branch_moved, grads_d], [((0, 0, D), (2, D, 4 * D)), ((2, 0, D), (1, 0, D))]
    )
    late = scatter(after(late, grad_hidden_d), ("gx", "gy"))
    d_tqkv, d_tout = late[:, :n_sqkv], late[:, n_sqkv : n_sqkv + n_one]

    grads_c, grad_b, sums_c = run(
        functools.partial(ff_back_kernel, win_up, nx, ny),
        [
            shape(rows, ff + D, dtype=bf16),
            shape(rows, D),
            shape(8, D),
        ],
        [smem()] + [vmem()] * 7 + [hbm(), hbm()],
        [
            pltpu.VMEM((nx, D, win_up.width), bf16),
            pltpu.VMEM((ny, D, ff_width), bf16),
            pltpu.SemaphoreType.DMA((nx,)),
            pltpu.SemaphoreType.DMA((ny,)),
            pltpu.VMEM((rows, win_up.width), bf16),
        ],
        (me, grad_out, grad_hidden_d, after_c, after_b, pre_act, branch_c, mod, full_up, full_down),
        22,
    )
    grads_other = swap(grads_c, "gx", 1)
    up_terms = up_grads(
        nx,
        me,
        [hidden_c, grads_c, activated],
        [rows_other[4], grads_other, g_other],
        trees,
    )
    if not trees:
        d_down = scatter(down_grads(grads_c[:, ff:], activated), row_axes).T
    up_sums = Scatter(*up_terms)
    up_first = up_sums.first()
    grad_b = after(grad_b, *up_terms)

    kv_width = w_ckv.shape[1]
    grads_b, grad_a, grad_out_a, text_terms, d_gate1 = run(
        functools.partial(text_back_kernel, win_rest, win_sout, win_cq, win_cout, nx),
        [
            shape(rows, 3 * D, dtype=bf16),
            shape(rows, D),
            shape(rows, D, dtype=bf16),
            shape(nx, slots, kv_width, dtype=bf16),
            shape(1, D),
        ],
        [smem()] + [vmem()] * 4 + [hbm(), vmem(), vmem(), smem()],
        [
            pltpu.VMEM((nx, D, win_rest.width), bf16),
            pltpu.SemaphoreType.DMA((nx,)),
            pltpu.VMEM((rows, max(w.width for w in (win_sout, win_cq, win_cout))), bf16),
            pltpu.VMEM((D, rows), f32),
            pltpu.VMEM((D, rows), f32),
            pltpu.VMEM((D, rows), f32),
            pltpu.VMEM((D, slots), f32),
            pltpu.VMEM((rows, D), bf16),
            pltpu.VMEM((slots, 2 * D), f32),
        ],
        (me, grad_b, after_a, branch_a, mod, full_a, query_b, text_pairs, length_here),
        20,
    )
    text_terms = jnp.where(clip_mark[None, :, None, None], text_terms[:, None], 0)

    done = [grad_out_a]
    grads_b_other = swap(grads_b, "gx", 1)
    text_terms = lax.psum_scatter(
        after(text_terms, late).reshape(nx, -1, kv_width), "gx", scatter_dimension=0, tiled=True
    )
    branch_d = reorder(after(branch_moved, *done))
    grad_out_a = after(grad_out_a, *done)

    grad_query_a, grad_pairs = run(
        functools.partial(spatial_back_kernel, count),
        [shape(rows, D, dtype=bf16), shape(count, rows, 2 * D, dtype=bf16)],
        [vmem() for _ in range(4 + count)],
        [pltpu.VMEM((D, rows), f32)] * 3
        + [pltpu.VMEM((D, keys), f32), pltpu.VMEM((D, rows), f32)]
        + [pltpu.VMEM((HEADS, rows, 128), bf16)] * 2
        + [pltpu.VMEM((HEADS, keys, 128), bf16)] * 4,
        (query_a, grad_out_a, out_a, lse_a, *pairs),
        28,
    )
    done = [grad_pairs, grads_b_other, branch_d]
    grad_pairs = after(grad_pairs, *done)
    up_second = up_sums.second(*done)
    done = up_sums.sent
    bit = 1
    while bit < frame_devs // 2:
        half = grad_pairs.shape[0] // 2
        come = swap(grad_pairs[half:], "gx", bit)
        grad_pairs = (grad_pairs[:half].astype(f32) + come.astype(f32)).astype(bf16)
        bit *= 2
    come = swap(grad_pairs[1], "gx", bit)
    mixed, d_gate3 = run(
        mixed_kernel,
        [shape(rows, D, dtype=bf16), shape(1, D)],
        [vmem(), vmem(), vmem(), vmem(), smem()],
        [],
        (branch_d, after_c, grad_out, mod, keep_here),
        3,
    )

    cross = Scatter(
        *weight_grads(
            nx,
            me,
            [hidden_b, out_b, after(grads_b, grad_pairs, *done)],
            [rows_other[2], rows_other[3], grads_b_other],
            [((0, 0, D), (2, D, 2 * D)), ((1, 0, D), (2, 0, D))],
        )
    )
    done = [come, *cross.sent, *up_second]
    cross_first = cross.first(*done)
    up_sums.line(*done)
    up_done = up_sums.along(fars[2:])
    grad_query_a = after(grad_query_a, *done, *up_sums.ends)
    win = win_sqkv
    grads_a, grad_tokens, sums_a = run(
        functools.partial(qkv_back_kernel, win, nx),
        [shape(rows, 3 * D, dtype=bf16), shape(rows, D, dtype=bf16), shape(2, D)],
        [smem()] + [vmem()] * 6 + [hbm()],
        [
            pltpu.VMEM((nx, D, win.width), bf16),
            pltpu.SemaphoreType.DMA((nx,)),
            pltpu.VMEM((rows, win.width), bf16),
        ],
        (me, grad_query_a, grad_pairs[0], come, tokens, mod, grad_a, full_a),
        11,
    )
    grads_a_other = swap(grads_a, "gx", 1)
    early = Scatter(
        *weight_grads(
            nx,
            me,
            [hidden_a, out_a, grads_a, grads_b],
            [rows_other[0], rows_other[1], grads_a_other, grads_b_other],
            [((0, 0, D), (2, 0, 3 * D)), ((1, 0, D), (3, 2 * D, 3 * D))],
        )
    )
    done = [*cross_first, *early.sent]
    cross_second = cross.second(*done)
    done = [*cross_second, *up_done]
    up_done = up_done + up_sums.along(fars[:2])
    early_first = early.first(*done)
    cross.line(*done)
    cross_done = cross.along(fars, *up_done)
    done = [*early_first, *up_done]
    early_second = early.second(*done)
    early.line(*early_second)
    early_done = early.along(fars)
    grad_mod = jnp.concatenate(
        [sums_a, d_gate1, sums_c[3:5], sums_c[2:3], sums_c[0:2], d_gate3]
    ).reshape(-1)
    grad_mod = after(lax.all_gather(grad_mod, row_axes, axis=0), *early.ends)
    width = w_ada.shape[1]
    grad_mod = lax.dynamic_slice_in_dim(grad_mod, gx * width, width, axis=1)
    device_clip = jnp.sum(
        (clip_ends[None, :] <= (jnp.arange(devices) // frame_devs)[:, None]).astype(jnp.int32),
        axis=1,
    )
    device_pick = (jnp.arange(CLIPS)[:, None] == device_clip[None, :]).astype(f32)
    grad_mod = jnp.dot(device_pick, grad_mod, precision=highest)
    d_ada = lax.dot_general(
        cond_rows, grad_mod, (((0,), (0,)), ((), ())), precision=highest
    )
    text_terms = after(text_terms[0], *early.ends).astype(f32)
    text_terms = text_terms + swap(text_terms.astype(bf16), "gy", 1).astype(f32)
    text_terms = text_terms + swap(text_terms.astype(bf16), "gy", 2).astype(f32)
    text_grad = text_terms.astype(bf16)
    d_ckv = jnp.einsum("rd,re->de", text_block, text_grad, preferred_element_type=f32)
    up, cross, early = up_sums.result(), cross.result(), early.result()
    d_up = up[:k_rows, :n_up]
    if trees:
        down = up[k_rows:]
        d_down = jnp.concatenate([down[:each], down[each:, : ff_width - fold]], axis=1).T
    d_cq, d_cout = cross[:, :n_one], cross[:, n_one : 2 * n_one]
    d_sqkv, d_sout = early[:, :n_sqkv], early[:, n_sqkv : n_sqkv + n_one]

    return (
        mixed,
        grad_tokens,
        d_ada,
        d_sqkv,
        d_sout,
        d_cq,
        d_ckv,
        d_cout,
        d_up,
        d_down,
        d_tqkv,
        d_tout,
    )


def solution(mesh):
    rows = P(("gy", "gx"), None)
    both = P("gy", "gx")
    return jax.shard_map(
        local,
        mesh=mesh,
        in_specs=(rows, rows, P(), P(), P(), P(), P()) + (both,) * 10 + (rows,),
        out_specs=(rows, rows) + (both,) * 10,
        check_vma=False,
    )
```

```python
import functools
import math

import jax
import jax.numpy as jnp
from jax import lax
from jax.experimental import pallas as pl
from jax.experimental.pallas import tpu as pltpu
from jax.sharding import PartitionSpec as P

D = 1152
HEADS = 16
HEAD_DIM = 72
FRAME = 1024
CLIPS = 4

norm_eps = 1e-06
masked_score = -1e30
highest = lax.Precision.HIGHEST
f32 = jnp.float32
bf16 = jnp.bfloat16
score_scale = HEAD_DIM ** (-0.5)
log2_scale = score_scale * math.log2(math.e)
row_axes = ("gy", "gx")
nt = (((1,), (1,)), ((), ()))


def vmem():
    return pl.BlockSpec(memory_space=pltpu.VMEM)


def smem():
    return pl.BlockSpec(memory_space=pltpu.SMEM)


def hbm():
    return pl.BlockSpec(memory_space=pl.ANY)


def shape(*size, dtype=f32):
    return jax.ShapeDtypeStruct(size, dtype)


def cost(micros):
    return pl.CostEstimate(flops=micros * 20000000, bytes_accessed=0, transcendentals=0)


def run(kernel, outs, specs, scratch, args, micros):
    flat, tree = jax.tree.flatten(tuple(args))
    flat_specs = []
    for arg, spec in zip(args, specs):
        flat_specs += [spec] * len(jax.tree.leaves(arg))

    def grouped(*refs):
        kernel(*jax.tree.unflatten(tree, refs[: len(flat)]), *refs[len(flat) :])

    return pl.pallas_call(
        grouped,
        out_shape=outs,
        in_specs=flat_specs,
        out_specs=[vmem() for _ in outs],
        scratch_shapes=scratch,
        compiler_params=pltpu.CompilerParams(vmem_limit_bytes=56 << 20),
        cost_estimate=cost(micros),
    )(*flat)


class Window:
    def __init__(self, lo, hi):
        self.lo, self.hi = lo, hi
        self.start = lo // 128 * 128
        self.stop = -(-hi // 128) * 128
        self.off = lo - self.start
        self.n = hi - lo
        self.width = self.stop - self.start

    def inside(self, outer):
        return Window(self.lo - outer.start, self.hi - outer.start)


def padded(lanes):
    return -(-lanes // 128) * 128


def piece_places(nx):
    half = nx // 4
    for core in range(2):
        for k, (first, last, low) in enumerate(((1, 0, 0), (1, 2, 0), (2, 0, half), (2, 1, half))):
            for i in range(2):
                for j in range(half):
                    yield core * 4 + k, i, j, (2 * (low + j)) ^ core, (first * i) ^ last


class Pieces:
    def __init__(self, sources, me, window, buffer, sems, nx):
        rows = buffer.shape[1] // 4
        columns = slice(window.start, window.stop)
        for k, i, j, far_x, far_y in piece_places(nx):
            x, y = me[0] ^ far_x, me[1] ^ far_y
            pltpu.make_async_copy(
                sources[k].at[i, j, :rows, columns],
                buffer.at[x, pl.ds(pl.multiple_of(y * rows, 16), rows), :],
                sems.at[x],
            ).start()
        self.buffer, self.sems = buffer, sems

    def wait(self, x):
        pltpu.make_async_copy(self.buffer.at[x], self.buffer.at[x], self.sems.at[x]).wait()


class Blocks:
    def __init__(self, source, buffer, sems):
        self.copies = [
            pltpu.make_async_copy(source.at[i], buffer.at[i], sems.at[i])
            for i in range(source.shape[0])
        ]
        for copy in self.copies:
            copy.start()

    def wait(self, i):
        self.copies[i].wait()


class Folded:
    def __init__(self, sources, me, buffer, sems, nx):
        rows = buffer.shape[1] // nx
        base = sources[0].shape[2] - 2 * rows
        width = buffer.shape[2]
        fold = fold_width(width)
        for k, i, j, far_x, far_y in piece_places(nx):
            x, y = me[0] ^ far_x, me[1] ^ far_y
            place = pl.ds(pl.multiple_of(x * rows, 16), rows)
            for top, columns in ((base, slice(0, fold)), (base + rows, slice(fold, width))):
                pltpu.make_async_copy(
                    sources[k].at[i, j, top : top + rows, : columns.stop - columns.start],
                    buffer.at[y, place, columns],
                    sems.at[y],
                ).start()
        self.buffer, self.sems = buffer, sems

    def wait(self, y):
        pltpu.make_async_copy(self.buffer.at[y], self.buffer.at[y], self.sems.at[y]).wait()


def fold_width(width):
    return padded(width // 2)


def down_blocks(up_refs, down_ref, me_ref, buf, sems, nx):
    if down_ref is None:
        return Folded(up_refs, me_ref, buf, sems, nx)
    return Blocks(down_ref, buf, sems)


def stats(values):
    centred = values - jnp.mean(values, axis=-1, keepdims=True)
    inv_std = lax.rsqrt(jnp.mean(centred * centred, axis=-1, keepdims=True) + norm_eps)
    return centred * inv_std, inv_std


def stats_back(grad_norm, normed, inv_std):
    return inv_std * (
        grad_norm
        - jnp.mean(grad_norm, axis=-1, keepdims=True)
        - normed * jnp.mean(grad_norm * normed, axis=-1, keepdims=True)
    )


def mm(left, right):
    return jnp.dot(left, right, preferred_element_type=f32)


def mm_nt(left, right):
    return lax.dot_general(left, right, nt, preferred_element_type=f32)


def put(dests, start, value):
    base, width = 0, value.shape[1]
    for ref in dests:
        size = ref.shape[1]
        lo, hi = max(start, base), min(start + width, base + size)
        if lo < hi:
            ref[:, lo - base : hi - base] = value[:, lo - start : hi - start].astype(ref.dtype)
        base += size


def take(pad, off, sources, start, width):
    base = 0
    for ref in sources:
        size = ref.shape[1]
        lo, hi = max(start, base), min(start + width, base + size)
        if lo < hi:
            pad[:, off + lo - start : off + hi - start] = ref[:, lo - base : hi - base]
        base += size


def head(h):
    return slice(h * HEAD_DIM, (h + 1) * HEAD_DIM)


def gelu_parts(u):
    c = math.sqrt(2.0 / math.pi)
    square = u * u
    return jnp.tanh(c * u * (1.0 + 0.044715 * square)), square, c


def qkv_kernel(win, nx, me_ref, x_ref, mod_ref, w_refs, h_ref, q_ref, kv_ref, buf, sems):
    pieces = Pieces(w_refs, me_ref, win, buf, sems, nx)
    normed, _ = stats(x_ref[...].astype(f32))
    hidden = (normed * (1.0 + mod_ref[1:2, :]) + mod_ref[0:1, :]).astype(bf16)
    h_ref[...] = hidden
    for x in range(nx):
        pieces.wait(x)
        block = mm(hidden, buf[x])[:, win.off : win.off + win.n]
        put([q_ref, kv_ref], x * win.n, block)


def stage_heads(dest, row, source, start):
    rows = source.shape[0]
    for h in range(HEADS):
        dest[h, row : row + rows, :HEAD_DIM] = source[
            :, start + h * HEAD_DIM : start + (h + 1) * HEAD_DIM
        ]


def spatial_kernel(pieces, *refs):
    q_ref = refs[0]
    kv_refs = refs[1 : 1 + pieces]
    o_ref, lse_ref, q_t, v_t, k_heads, o_t = refs[1 + pieces :]
    rows = q_ref.shape[0]
    q_t[...] = q_ref[...].astype(f32).T
    for i, kv in enumerate(kv_refs):
        v_t[:, i * rows : (i + 1) * rows] = kv[:, D:].astype(f32).T
        stage_heads(k_heads, i * rows, kv, 0)

    def one_head(h, carry):
        span = pl.ds(pl.multiple_of(h * HEAD_DIM, 8), HEAD_DIM)
        scores = mm(k_heads[h, :, :HEAD_DIM], q_t[span, :].astype(bf16)) * log2_scale
        top = jnp.max(scores, axis=0, keepdims=True)
        weights = jnp.exp2(scores - top)
        total = jnp.sum(weights, axis=0, keepdims=True)
        o_t[span, :] = mm(v_t[span, :].astype(bf16), weights.astype(bf16)) / total
        lse_ref[pl.ds(h, 1), :] = top + jnp.log2(total)
        return carry

    lax.fori_loop(0, HEADS, one_head, 0)
    o_ref[...] = o_t[...].T.astype(bf16)


def text_probs(text_ref, q_t, h, length):
    scores = mm(text_ref[:, head(h)], q_t[head(h), :].astype(bf16)) * score_scale
    slot = lax.broadcasted_iota(jnp.int32, scores.shape, 0)
    scores = jnp.where(slot < length, scores, masked_score)
    weights = jnp.exp(scores - jnp.max(scores, axis=0, keepdims=True))
    return weights / jnp.sum(weights, axis=0, keepdims=True)


def text_kernel(
    outer, w_out, w_cq, w_cout, nx, me_ref, x_ref, o_ref, mod_ref, w_refs, text_ref, length_ref,
    a1_ref, x1_ref, hc_ref, qc_ref, oc_ref, x2_ref, h3_ref,
    buf, sems, acc, q_t, v_t,
):
    pieces = Pieces(w_refs, me_ref, outer, buf, sems, nx)

    def product(left, win, dest, wait=False):
        for x in range(nx):
            if wait:
                pieces.wait(x)
            block = mm(left, buf[x, :, win.start : win.stop])[:, win.off : win.off + win.n]
            put([dest], x * win.n, block)

    product(o_ref[...], w_out, a1_ref, wait=True)
    after_a = x_ref[...].astype(f32) + mod_ref[2:3, :] * a1_ref[...]
    x1_ref[...] = after_a
    hidden = stats(after_a)[0].astype(bf16)
    hc_ref[...] = hidden
    product(hidden, w_cq, qc_ref)
    q_t[...] = qc_ref[...].astype(f32).T
    v_t[...] = text_ref[:, D:].astype(f32).T
    length = length_ref[0]
    for h in range(HEADS):
        probs = text_probs(text_ref, q_t, h, length).astype(bf16)
        acc[head(h), :] = mm(v_t[head(h), :].astype(bf16), probs)
    oc_ref[...] = acc[...].T.astype(bf16)
    product(oc_ref[...], w_cout, x2_ref)
    after_b = x1_ref[...] + x2_ref[...]
    x2_ref[...] = after_b
    h3_ref[...] = (
        stats(after_b)[0] * (1.0 + mod_ref[4:5, :]) + mod_ref[3:4, :]
    ).astype(bf16)


def ff_kernel(
    win, nx, ny, me_ref, h_ref, x2_ref, mod_ref, up_refs, down_ref,
    u_ref, g_ref, m_ref, x3_ref, h4_ref, up_buf, down_buf, up_sems, down_sems,
):
    ups = Pieces(up_refs, me_ref, win, up_buf, up_sems, nx)
    width = down_buf.shape[2]
    downs = down_blocks(up_refs, down_ref, me_ref, down_buf, down_sems, nx)
    hidden = h_ref[...]
    for x in range(nx):
        ups.wait(x)
        u = mm(hidden, up_buf[x])[:, win.off : win.off + win.n]
        put([u_ref], x * win.n, u)
        put([g_ref], x * win.n, 0.5 * u * (1.0 + gelu_parts(u)[0]))
    total = jnp.zeros(m_ref.shape, f32)
    for i in range(ny):
        downs.wait(i)
        total = total + mm_nt(g_ref[:, i * width : (i + 1) * width], down_buf[i])
    m_ref[...] = total
    after_c = x2_ref[...] + mod_ref[5:6, :] * total
    x3_ref[...] = after_c
    h4_ref[...] = (
        stats(after_c)[0] * (1.0 + mod_ref[7:8, :]) + mod_ref[6:7, :]
    ).astype(bf16)


def temporal_kernel(
    win, w_out, nx, frames, h_ref, da_ref, w_ref, row_clip, frame_clip,
    grad_ref, at_ref, dh_ref, buf, sems, pad, q_s, k_s, v_s, do_s, o_s, dq_s, dk_s, dv_s, qkv_s,
):
    pieces = Blocks(w_ref, buf, sems)
    o_ref, dqkv_ref = grad_ref.at[:, :D], grad_ref.at[:, D:]
    rows = h_ref.shape[0]
    spots = rows // frames
    hidden = h_ref[...]
    out_cols = slice(w_out.start, w_out.stop)
    pad[...] = jnp.zeros(pad.shape, bf16)
    total = jnp.zeros(h_ref.shape, f32)
    for x in range(nx):
        pieces.wait(x)
        block = mm(hidden, buf[x, :, win.start : win.stop])[:, win.off : win.off + win.n]
        put([qkv_s], x * win.n, block)
        take(pad, w_out.off, [da_ref], x * w_out.n, w_out.n)
        total = total + mm_nt(pad[:, : w_out.width], buf[x, :, out_cols])
    do_s[...] = total.astype(bf16).astype(f32)
    q_s[...] = qkv_s[:, :D].astype(f32)
    k_s[...] = qkv_s[:, D : 2 * D].astype(f32)
    v_s[...] = qkv_s[:, 2 * D :].astype(f32)
    dk_s[...] = jnp.zeros(dk_s.shape, f32)
    dv_s[...] = jnp.zeros(dv_s.shape, f32)

    def one_hot(size, feature, slot):
        first = lax.broadcasted_iota(jnp.int32, size, slot) * HEAD_DIM
        place = lax.broadcasted_iota(jnp.int32, size, feature)
        return jnp.where((place >= first) & (place < first + HEAD_DIM), 1.0, 0.0).astype(bf16)

    gather = one_hot((D, 128), 0, 1)
    spread = one_hot((128, D), 1, 0)

    def per_head(values):
        high = values.astype(bf16)
        low = (values - high.astype(f32)).astype(bf16)
        return mm(high, gather) + mm(low, gather)

    def every_frame(values):
        return jnp.broadcast_to(values[None], (frames, spots, D)).reshape(rows, D)

    def over_frames(values):
        return jnp.sum(values.reshape(frames, spots, values.shape[-1]), axis=0)

    def one_frame(f, carry):
        span = pl.ds(pl.multiple_of(f * spots, 8), spots)
        queries = every_frame(q_s[span, :])
        grads = every_frame(do_s[span, :])
        scores = per_head(queries * k_s[...]) * score_scale
        scores = jnp.where(row_clip[...] == frame_clip[f], scores, masked_score)
        scores = scores.reshape(frames, spots, 128)
        weights = jnp.exp(scores - jnp.max(scores, axis=0, keepdims=True))
        probs = weights / jnp.sum(weights, axis=0, keepdims=True)
        grad_probs = per_head(grads * v_s[...]).reshape(frames, spots, 128)
        inner = jnp.sum(probs * grad_probs, axis=0, keepdims=True)
        grad_scores = (probs * (grad_probs - inner)).reshape(rows, 128).astype(bf16)
        probs_wide = mm(probs.reshape(rows, 128).astype(bf16), spread)
        grads_wide = mm(grad_scores, spread)
        o_s[span, :] = over_frames(probs_wide * v_s[...])
        dq_s[span, :] = over_frames(grads_wide * k_s[...]) * score_scale
        dk_s[...] += grads_wide * queries
        dv_s[...] += probs_wide * grads
        return carry

    lax.fori_loop(0, frames, one_frame, 0)
    o_ref[...] = o_s[...].astype(bf16)
    for x in range(nx):
        block = mm(o_ref[...], buf[x, :, out_cols])[:, w_out.off : w_out.off + w_out.n]
        put([at_ref], x * w_out.n, block)
    dqkv_ref[:, :D] = dq_s[...].astype(bf16)
    dqkv_ref[:, D : 2 * D] = (dk_s[...] * score_scale).astype(bf16)
    dqkv_ref[:, 2 * D :] = dv_s[...].astype(bf16)
    pad[...] = jnp.zeros(pad.shape, bf16)
    total = jnp.zeros(dh_ref.shape, f32)
    for x in range(nx):
        take(pad, win.off, [dqkv_ref], x * win.n, win.n)
        total = total + mm_nt(pad[:, : win.width], buf[x, :, win.start : win.stop])
    dh_ref[...] = total.astype(bf16)


def mixed_kernel(at_ref, x3_ref, g_ref, mod_ref, keep_ref, y_ref, gate_ref):
    branch = at_ref[...].astype(f32)
    keep = keep_ref[0]
    y_ref[...] = (x3_ref[...] + keep * mod_ref[8:9, :] * branch).astype(bf16)
    gate_ref[...] = jnp.sum(keep * g_ref[...].astype(f32) * branch, axis=0, keepdims=True)


def column_sum(values):
    return jnp.sum(values, axis=0, keepdims=True)


def ff_back_kernel(
    win, nx, ny, me_ref, g_ref, dh4_ref, x3_ref, x2_ref, u_ref, m_ref, mod_ref, up_refs, down_ref,
    grad_ref, dx2_ref, sum_ref, up_buf, down_buf, up_sems, down_sems, pad,
):
    ff = u_ref.shape[1]
    du_s, dm_ref = grad_ref.at[:, :ff], grad_ref.at[:, ff:]
    width = down_buf.shape[2]
    downs = down_blocks(up_refs, down_ref, me_ref, down_buf, down_sems, nx)
    ups = Pieces(up_refs, me_ref, win, up_buf, up_sems, nx)
    dh4 = dh4_ref[...].astype(f32)
    normed, inv_std = stats(x3_ref[...])
    dx3 = g_ref[...].astype(f32) + stats_back(dh4 * (1.0 + mod_ref[7:8, :]), normed, inv_std)
    sum_ref[0:1, :] = column_sum(dh4)
    sum_ref[1:2, :] = column_sum(dh4 * normed)
    sum_ref[2:3, :] = column_sum(dx3 * m_ref[...])
    dm = (mod_ref[5:6, :] * dx3).astype(bf16)
    dm_ref[...] = dm
    for i in range(ny):
        downs.wait(i)
        grad = mm(dm, down_buf[i])
        u = u_ref[:, i * width : (i + 1) * width]
        tanh, square, c = gelu_parts(u)
        slope = 0.5 * (1.0 + tanh) + 0.5 * u * (1.0 - tanh * tanh) * (
            c * (1.0 + 3.0 * 0.044715 * square)
        )
        du_s[:, i * width : (i + 1) * width] = (grad * slope).astype(bf16)
    pad[...] = jnp.zeros(pad.shape, bf16)
    total = jnp.zeros(dx2_ref.shape, f32)
    for x in range(nx):
        ups.wait(x)
        take(pad, win.off, [du_s], x * win.n, win.n)
        total = total + mm_nt(pad[...], up_buf[x])
    normed, inv_std = stats(x2_ref[...])
    sum_ref[3:4, :] = column_sum(total)
    sum_ref[4:5, :] = column_sum(total * normed)
    sum_ref[5:8, :] = jnp.zeros((3, D), f32)
    dx2_ref[...] = dx3 + stats_back(total * (1.0 + mod_ref[4:5, :]), normed, inv_std)


def text_back_kernel(
    outer, w_out, w_cq, w_cout, nx, me_ref, dx2_ref, x1_ref, a1_ref, mod_ref, w_refs, qc_ref, text_ref,
    length_ref, grad_ref, dx1_ref, do1_ref, dtext_ref, gate_ref,
    buf, sems, pad, acc, q_t, do_t, k_t, do_s, dtext_s,
):
    dac_ref, dqc_ref, da1_ref = [grad_ref.at[:, i * D : (i + 1) * D] for i in range(3)]
    pieces = Pieces(w_refs, me_ref, outer, buf, sems, nx)

    def product(source, win, wait=False):
        pad[...] = jnp.zeros(pad.shape, bf16)
        total = jnp.zeros(dx2_ref.shape, f32)
        for x in range(nx):
            if wait:
                pieces.wait(x)
            take(pad, win.off, [source], x * win.n, win.n)
            total = total + mm_nt(pad[:, : win.width], buf[x, :, win.start : win.stop])
        return total

    dx2 = dx2_ref[...]
    dac_ref[...] = dx2.astype(bf16)
    grad_o = product(dac_ref, w_cout, wait=True).astype(bf16)
    do_s[...] = grad_o
    do_t[...] = grad_o.astype(f32).T
    q_t[...] = qc_ref[...].astype(f32).T
    k_t[...] = text_ref[:, :D].astype(f32).T
    length = length_ref[0]
    for h in range(HEADS):
        probs = text_probs(text_ref, q_t, h, length)
        values = text_ref[:, D + h * HEAD_DIM : D + (h + 1) * HEAD_DIM]
        grad_probs = mm(values, do_t[head(h), :].astype(bf16))
        inner = jnp.sum(probs * grad_probs, axis=0, keepdims=True)
        grad_scores = (probs * (grad_probs - inner)).astype(bf16)
        dtext_s[:, head(h)] = mm(grad_scores, qc_ref[:, head(h)]) * score_scale
        dtext_s[:, D + h * HEAD_DIM : D + (h + 1) * HEAD_DIM] = mm(
            probs.astype(bf16), do_s[:, head(h)]
        )
        acc[head(h), :] = mm(k_t[head(h), :].astype(bf16), grad_scores) * score_scale
    width = dtext_ref.shape[2]
    for x in range(nx):
        dtext_ref[x] = dtext_s[:, x * width : (x + 1) * width].astype(bf16)
    dqc_ref[...] = acc[...].T.astype(bf16)
    normed, inv_std = stats(x1_ref[...])
    dx1 = dx2 + stats_back(product(dqc_ref, w_cq), normed, inv_std)
    dx1_ref[...] = dx1
    gate_ref[...] = column_sum(dx1 * a1_ref[...])
    da1_ref[...] = (mod_ref[2:3, :] * dx1).astype(bf16)
    do1_ref[...] = product(da1_ref, w_out).astype(bf16)


def spatial_back_kernel(pieces, *refs):
    q_ref, do_ref, o_ref, lse_ref = refs[:4]
    kv_refs = refs[4 : 4 + pieces]
    (
        dq_ref, dkv_ref,
        q_t, do_t, o_t, k_t, dq_t, q_heads, do_heads, k_heads, v_heads, dk_heads, dv_heads,
    ) = refs[4 + pieces :]
    rows = q_ref.shape[0]
    q_t[...] = q_ref[...].astype(f32).T
    do_t[...] = do_ref[...].astype(f32).T
    o_t[...] = o_ref[...].astype(f32).T
    stage_heads(q_heads, 0, q_ref, 0)
    stage_heads(do_heads, 0, do_ref, 0)
    for i, kv in enumerate(kv_refs):
        k_t[:, i * rows : (i + 1) * rows] = kv[:, :D].astype(f32).T
        stage_heads(k_heads, i * rows, kv, 0)
        stage_heads(v_heads, i * rows, kv, D)

    def one_head(h, carry):
        span = pl.ds(pl.multiple_of(h * HEAD_DIM, 8), HEAD_DIM)
        grad_o = do_t[span, :]
        inner = jnp.sum(grad_o * o_t[span, :], axis=0, keepdims=True)
        scores = mm(k_heads[h, :, :HEAD_DIM], q_t[span, :].astype(bf16)) * log2_scale
        probs = jnp.exp2(scores - lse_ref[pl.ds(h, 1), :])
        grad_probs = mm(v_heads[h, :, :HEAD_DIM], grad_o.astype(bf16))
        grad_scores = (probs * (grad_probs - inner)).astype(bf16)
        dv_heads[h, :, :HEAD_DIM] = mm(probs.astype(bf16), do_heads[h, :, :HEAD_DIM]).astype(bf16)
        dk_heads[h, :, :HEAD_DIM] = (
            mm(grad_scores, q_heads[h, :, :HEAD_DIM]) * score_scale
        ).astype(bf16)
        dq_t[span, :] = mm(k_t[span, :].astype(bf16), grad_scores) * score_scale
        return carry

    lax.fori_loop(0, HEADS, one_head, 0)
    dq_ref[...] = dq_t[...].T.astype(bf16)
    for i in range(pieces):
        span = slice(i * rows, (i + 1) * rows)
        for h in range(HEADS):
            dkv_ref[i, :, head(h)] = dk_heads[h, span, :HEAD_DIM]
            dkv_ref[i, :, D + h * HEAD_DIM : D + (h + 1) * HEAD_DIM] = dv_heads[
                h, span, :HEAD_DIM
            ]


def qkv_back_kernel(
    win, nx, me_ref, dq_ref, own_ref, come_ref, x_ref, mod_ref, dx1_ref, w_refs,
    grad_ref, gx_ref, sum_ref, buf, sems, pad,
):
    dkv_ref = grad_ref.at[:, D:]
    grad_ref[:, :D] = dq_ref[...]
    pieces = Pieces(w_refs, me_ref, win, buf, sems, nx)
    dkv_ref[...] = (own_ref[...].astype(f32) + come_ref[...].astype(f32)).astype(bf16)
    pad[...] = jnp.zeros(pad.shape, bf16)
    total = jnp.zeros(dx1_ref.shape, f32)
    for x in range(nx):
        pieces.wait(x)
        take(pad, win.off, [grad_ref], x * win.n, win.n)
        total = total + mm_nt(pad[...], buf[x])
    normed, inv_std = stats(x_ref[...].astype(f32))
    sum_ref[0:1, :] = column_sum(total)
    sum_ref[1:2, :] = column_sum(total * normed)
    gx_ref[...] = (
        dx1_ref[...] + stats_back(total * (1.0 + mod_ref[1:2, :]), normed, inv_std)
    ).astype(bf16)


def turn_rows(turn, at, value, me_y, ny):
    rows = turn.shape[0] // ny
    flipped = value.astype(f32).T.astype(bf16)
    for y in range(ny):
        place = pl.ds(pl.multiple_of((y ^ me_y) * rows, 16), rows)
        turn[place, at : at + value.shape[0]] = flipped[y * rows : (y + 1) * rows]


def write_blocks(outs, half, columns, block, first=0):
    some_send, rest_send, some_keep, rest_keep = outs
    rows, each = block.shape[0] // 4, some_keep.shape[1] // 2
    step = pl.program_id(0)

    def write(ref, at, y):
        start = at * each + first
        ref[0, start : start + rows, columns] = block[y * rows : (y + 1) * rows]

    @pl.when(step < half)
    def _():
        for at in range(2):
            write(some_keep, at, at)
            write(some_send, at, 2 + at)

    @pl.when(step >= half)
    def _():
        for at in range(2):
            write(rest_keep, at, 2 * at)
            write(rest_send, at, 2 * at + 1)


def block_outs(nx, depth, lanes):
    half = nx // 4
    size = (1, depth // 2, lanes)
    some = pl.BlockSpec(size, lambda t, me: (jnp.minimum(t, half - 1), 0, 0))
    rest = pl.BlockSpec(size, lambda t, me: (jnp.maximum(t - half, 0), 0, 0))
    return [shape(half, depth // 2, lanes, dtype=bf16)] * 4, [some, rest, some, rest]


def view(refs, place):
    k, first, last = place
    return refs[k].at[:, first:last]


def weight_kernel(nx, ny, lanes, count, pairs, me_ref, *refs):
    sides, outs = (refs[:count], refs[count : 2 * count]), refs[2 * count : 2 * count + 4]
    pads, turned = refs[2 * count + 4 :: 2], refs[2 * count + 5 :: 2]
    step = pl.program_id(0)
    x = me_ref[0] ^ (2 * step)
    rows = refs[0].shape[0]

    @pl.when(step == 0)
    def _():
        for (left, _), turn in zip(pairs, turned):
            for i, side in enumerate(sides):
                turn_rows(turn, i * rows, view(side, left)[...], me_ref[1], ny)

    at = 0
    for (_, right), pad, turn in zip(pairs, pads, turned):
        n = pad.shape[1]
        for i in range(nx):

            @pl.when(x == i)
            def _():
                for k, side in enumerate(sides):
                    take(pad.at[k * rows : (k + 1) * rows], 0, [view(side, right)], i * n, n)

        block = mm(turn[...], pad[...]).astype(bf16)
        write_blocks(outs, nx // 4, slice(at, at + n), block)
        at += n
    if at < lanes:
        write_blocks(outs, nx // 4, slice(at, lanes), jnp.zeros((D, lanes - at), bf16))


def weight_grads(nx, me, own, other, pairs):
    widths = [(last - first) // nx for _, (_, first, last) in pairs]
    lanes = padded(sum(widths))
    rows = own[0].shape[0]
    scratch = []
    for width in widths:
        scratch += [pltpu.VMEM((2 * rows, width), bf16), pltpu.VMEM((D, 2 * rows), bf16)]
    outs, out_specs = block_outs(nx, D, lanes)
    return pl.pallas_call(
        functools.partial(weight_kernel, nx, lax.axis_size("gy"), lanes, len(own), pairs),
        out_shape=outs,
        grid_spec=pltpu.PrefetchScalarGridSpec(
            num_scalar_prefetch=1,
            grid=(nx // 2,),
            in_specs=[vmem() for _ in range(2 * len(own))],
            out_specs=out_specs,
            scratch_shapes=scratch,
        ),
        compiler_params=pltpu.CompilerParams(vmem_limit_bytes=56 << 20),
        cost_estimate=cost(9),
    )(me, *own, *other)


def whole_kernel(nx, lanes, pairs, *refs):
    count = 1 + max(k for pair in pairs for k, _, _ in pair)
    ins, out_ref = refs[:count], refs[count]
    pads, turned = refs[count + 1 :: 2], refs[count + 2 :: 2]
    x = pl.program_id(0)

    @pl.when(x == 0)
    def _():
        for (left, _), turn in zip(pairs, turned):
            turn[...] = view(ins, left)[...].astype(f32).T.astype(bf16)

    at = 0
    for (_, right), pad, turn in zip(pairs, pads, turned):
        n = pad.shape[1]
        for i in range(nx):

            @pl.when(x == i)
            def _():
                take(pad, 0, [view(ins, right)], i * n, n)

        out_ref[0, :, at : at + n] = mm(turn[...], pad[...]).astype(bf16)
        at += n
    if at < lanes:
        out_ref[0, :, at:] = jnp.zeros((D, lanes - at), bf16)


def whole_grads(nx, arrays, pairs):
    widths = [(last - first) // nx for _, (_, first, last) in pairs]
    lanes = padded(sum(widths))
    rows = arrays[0].shape[0]
    scratch = []
    for width in widths:
        scratch += [pltpu.VMEM((rows, width), bf16), pltpu.VMEM((D, rows), bf16)]
    return pl.pallas_call(
        functools.partial(whole_kernel, nx, lanes, pairs),
        out_shape=shape(nx, D, lanes, dtype=bf16),
        grid=(nx,),
        in_specs=[vmem() for _ in arrays],
        out_specs=pl.BlockSpec((1, D, lanes), lambda x: (x, 0, 0)),
        scratch_shapes=scratch,
        compiler_params=pltpu.CompilerParams(vmem_limit_bytes=56 << 20),
        cost_estimate=cost(13),
    )(*arrays)


def up_grads(nx, me, own, other, folding):
    rows, ff = own[2].shape
    n = ff // nx
    ny = lax.axis_size("gy")
    start = padded(n)
    width = ff // ny
    fold = fold_width(width)
    each = D // nx

    def kernel(me_ref, *refs):
        sides, outs = (refs[:3], refs[3:6]), refs[6:10]
        turn, pad, down_turn, down_pad = refs[-4:]
        step = pl.program_id(0)
        x = me_ref[0] ^ (2 * step)

        @pl.when(step == 0)
        def _():
            for k, (h_ref, grad_ref, _) in enumerate(sides):
                turn_rows(turn, k * rows, h_ref[...], me_ref[1], ny)
                if folding:
                    down_turn[:, k * rows : (k + 1) * rows] = (
                        grad_ref[:, ff:].astype(f32).T.astype(bf16)
                    )

        for i in range(nx):

            @pl.when(x == i)
            def _():
                for k, (_, grad_ref, _) in enumerate(sides):
                    pad[k * rows : (k + 1) * rows] = grad_ref[:, i * n : (i + 1) * n]

        write_blocks(outs, nx // 4, slice(0, n), mm(turn[...], pad[...]).astype(bf16))
        if n < start:
            write_blocks(outs, nx // 4, slice(n, start), jnp.zeros((D, start - n), bf16))
        if not folding:
            return
        left = down_turn[pl.ds(pl.multiple_of(x * each, 16), each), :]
        for y in range(ny):
            columns = slice(y * width, (y + 1) * width)
            block = mm(left[:, :rows], sides[0][2][:, columns])
            block = (block + mm(left[:, rows:], sides[1][2][:, columns])).astype(bf16)
            top = (y ^ me_ref[1]) * 2 * each
            down_pad[pl.ds(pl.multiple_of(top, 16), each), :] = block[:, :fold]
            low = pl.multiple_of(top + each, 16)
            down_pad[pl.ds(low, each), : width - fold] = block[:, fold:]
            down_pad[pl.ds(low, each), width - fold :] = jnp.zeros((each, 2 * fold - width), bf16)
        write_blocks(outs, nx // 4, slice(0, fold), down_pad[...], D // ny)

    outs, out_specs = block_outs(nx, 2 * D if folding else D, start)
    return pl.pallas_call(
        kernel,
        out_shape=outs,
        grid_spec=pltpu.PrefetchScalarGridSpec(
            num_scalar_prefetch=1,
            grid=(nx // 2,),
            in_specs=[vmem()] * 6,
            out_specs=out_specs,
            scratch_shapes=[
                pltpu.VMEM((D, 2 * rows), bf16),
                pltpu.VMEM((2 * rows, n), bf16),
                pltpu.VMEM((D, 2 * rows), bf16),
                pltpu.VMEM((D, fold), bf16),
            ],
        ),
        compiler_params=pltpu.CompilerParams(vmem_limit_bytes=56 << 20),
        cost_estimate=cost(16),
    )(me, *own, *other)


def down_grads(dm, g):
    rows = g.shape[0]
    ny = lax.axis_size("gy")
    width = g.shape[1] // ny

    def kernel(dm_ref, g_ref, out_ref, turn):
        @pl.when(pl.program_id(0) == 0)
        def _():
            turn[...] = dm_ref[...].astype(f32).T.astype(bf16)

        out_ref[0] = mm(turn[...], g_ref[...]).astype(bf16)

    return pl.pallas_call(
        kernel,
        out_shape=shape(ny, D, width, dtype=bf16),
        grid=(ny,),
        in_specs=[vmem(), pl.BlockSpec((rows, width), lambda i: (0, i))],
        out_specs=pl.BlockSpec((1, D, width), lambda i: (i, 0, 0)),
        scratch_shapes=[pltpu.VMEM((D, rows), bf16)],
        compiler_params=pltpu.CompilerParams(vmem_limit_bytes=56 << 20),
        cost_estimate=cost(12),
    )(dm, g)


def after(value, *others):
    return lax.optimization_barrier((value, others))[0]


class Gather:
    def __init__(self, shard):
        self.line = [shard]

    def along(self, fars, *others):
        shard = after(self.line[0], *others)
        new = [swap(shard, "gx", 2 * far) for far in fars]
        self.line = self.line + new
        return new

    def first(self, *others):
        line = after(self.line, *others)
        half = len(line) // 2
        some, rest = jnp.stack(line[:half]), jnp.stack(line[half:])
        self.near = (some, rest)
        self.far = [swap(some, "gy", 1), swap(rest, "gy", 2)]
        return self.far

    def second(self, *others):
        far = after(self.far, *others)
        self.own = [jnp.stack(pair) for pair in zip(self.near, far)]
        self.new = [swap(self.own[0], "gy", 2), swap(self.own[1], "gy", 1)]
        return self.new

    def own_core(self, *others):
        self.own_other = [swap(array, "gx", 1) for array in after(self.own, *others)]
        return self.own_other

    def new_core(self, *others):
        self.new_other = [swap(array, "gx", 1) for array in after(self.new, *others)]
        return self.new_other

    def arrays(self):
        pairs = ((self.own, self.new), (self.own_other, self.new_other))
        return tuple(side[i] for own, new in pairs for i in range(2) for side in (own, new))


def gather_rows(shard):
    ny = lax.axis_size("gy")
    whole = lax.all_gather(shard, row_axes, axis=0, tiled=True)
    return whole.reshape(ny, -1, shard.shape[1])


def total(*terms):
    return sum(term.astype(f32) for term in terms).astype(bf16)


class Scatter:
    def __init__(self, some_send, rest_send, some_keep, rest_keep):
        self.sent = [some_send, rest_send]
        self.kept = [some_keep, rest_keep]
        half, depth, lanes = some_keep.shape
        self.half, self.size = half, (half, 2, depth // 2, lanes)

    def first(self, *others):
        some, rest = after(self.sent, *others)
        self.come = [swap(some, "gy", 2), swap(rest, "gy", 1)]
        return self.come

    def second(self, *others):
        kept = [array.reshape(self.size) for array in self.kept]
        come = [array.reshape(self.size) for array in after(self.come, *others)]
        self.near = list(zip(kept, come))
        self.sent = [total(mine[:, 1], theirs[:, 1]) for mine, theirs in self.near]
        self.come = [swap(self.sent[0], "gy", 1), swap(self.sent[1], "gy", 2)]
        return self.come

    def line(self, *others):
        come = after(self.come, *others)
        some, rest = [
            total(mine[:, 0], theirs[:, 0], last)
            for (mine, theirs), last in zip(self.near, come)
        ]
        self.ends = [some[i] for i in range(self.half)] + [rest[i] for i in range(self.half)]
        self.got = []

    def along(self, fars, *others):
        new = [swap(after(self.ends[far], *others), "gx", 2 * far) for far in fars]
        self.got = self.got + new
        return new

    def result(self):
        return sum([term.astype(f32) for term in self.got], self.ends[0].astype(f32))


def scatter(blocks, axes):
    flat = blocks.reshape(-1, blocks.shape[-1])
    return lax.psum_scatter(flat, axes, scatter_dimension=0, tiled=True).astype(f32)


def swap(values, axis, mask):
    return lax.ppermute(values, axis, [(i, i ^ mask) for i in range(lax.axis_size(axis))])


def reorder(values):
    devices = lax.axis_size(row_axes)
    return lax.all_to_all(
        values.reshape(devices, values.shape[0] // devices, values.shape[1]),
        row_axes,
        split_axis=0,
        concat_axis=0,
        tiled=True,
    ).reshape(values.shape)


def pad_lanes(values):
    return jnp.pad(values, ((0, 0), (0, padded(values.shape[1]) - values.shape[1])))


def condition(timesteps, pooled_text):
    half_width = D // 2
    frequency = jnp.exp(
        -math.log(10000.0) * jnp.arange(half_width).astype(jnp.float32) / half_width
    )
    angles = timesteps.astype(jnp.float32)[:, None] * frequency[None, :]
    embedded = jnp.concatenate([jnp.cos(angles), jnp.sin(angles)], axis=1)
    return jax.nn.silu(embedded + pooled_text)


def local(
    tokens,
    text_states,
    pooled_text,
    timesteps,
    frame_counts,
    still_clips,
    text_lengths,
    w_ada,
    w_sqkv,
    w_sout,
    w_cq,
    w_ckv,
    w_cout,
    w_up,
    w_down,
    w_tqkv,
    w_tout,
    grad_out,
):
    nx, ny = lax.axis_size("gx"), lax.axis_size("gy")
    gx, gy = lax.axis_index("gx"), lax.axis_index("gy")
    devices = nx * ny
    me = jnp.stack([gx, gy]).astype(jnp.int32)
    device = gy * nx + gx
    rows = tokens.shape[0]
    frame_devs = FRAME // rows
    frames = rows * devices // FRAME
    k_rows = w_ada.shape[0]
    clip_ends = jnp.cumsum(frame_counts)
    clip_here = jnp.sum((clip_ends <= device // frame_devs).astype(jnp.int32))
    clip_mark = jnp.arange(CLIPS) == clip_here
    clip_pick = clip_mark.astype(f32)
    keep_here = (1.0 - jnp.sum(clip_pick * still_clips.astype(f32))).reshape(1)
    length_here = jnp.sum(jnp.where(clip_mark, text_lengths, 0)).reshape(1)
    frame_clip = jnp.sum(
        (clip_ends[None, :] <= jnp.arange(frames)[:, None]).astype(jnp.int32), axis=1
    ).astype(f32)
    row_clip = jnp.repeat(frame_clip, rows // frames)[:, None]

    n_sqkv, n_one, n_up = w_sqkv.shape[1], w_sout.shape[1], w_up.shape[1]
    shard_a = pad_lanes(jnp.concatenate([w_sqkv, w_sout, w_cq, w_cout], axis=1))
    shard_d = pad_lanes(jnp.concatenate([w_tqkv, w_tout], axis=1))
    shard_up = pad_lanes(w_up)
    each = w_down.shape[1]
    fold = fold_width(w_down.shape[0])
    trees = each % 16 == 0 and 2 * each == k_rows and fold == padded(n_up)
    if trees:
        turned = w_down.T
        rest = jnp.pad(turned[:, fold:], ((0, 0), (0, 2 * fold - turned.shape[1])))
        shard_up = jnp.concatenate([shard_up, turned[:, :fold], rest])
    fars = range(1, nx // 2)
    get_a, get_up = Gather(shard_a), Gather(shard_up)
    get_a.along(fars)
    cond_all = condition(timesteps, pooled_text)
    cond_rows = lax.dynamic_slice_in_dim(cond_all, gy * k_rows, k_rows, axis=1)
    mod_part = jnp.dot(cond_rows, w_ada.astype(f32), precision=highest)
    mod_part = mod_part + swap(mod_part, "gy", 1)
    mod_all = (mod_part + swap(mod_part, "gy", 2))[None]
    mod_first = mod_all
    own_text = text_states.shape[0]
    text_rows = text_states.reshape(own_text // CLIPS, CLIPS, -1).transpose(1, 0, 2)
    depth = w_ckv.shape[0]
    text_rows = after(text_rows.reshape(own_text, ny, depth).transpose(1, 0, 2), mod_first)
    text_rows = lax.all_to_all(text_rows, "gy", split_axis=0, concat_axis=0, tiled=True)
    text_rows = lax.all_gather(text_rows, "gx", axis=0)
    bit = 1
    while bit < nx:
        if 2 * bit == nx:
            mod_all = after(mod_all, text_rows, *get_a.line)
        come = swap(mod_all, "gx", bit)
        mod_all = jnp.where(
            gx & bit != 0,
            jnp.concatenate([come, mod_all]),
            jnp.concatenate([mod_all, come]),
        )
        bit *= 2
    mod = lax.dynamic_index_in_dim(mod_all, clip_here, axis=1, keepdims=False).reshape(9, D)
    done = [mod_all]
    held = done
    done = get_a.first(*held) + get_up.along(fars[:2], *held)
    text_block = (
        after(text_rows, *held)
        .reshape(nx, ny, CLIPS, own_text // CLIPS, depth)
        .transpose(2, 1, 0, 3, 4)
        .reshape(own_text * devices, depth)
    )
    text_part = jnp.dot(text_block, w_ckv, preferred_element_type=f32)
    done += [text_part]
    grad_branch_d = (keep_here[0] * mod[8] * grad_out.astype(f32)).astype(bf16)
    held = done
    done = get_a.second(*held) + get_a.own_core()
    done += get_up.along(fars[2:], *held, *get_a.own_other)
    text_sum = lax.psum_scatter(
        after(text_part, *held), "gy", scatter_dimension=0, tiled=True
    )
    done += [text_sum]
    held = done
    up_far = get_up.first(*held)
    done = get_a.new_core(*held, *get_up.near)
    full_a = get_a.arrays()
    ff_width = w_down.shape[0]
    ff = ff_width * ny
    win_sqkv = Window(0, n_sqkv)
    at = n_sqkv
    win_rest = Window(at, at + 3 * n_one)
    win_sout, win_cq, win_cout = [
        Window(at + i * n_one, at + (i + 1) * n_one).inside(win_rest) for i in range(3)
    ]
    win_up = Window(0, n_up)
    win_d = Window(0, n_sqkv + n_one)
    win_tqkv = Window(0, n_sqkv)
    win_tout = Window(n_sqkv, n_sqkv + n_one)


    win = win_sqkv
    hidden_a, query_a, pair_a = run(
        functools.partial(qkv_kernel, win, nx),
        [
            shape(rows, D, dtype=bf16),
            shape(rows, D, dtype=bf16),
            shape(rows, 2 * D, dtype=bf16),
        ],
        [smem()] + [vmem(), vmem(), hbm()],
        [pltpu.VMEM((nx, D, win.width), bf16), pltpu.SemaphoreType.DMA((nx,))],
        (me, tokens, after(mod, *done), full_a),
        9,
    )
    up_near = get_up.second(*up_far, pair_a)
    up_own = get_up.own_core()
    pairs = [after(pair_a, *up_far)]
    bit = frame_devs // 2
    while bit:
        pairs = pairs + [swap(p, "gx", bit) for p in pairs]
        bit //= 2
    text_all = lax.all_gather(after(text_sum, *held).astype(bf16), row_axes, axis=0)
    full_d = lax.all_gather(after(shard_d, text_all), ("gx", "gy"), axis=0, tiled=True)
    full_d = full_d.reshape(nx, D, -1)
    slots = own_text * devices // CLIPS
    text_all = text_all.reshape(ny, nx, -1, w_ckv.shape[1]).transpose(0, 2, 1, 3)
    text_all = text_all.reshape(CLIPS, slots, 2 * D)
    text_pairs = lax.dynamic_index_in_dim(text_all, clip_here, axis=0, keepdims=False)
    done = [*pairs, *up_own]
    query_a = after(query_a, *done)
    grad_branch_moved = reorder(after(grad_branch_d, *done))
    count = len(pairs)
    keys = count * rows
    out_a, lse_a = run(
        functools.partial(spatial_kernel, count),
        [shape(rows, D, dtype=bf16), shape(HEADS, rows)],
        [vmem() for _ in range(1 + count)],
        [
            pltpu.VMEM((D, rows), f32),
            pltpu.VMEM((D, keys), f32),
            pltpu.VMEM((HEADS, keys, 128), bf16),
            pltpu.VMEM((D, rows), f32),
        ],
        (query_a, *pairs),
        18,
    )

    done = [out_a, text_pairs]
    out_a = after(out_a, *done)
    branch_a, after_a, hidden_b, query_b, out_b, after_b, hidden_c = run(
        functools.partial(text_kernel, win_rest, win_sout, win_cq, win_cout, nx),
        [
            shape(rows, D),
            shape(rows, D),
            shape(rows, D, dtype=bf16),
            shape(rows, D, dtype=bf16),
            shape(rows, D, dtype=bf16),
            shape(rows, D),
            shape(rows, D, dtype=bf16),
        ],
        [smem()] + [vmem(), vmem(), vmem(), hbm(), vmem(), smem()],
        [
            pltpu.VMEM((nx, D, win_rest.width), bf16),
            pltpu.SemaphoreType.DMA((nx,)),
            pltpu.VMEM((D, rows), f32),
            pltpu.VMEM((D, rows), f32),
            pltpu.VMEM((D, slots), f32),
        ],
        (me, tokens, out_a, mod, full_a, text_pairs, length_here),
        18,
    )

    done = [hidden_c, *up_near]
    done = get_up.new_core(*done)
    full_up = get_up.arrays()
    full_down = None if trees else gather_rows(after(w_down.T, *up_near))
    hidden_c = after(hidden_c, *done)
    pre_act, activated, branch_c, after_c, hidden_d = run(
        functools.partial(ff_kernel, win_up, nx, ny),
        [
            shape(rows, ff),
            shape(rows, ff, dtype=bf16),
            shape(rows, D),
            shape(rows, D),
            shape(rows, D, dtype=bf16),
        ],
        [smem()] + [vmem(), vmem(), vmem(), hbm(), hbm()],
        [
            pltpu.VMEM((nx, D, win_up.width), bf16),
            pltpu.VMEM((ny, D, ff_width), bf16),
            pltpu.SemaphoreType.DMA((nx,)),
            pltpu.SemaphoreType.DMA((ny,)),
        ],
        (me, hidden_c, after_b, mod, full_up, full_down),
        20,
    )

    rows_own = [hidden_a, out_a, hidden_b, out_b, hidden_c]
    rows_other = swap(after(jnp.stack(rows_own), hidden_d), "gx", 1)
    g_other = swap(after(activated, hidden_d), "gx", 1)
    moved_d = reorder(hidden_d)
    moved_d = after(moved_d, rows_other, g_other, grad_branch_moved)
    pad_width = max(win_tqkv.width, win_tout.width)
    grads_d, branch_moved, grad_hidden_moved = run(
        functools.partial(temporal_kernel, win_tqkv, win_tout, nx, frames),
        [
            shape(rows, 4 * D, dtype=bf16),
            shape(rows, D, dtype=bf16),
            shape(rows, D, dtype=bf16),
        ],
        [vmem(), vmem(), hbm(), vmem(), smem()],
        [
            pltpu.VMEM((nx, D, win_d.width), bf16),
            pltpu.SemaphoreType.DMA((nx,)),
            pltpu.VMEM((rows, pad_width), bf16),
        ]
        + [pltpu.VMEM((rows, D), f32)] * 8
        + [pltpu.VMEM((rows, 3 * D), bf16)],
        (moved_d, grad_branch_moved, full_d, row_clip, frame_clip),
        25,
    )
    grad_hidden_d = reorder(grad_hidden_moved)
    late = whole_grads(
        nx, [moved_d, grad_branch_moved, grads_d], [((0, 0, D), (2, D, 4 * D)), ((2, 0, D), (1, 0, D))]
    )
    late = scatter(after(late, grad_hidden_d), ("gx", "gy"))
    d_tqkv, d_tout = late[:, :n_sqkv], late[:, n_sqkv : n_sqkv + n_one]

    grads_c, grad_b, sums_c = run(
        functools.partial(ff_back_kernel, win_up, nx, ny),
        [
            shape(rows, ff + D, dtype=bf16),
            shape(rows, D),
            shape(8, D),
        ],
        [smem()] + [vmem()] * 7 + [hbm(), hbm()],
        [
            pltpu.VMEM((nx, D, win_up.width), bf16),
            pltpu.VMEM((ny, D, ff_width), bf16),
            pltpu.SemaphoreType.DMA((nx,)),
            pltpu.SemaphoreType.DMA((ny,)),
            pltpu.VMEM((rows, win_up.width), bf16),
        ],
        (me, grad_out, grad_hidden_d, after_c, after_b, pre_act, branch_c, mod, full_up, full_down),
        22,
    )
    branch_d = reorder(after(branch_moved, grad_hidden_d))
    grads_c = after(grads_c, branch_d)
    grads_other = swap(grads_c, "gx", 1)
    up_terms = up_grads(
        nx,
        me,
        [hidden_c, grads_c, activated],
        [rows_other[4], grads_other, g_other],
        trees,
    )
    if not trees:
        d_down = scatter(down_grads(grads_c[:, ff:], activated), row_axes).T
    up_sums = Scatter(*up_terms)
    up_first = up_sums.first()
    grad_b = after(grad_b, *up_terms)

    kv_width = w_ckv.shape[1]
    grads_b, grad_a, grad_out_a, text_terms, d_gate1 = run(
        functools.partial(text_back_kernel, win_rest, win_sout, win_cq, win_cout, nx),
        [
            shape(rows, 3 * D, dtype=bf16),
            shape(rows, D),
            shape(rows, D, dtype=bf16),
            shape(nx, slots, kv_width, dtype=bf16),
            shape(1, D),
        ],
        [smem()] + [vmem()] * 4 + [hbm(), vmem(), vmem(), smem()],
        [
            pltpu.VMEM((nx, D, win_rest.width), bf16),
            pltpu.SemaphoreType.DMA((nx,)),
            pltpu.VMEM((rows, max(w.width for w in (win_sout, win_cq, win_cout))), bf16),
            pltpu.VMEM((D, rows), f32),
            pltpu.VMEM((D, rows), f32),
            pltpu.VMEM((D, rows), f32),
            pltpu.VMEM((D, slots), f32),
            pltpu.VMEM((rows, D), bf16),
            pltpu.VMEM((slots, 2 * D), f32),
        ],
        (me, grad_b, after_a, branch_a, mod, full_a, query_b, text_pairs, length_here),
        20,
    )
    text_terms = jnp.where(clip_mark[None, :, None, None], text_terms[:, None], 0)

    done = [grad_out_a]
    grads_b_other = swap(grads_b, "gx", 1)
    text_terms = lax.psum_scatter(
        after(text_terms, late).reshape(nx, -1, kv_width), "gx", scatter_dimension=0, tiled=True
    )
    grad_out_a = after(grad_out_a, *done)

    grad_query_a, grad_pairs = run(
        functools.partial(spatial_back_kernel, count),
        [shape(rows, D, dtype=bf16), shape(count, rows, 2 * D, dtype=bf16)],
        [vmem() for _ in range(4 + count)],
        [pltpu.VMEM((D, rows), f32)] * 3
        + [pltpu.VMEM((D, keys), f32), pltpu.VMEM((D, rows), f32)]
        + [pltpu.VMEM((HEADS, rows, 128), bf16)] * 2
        + [pltpu.VMEM((HEADS, keys, 128), bf16)] * 4,
        (query_a, grad_out_a, out_a, lse_a, *pairs),
        28,
    )
    done = [grad_pairs, grads_b_other]
    grad_pairs = after(grad_pairs, *done)
    up_second = up_sums.second(*done)
    done = up_sums.sent
    bit = 1
    while bit < frame_devs // 2:
        half = grad_pairs.shape[0] // 2
        come = swap(grad_pairs[half:], "gx", bit)
        grad_pairs = (grad_pairs[:half].astype(f32) + come.astype(f32)).astype(bf16)
        bit *= 2
    come = swap(grad_pairs[1], "gx", bit)
    mixed, d_gate3 = run(
        mixed_kernel,
        [shape(rows, D, dtype=bf16), shape(1, D)],
        [vmem(), vmem(), vmem(), vmem(), smem()],
        [],
        (branch_d, after_c, grad_out, mod, keep_here),
        3,
    )

    cross = Scatter(
        *weight_grads(
            nx,
            me,
            [hidden_b, out_b, after(grads_b, grad_pairs, *done)],
            [rows_other[2], rows_other[3], grads_b_other],
            [((0, 0, D), (2, D, 2 * D)), ((1, 0, D), (2, 0, D))],
        )
    )
    done = [come, *cross.sent, *up_second]
    cross_first = cross.first(*done)
    up_sums.line(*done)
    up_done = up_sums.along(fars[2:])
    grad_query_a = after(grad_query_a, *done, *up_sums.ends)
    win = win_sqkv
    grads_a, grad_tokens, sums_a = run(
        functools.partial(qkv_back_kernel, win, nx),
        [shape(rows, 3 * D, dtype=bf16), shape(rows, D, dtype=bf16), shape(2, D)],
        [smem()] + [vmem()] * 6 + [hbm()],
        [
            pltpu.VMEM((nx, D, win.width), bf16),
            pltpu.SemaphoreType.DMA((nx,)),
            pltpu.VMEM((rows, win.width), bf16),
        ],
        (me, grad_query_a, grad_pairs[0], come, tokens, mod, grad_a, full_a),
        11,
    )
    grads_a_other = swap(grads_a, "gx", 1)
    early = Scatter(
        *weight_grads(
            nx,
            me,
            [hidden_a, out_a, grads_a, grads_b],
            [rows_other[0], rows_other[1], grads_a_other, grads_b_other],
            [((0, 0, D), (2, 0, 3 * D)), ((1, 0, D), (3, 2 * D, 3 * D))],
        )
    )
    done = [*cross_first, *early.sent]
    cross_second = cross.second(*done)
    done = [*cross_second, *up_done]
    up_done = up_done + up_sums.along(fars[:2])
    early_first = early.first(*done)
    cross.line(*done)
    cross_done = cross.along(fars, *up_done)
    done = [*early_first, *up_done]
    early_second = early.second(*done)
    early.line(*early_second)
    early_done = early.along(fars)
    grad_mod = jnp.concatenate(
        [sums_a, d_gate1, sums_c[3:5], sums_c[2:3], sums_c[0:2], d_gate3]
    ).reshape(-1)
    grad_mod = after(lax.all_gather(grad_mod, row_axes, axis=0), *early.ends)
    width = w_ada.shape[1]
    grad_mod = lax.dynamic_slice_in_dim(grad_mod, gx * width, width, axis=1)
    device_clip = jnp.sum(
        (clip_ends[None, :] <= (jnp.arange(devices) // frame_devs)[:, None]).astype(jnp.int32),
        axis=1,
    )
    device_pick = (jnp.arange(CLIPS)[:, None] == device_clip[None, :]).astype(f32)
    grad_mod = jnp.dot(device_pick, grad_mod, precision=highest)
    d_ada = lax.dot_general(
        cond_rows, grad_mod, (((0,), (0,)), ((), ())), precision=highest
    )
    text_terms = after(text_terms[0], *early.ends).astype(f32)
    text_terms = text_terms + swap(text_terms.astype(bf16), "gy", 1).astype(f32)
    text_terms = text_terms + swap(text_terms.astype(bf16), "gy", 2).astype(f32)
    text_grad = text_terms.astype(bf16)
    d_ckv = jnp.einsum("rd,re->de", text_block, text_grad, preferred_element_type=f32)
    up, cross, early = up_sums.result(), cross.result(), early.result()
    d_up = up[:k_rows, :n_up]
    if trees:
        down = up[k_rows:]
        d_down = jnp.concatenate([down[:each], down[each:, : ff_width - fold]], axis=1).T
    d_cq, d_cout = cross[:, :n_one], cross[:, n_one : 2 * n_one]
    d_sqkv, d_sout = early[:, :n_sqkv], early[:, n_sqkv : n_sqkv + n_one]

    return (
        mixed,
        grad_tokens,
        d_ada,
        d_sqkv,
        d_sout,
        d_cq,
        d_ckv,
        d_cout,
        d_up,
        d_down,
        d_tqkv,
        d_tout,
    )


def solution(mesh):
    rows = P(("gy", "gx"), None)
    both = P("gy", "gx")
    return jax.shard_map(
        local,
        mesh=mesh,
        in_specs=(rows, rows, P(), P(), P(), P(), P()) + (both,) * 10 + (rows,),
        out_specs=(rows, rows) + (both,) * 10,
        check_vma=False,
    )
```

```python
import functools
import math

import jax
import jax.numpy as jnp
from jax import lax
from jax.experimental import pallas as pl
from jax.experimental.pallas import tpu as pltpu
from jax.sharding import PartitionSpec as P

D = 1152
HEADS = 16
HEAD_DIM = 72
FRAME = 1024
CLIPS = 4

norm_eps = 1e-06
masked_score = -1e30
highest = lax.Precision.HIGHEST
f32 = jnp.float32
bf16 = jnp.bfloat16
score_scale = HEAD_DIM ** (-0.5)
log2_scale = score_scale * math.log2(math.e)
row_axes = ("gy", "gx")
nt = (((1,), (1,)), ((), ()))


def vmem():
    return pl.BlockSpec(memory_space=pltpu.VMEM)


def smem():
    return pl.BlockSpec(memory_space=pltpu.SMEM)


def hbm():
    return pl.BlockSpec(memory_space=pl.ANY)


def shape(*size, dtype=f32):
    return jax.ShapeDtypeStruct(size, dtype)


def cost(micros):
    return pl.CostEstimate(flops=micros * 20000000, bytes_accessed=0, transcendentals=0)


def run(kernel, outs, specs, scratch, args, micros):
    flat, tree = jax.tree.flatten(tuple(args))
    flat_specs = []
    for arg, spec in zip(args, specs):
        flat_specs += [spec] * len(jax.tree.leaves(arg))

    def grouped(*refs):
        kernel(*jax.tree.unflatten(tree, refs[: len(flat)]), *refs[len(flat) :])

    return pl.pallas_call(
        grouped,
        out_shape=outs,
        in_specs=flat_specs,
        out_specs=[vmem() for _ in outs],
        scratch_shapes=scratch,
        compiler_params=pltpu.CompilerParams(vmem_limit_bytes=56 << 20),
        cost_estimate=cost(micros),
    )(*flat)


class Window:
    def __init__(self, lo, hi):
        self.lo, self.hi = lo, hi
        self.start = lo // 128 * 128
        self.stop = -(-hi // 128) * 128
        self.off = lo - self.start
        self.n = hi - lo
        self.width = self.stop - self.start

    def inside(self, outer):
        return Window(self.lo - outer.start, self.hi - outer.start)


def padded(lanes):
    return -(-lanes // 128) * 128


def piece_places(nx):
    half = nx // 4
    for core in range(2):
        for k, (first, last, low) in enumerate(((1, 0, 0), (1, 2, 0), (2, 0, half), (2, 1, half))):
            for i in range(2):
                for j in range(half):
                    yield core * 4 + k, i, j, (2 * (low + j)) ^ core, (first * i) ^ last


class Pieces:
    def __init__(self, sources, me, window, buffer, sems, nx):
        rows = buffer.shape[1] // 4
        columns = slice(window.start, window.stop)
        for k, i, j, far_x, far_y in piece_places(nx):
            x, y = me[0] ^ far_x, me[1] ^ far_y
            pltpu.make_async_copy(
                sources[k].at[i, j, :rows, columns],
                buffer.at[x, pl.ds(pl.multiple_of(y * rows, 16), rows), :],
                sems.at[x],
            ).start()
        self.buffer, self.sems = buffer, sems

    def wait(self, x):
        pltpu.make_async_copy(self.buffer.at[x], self.buffer.at[x], self.sems.at[x]).wait()


class Blocks:
    def __init__(self, source, buffer, sems):
        self.copies = [
            pltpu.make_async_copy(source.at[i], buffer.at[i], sems.at[i])
            for i in range(source.shape[0])
        ]
        for copy in self.copies:
            copy.start()

    def wait(self, i):
        self.copies[i].wait()


class Folded:
    def __init__(self, sources, me, buffer, sems, nx):
        rows = buffer.shape[1] // nx
        base = sources[0].shape[2] - 2 * rows
        width = buffer.shape[2]
        fold = fold_width(width)
        for k, i, j, far_x, far_y in piece_places(nx):
            x, y = me[0] ^ far_x, me[1] ^ far_y
            place = pl.ds(pl.multiple_of(x * rows, 16), rows)
            for top, columns in ((base, slice(0, fold)), (base + rows, slice(fold, width))):
                pltpu.make_async_copy(
                    sources[k].at[i, j, top : top + rows, : columns.stop - columns.start],
                    buffer.at[y, place, columns],
                    sems.at[y],
                ).start()
        self.buffer, self.sems = buffer, sems

    def wait(self, y):
        pltpu.make_async_copy(self.buffer.at[y], self.buffer.at[y], self.sems.at[y]).wait()


def fold_width(width):
    return padded(width // 2)


def down_blocks(up_refs, down_ref, me_ref, buf, sems, nx):
    if down_ref is None:
        return Folded(up_refs, me_ref, buf, sems, nx)
    return Blocks(down_ref, buf, sems)


def stats(values):
    centred = values - jnp.mean(values, axis=-1, keepdims=True)
    inv_std = lax.rsqrt(jnp.mean(centred * centred, axis=-1, keepdims=True) + norm_eps)
    return centred * inv_std, inv_std


def stats_back(grad_norm, normed, inv_std):
    return inv_std * (
        grad_norm
        - jnp.mean(grad_norm, axis=-1, keepdims=True)
        - normed * jnp.mean(grad_norm * normed, axis=-1, keepdims=True)
    )


def mm(left, right):
    return jnp.dot(left, right, preferred_element_type=f32)


def mm_nt(left, right):
    return lax.dot_general(left, right, nt, preferred_element_type=f32)


def put(dests, start, value):
    base, width = 0, value.shape[1]
    for ref in dests:
        size = ref.shape[1]
        lo, hi = max(start, base), min(start + width, base + size)
        if lo < hi:
            ref[:, lo - base : hi - base] = value[:, lo - start : hi - start].astype(ref.dtype)
        base += size


def take(pad, off, sources, start, width):
    base = 0
    for ref in sources:
        size = ref.shape[1]
        lo, hi = max(start, base), min(start + width, base + size)
        if lo < hi:
            pad[:, off + lo - start : off + hi - start] = ref[:, lo - base : hi - base]
        base += size


def head(h):
    return slice(h * HEAD_DIM, (h + 1) * HEAD_DIM)


def gelu_parts(u):
    c = math.sqrt(2.0 / math.pi)
    square = u * u
    return jnp.tanh(c * u * (1.0 + 0.044715 * square)), square, c


def qkv_kernel(win, nx, me_ref, x_ref, mod_ref, w_refs, h_ref, q_ref, kv_ref, buf, sems):
    pieces = Pieces(w_refs, me_ref, win, buf, sems, nx)
    normed, _ = stats(x_ref[...].astype(f32))
    hidden = (normed * (1.0 + mod_ref[1:2, :]) + mod_ref[0:1, :]).astype(bf16)
    h_ref[...] = hidden
    for x in range(nx):
        pieces.wait(x)
        block = mm(hidden, buf[x])[:, win.off : win.off + win.n]
        put([q_ref, kv_ref], x * win.n, block)


def stage_heads(dest, row, source, start):
    rows = source.shape[0]
    for h in range(HEADS):
        dest[h, row : row + rows, :HEAD_DIM] = source[
            :, start + h * HEAD_DIM : start + (h + 1) * HEAD_DIM
        ]


def spatial_kernel(pieces, *refs):
    q_ref = refs[0]
    kv_refs = refs[1 : 1 + pieces]
    o_ref, lse_ref, q_t, v_t, k_heads, o_t = refs[1 + pieces :]
    rows = q_ref.shape[0]
    q_t[...] = q_ref[...].astype(f32).T
    for i, kv in enumerate(kv_refs):
        v_t[:, i * rows : (i + 1) * rows] = kv[:, D:].astype(f32).T
        stage_heads(k_heads, i * rows, kv, 0)

    def one_head(h, carry):
        span = pl.ds(pl.multiple_of(h * HEAD_DIM, 8), HEAD_DIM)
        scores = mm(k_heads[h, :, :HEAD_DIM], q_t[span, :].astype(bf16)) * log2_scale
        top = jnp.max(scores, axis=0, keepdims=True)
        weights = jnp.exp2(scores - top)
        total = jnp.sum(weights, axis=0, keepdims=True)
        o_t[span, :] = mm(v_t[span, :].astype(bf16), weights.astype(bf16)) / total
        lse_ref[pl.ds(h, 1), :] = top + jnp.log2(total)
        return carry

    lax.fori_loop(0, HEADS, one_head, 0)
    o_ref[...] = o_t[...].T.astype(bf16)


def text_probs(text_ref, q_t, h, length):
    scores = mm(text_ref[:, head(h)], q_t[head(h), :].astype(bf16)) * score_scale
    slot = lax.broadcasted_iota(jnp.int32, scores.shape, 0)
    scores = jnp.where(slot < length, scores, masked_score)
    weights = jnp.exp(scores - jnp.max(scores, axis=0, keepdims=True))
    return weights / jnp.sum(weights, axis=0, keepdims=True)


def text_kernel(
    outer, w_out, w_cq, w_cout, nx, me_ref, x_ref, o_ref, mod_ref, w_refs, text_ref, length_ref,
    a1_ref, x1_ref, hc_ref, qc_ref, oc_ref, x2_ref, h3_ref,
    buf, sems, acc, q_t, v_t,
):
    pieces = Pieces(w_refs, me_ref, outer, buf, sems, nx)

    def product(left, win, dest, wait=False):
        for x in range(nx):
            if wait:
                pieces.wait(x)
            block = mm(left, buf[x, :, win.start : win.stop])[:, win.off : win.off + win.n]
            put([dest], x * win.n, block)

    product(o_ref[...], w_out, a1_ref, wait=True)
    after_a = x_ref[...].astype(f32) + mod_ref[2:3, :] * a1_ref[...]
    x1_ref[...] = after_a
    hidden = stats(after_a)[0].astype(bf16)
    hc_ref[...] = hidden
    product(hidden, w_cq, qc_ref)
    q_t[...] = qc_ref[...].astype(f32).T
    v_t[...] = text_ref[:, D:].astype(f32).T
    length = length_ref[0]
    for h in range(HEADS):
        probs = text_probs(text_ref, q_t, h, length).astype(bf16)
        acc[head(h), :] = mm(v_t[head(h), :].astype(bf16), probs)
    oc_ref[...] = acc[...].T.astype(bf16)
    product(oc_ref[...], w_cout, x2_ref)
    after_b = x1_ref[...] + x2_ref[...]
    x2_ref[...] = after_b
    h3_ref[...] = (
        stats(after_b)[0] * (1.0 + mod_ref[4:5, :]) + mod_ref[3:4, :]
    ).astype(bf16)


def ff_kernel(
    win, nx, ny, me_ref, h_ref, x2_ref, mod_ref, up_refs, down_ref,
    u_ref, g_ref, m_ref, x3_ref, h4_ref, up_buf, down_buf, up_sems, down_sems,
):
    ups = Pieces(up_refs, me_ref, win, up_buf, up_sems, nx)
    width = down_buf.shape[2]
    downs = down_blocks(up_refs, down_ref, me_ref, down_buf, down_sems, nx)
    hidden = h_ref[...]
    for x in range(nx):
        ups.wait(x)
        u = mm(hidden, up_buf[x])[:, win.off : win.off + win.n]
        put([u_ref], x * win.n, u)
        put([g_ref], x * win.n, 0.5 * u * (1.0 + gelu_parts(u)[0]))
    total = jnp.zeros(m_ref.shape, f32)
    for i in range(ny):
        downs.wait(i)
        total = total + mm_nt(g_ref[:, i * width : (i + 1) * width], down_buf[i])
    m_ref[...] = total
    after_c = x2_ref[...] + mod_ref[5:6, :] * total
    x3_ref[...] = after_c
    h4_ref[...] = (
        stats(after_c)[0] * (1.0 + mod_ref[7:8, :]) + mod_ref[6:7, :]
    ).astype(bf16)


def temporal_kernel(
    win, w_out, nx, frames, h_ref, da_ref, w_ref, row_clip, frame_clip,
    grad_ref, at_ref, dh_ref, buf, sems, pad, q_s, k_s, v_s, do_s, o_s, dq_s, dk_s, dv_s, qkv_s,
):
    pieces = Blocks(w_ref, buf, sems)
    o_ref, dqkv_ref = grad_ref.at[:, :D], grad_ref.at[:, D:]
    rows = h_ref.shape[0]
    spots = rows // frames
    hidden = h_ref[...]
    out_cols = slice(w_out.start, w_out.stop)
    pad[...] = jnp.zeros(pad.shape, bf16)
    total = jnp.zeros(h_ref.shape, f32)
    for x in range(nx):
        pieces.wait(x)
        block = mm(hidden, buf[x, :, win.start : win.stop])[:, win.off : win.off + win.n]
        put([qkv_s], x * win.n, block)
        take(pad, w_out.off, [da_ref], x * w_out.n, w_out.n)
        total = total + mm_nt(pad[:, : w_out.width], buf[x, :, out_cols])
    do_s[...] = total.astype(bf16).astype(f32)
    q_s[...] = qkv_s[:, :D].astype(f32)
    k_s[...] = qkv_s[:, D : 2 * D].astype(f32)
    v_s[...] = qkv_s[:, 2 * D :].astype(f32)
    dk_s[...] = jnp.zeros(dk_s.shape, f32)
    dv_s[...] = jnp.zeros(dv_s.shape, f32)

    def one_hot(size, feature, slot):
        first = lax.broadcasted_iota(jnp.int32, size, slot) * HEAD_DIM
        place = lax.broadcasted_iota(jnp.int32, size, feature)
        return jnp.where((place >= first) & (place < first + HEAD_DIM), 1.0, 0.0).astype(bf16)

    gather = one_hot((D, 128), 0, 1)
    spread = one_hot((128, D), 1, 0)

    def per_head(values):
        high = values.astype(bf16)
        low = (values - high.astype(f32)).astype(bf16)
        return mm(high, gather) + mm(low, gather)

    def every_frame(values):
        return jnp.broadcast_to(values[None], (frames, spots, D)).reshape(rows, D)

    def over_frames(values):
        return jnp.sum(values.reshape(frames, spots, values.shape[-1]), axis=0)

    def one_frame(f, carry):
        span = pl.ds(pl.multiple_of(f * spots, 8), spots)
        queries = every_frame(q_s[span, :])
        grads = every_frame(do_s[span, :])
        scores = per_head(queries * k_s[...]) * score_scale
        scores = jnp.where(row_clip[...] == frame_clip[f], scores, masked_score)
        scores = scores.reshape(frames, spots, 128)
        weights = jnp.exp(scores - jnp.max(scores, axis=0, keepdims=True))
        probs = weights / jnp.sum(weights, axis=0, keepdims=True)
        grad_probs = per_head(grads * v_s[...]).reshape(frames, spots, 128)
        inner = jnp.sum(probs * grad_probs, axis=0, keepdims=True)
        grad_scores = (probs * (grad_probs - inner)).reshape(rows, 128).astype(bf16)
        probs_wide = mm(probs.reshape(rows, 128).astype(bf16), spread)
        grads_wide = mm(grad_scores, spread)
        o_s[span, :] = over_frames(probs_wide * v_s[...])
        dq_s[span, :] = over_frames(grads_wide * k_s[...]) * score_scale
        dk_s[...] += grads_wide * queries
        dv_s[...] += probs_wide * grads
        return carry

    lax.fori_loop(0, frames, one_frame, 0)
    o_ref[...] = o_s[...].astype(bf16)
    for x in range(nx):
        block = mm(o_ref[...], buf[x, :, out_cols])[:, w_out.off : w_out.off + w_out.n]
        put([at_ref], x * w_out.n, block)
    dqkv_ref[:, :D] = dq_s[...].astype(bf16)
    dqkv_ref[:, D : 2 * D] = (dk_s[...] * score_scale).astype(bf16)
    dqkv_ref[:, 2 * D :] = dv_s[...].astype(bf16)
    pad[...] = jnp.zeros(pad.shape, bf16)
    total = jnp.zeros(dh_ref.shape, f32)
    for x in range(nx):
        take(pad, win.off, [dqkv_ref], x * win.n, win.n)
        total = total + mm_nt(pad[:, : win.width], buf[x, :, win.start : win.stop])
    dh_ref[...] = total.astype(bf16)


def mixed_kernel(at_ref, x3_ref, g_ref, mod_ref, keep_ref, y_ref, gate_ref):
    branch = at_ref[...].astype(f32)
    keep = keep_ref[0]
    y_ref[...] = (x3_ref[...] + keep * mod_ref[8:9, :] * branch).astype(bf16)
    gate_ref[...] = jnp.sum(keep * g_ref[...].astype(f32) * branch, axis=0, keepdims=True)


def column_sum(values):
    return jnp.sum(values, axis=0, keepdims=True)


def ff_back_kernel(
    win, nx, ny, me_ref, g_ref, dh4_ref, x3_ref, x2_ref, u_ref, m_ref, mod_ref, up_refs, down_ref,
    grad_ref, dx2_ref, sum_ref, up_buf, down_buf, up_sems, down_sems, pad,
):
    ff = u_ref.shape[1]
    du_s, dm_ref = grad_ref.at[:, :ff], grad_ref.at[:, ff:]
    width = down_buf.shape[2]
    downs = down_blocks(up_refs, down_ref, me_ref, down_buf, down_sems, nx)
    ups = Pieces(up_refs, me_ref, win, up_buf, up_sems, nx)
    dh4 = dh4_ref[...].astype(f32)
    normed, inv_std = stats(x3_ref[...])
    dx3 = g_ref[...].astype(f32) + stats_back(dh4 * (1.0 + mod_ref[7:8, :]), normed, inv_std)
    sum_ref[0:1, :] = column_sum(dh4)
    sum_ref[1:2, :] = column_sum(dh4 * normed)
    sum_ref[2:3, :] = column_sum(dx3 * m_ref[...])
    dm = (mod_ref[5:6, :] * dx3).astype(bf16)
    dm_ref[...] = dm
    for i in range(ny):
        downs.wait(i)
        grad = mm(dm, down_buf[i])
        u = u_ref[:, i * width : (i + 1) * width]
        tanh, square, c = gelu_parts(u)
        slope = 0.5 * (1.0 + tanh) + 0.5 * u * (1.0 - tanh * tanh) * (
            c * (1.0 + 3.0 * 0.044715 * square)
        )
        du_s[:, i * width : (i + 1) * width] = (grad * slope).astype(bf16)
    pad[...] = jnp.zeros(pad.shape, bf16)
    total = jnp.zeros(dx2_ref.shape, f32)
    for x in range(nx):
        ups.wait(x)
        take(pad, win.off, [du_s], x * win.n, win.n)
        total = total + mm_nt(pad[...], up_buf[x])
    normed, inv_std = stats(x2_ref[...])
    sum_ref[3:4, :] = column_sum(total)
    sum_ref[4:5, :] = column_sum(total * normed)
    sum_ref[5:8, :] = jnp.zeros((3, D), f32)
    dx2_ref[...] = dx3 + stats_back(total * (1.0 + mod_ref[4:5, :]), normed, inv_std)


def text_back_kernel(
    outer, w_out, w_cq, w_cout, nx, me_ref, dx2_ref, x1_ref, a1_ref, mod_ref, w_refs, qc_ref, text_ref,
    length_ref, grad_ref, dx1_ref, do1_ref, dtext_ref, gate_ref,
    buf, sems, pad, acc, q_t, do_t, k_t, do_s, dtext_s,
):
    dac_ref, dqc_ref, da1_ref = [grad_ref.at[:, i * D : (i + 1) * D] for i in range(3)]
    pieces = Pieces(w_refs, me_ref, outer, buf, sems, nx)

    def product(source, win, wait=False):
        pad[...] = jnp.zeros(pad.shape, bf16)
        total = jnp.zeros(dx2_ref.shape, f32)
        for x in range(nx):
            if wait:
                pieces.wait(x)
            take(pad, win.off, [source], x * win.n, win.n)
            total = total + mm_nt(pad[:, : win.width], buf[x, :, win.start : win.stop])
        return total

    dx2 = dx2_ref[...]
    dac_ref[...] = dx2.astype(bf16)
    grad_o = product(dac_ref, w_cout, wait=True).astype(bf16)
    do_s[...] = grad_o
    do_t[...] = grad_o.astype(f32).T
    q_t[...] = qc_ref[...].astype(f32).T
    k_t[...] = text_ref[:, :D].astype(f32).T
    length = length_ref[0]
    for h in range(HEADS):
        probs = text_probs(text_ref, q_t, h, length)
        values = text_ref[:, D + h * HEAD_DIM : D + (h + 1) * HEAD_DIM]
        grad_probs = mm(values, do_t[head(h), :].astype(bf16))
        inner = jnp.sum(probs * grad_probs, axis=0, keepdims=True)
        grad_scores = (probs * (grad_probs - inner)).astype(bf16)
        dtext_s[:, head(h)] = mm(grad_scores, qc_ref[:, head(h)]) * score_scale
        dtext_s[:, D + h * HEAD_DIM : D + (h + 1) * HEAD_DIM] = mm(
            probs.astype(bf16), do_s[:, head(h)]
        )
        acc[head(h), :] = mm(k_t[head(h), :].astype(bf16), grad_scores) * score_scale
    width = dtext_ref.shape[2]
    for x in range(nx):
        dtext_ref[x] = dtext_s[:, x * width : (x + 1) * width].astype(bf16)
    dqc_ref[...] = acc[...].T.astype(bf16)
    normed, inv_std = stats(x1_ref[...])
    dx1 = dx2 + stats_back(product(dqc_ref, w_cq), normed, inv_std)
    dx1_ref[...] = dx1
    gate_ref[...] = column_sum(dx1 * a1_ref[...])
    da1_ref[...] = (mod_ref[2:3, :] * dx1).astype(bf16)
    do1_ref[...] = product(da1_ref, w_out).astype(bf16)


def spatial_back_kernel(pieces, *refs):
    q_ref, do_ref, o_ref, lse_ref = refs[:4]
    kv_refs = refs[4 : 4 + pieces]
    (
        dq_ref, dkv_ref,
        q_t, do_t, o_t, k_t, dq_t, q_heads, do_heads, k_heads, v_heads, dk_heads, dv_heads,
    ) = refs[4 + pieces :]
    rows = q_ref.shape[0]
    q_t[...] = q_ref[...].astype(f32).T
    do_t[...] = do_ref[...].astype(f32).T
    o_t[...] = o_ref[...].astype(f32).T
    stage_heads(q_heads, 0, q_ref, 0)
    stage_heads(do_heads, 0, do_ref, 0)
    for i, kv in enumerate(kv_refs):
        k_t[:, i * rows : (i + 1) * rows] = kv[:, :D].astype(f32).T
        stage_heads(k_heads, i * rows, kv, 0)
        stage_heads(v_heads, i * rows, kv, D)

    def one_head(h, carry):
        span = pl.ds(pl.multiple_of(h * HEAD_DIM, 8), HEAD_DIM)
        grad_o = do_t[span, :]
        inner = jnp.sum(grad_o * o_t[span, :], axis=0, keepdims=True)
        scores = mm(k_heads[h, :, :HEAD_DIM], q_t[span, :].astype(bf16)) * log2_scale
        probs = jnp.exp2(scores - lse_ref[pl.ds(h, 1), :])
        grad_probs = mm(v_heads[h, :, :HEAD_DIM], grad_o.astype(bf16))
        grad_scores = (probs * (grad_probs - inner)).astype(bf16)
        dv_heads[h, :, :HEAD_DIM] = mm(probs.astype(bf16), do_heads[h, :, :HEAD_DIM]).astype(bf16)
        dk_heads[h, :, :HEAD_DIM] = (
            mm(grad_scores, q_heads[h, :, :HEAD_DIM]) * score_scale
        ).astype(bf16)
        dq_t[span, :] = mm(k_t[span, :].astype(bf16), grad_scores) * score_scale
        return carry

    lax.fori_loop(0, HEADS, one_head, 0)
    dq_ref[...] = dq_t[...].T.astype(bf16)
    for i in range(pieces):
        span = slice(i * rows, (i + 1) * rows)
        for h in range(HEADS):
            dkv_ref[i, :, head(h)] = dk_heads[h, span, :HEAD_DIM]
            dkv_ref[i, :, D + h * HEAD_DIM : D + (h + 1) * HEAD_DIM] = dv_heads[
                h, span, :HEAD_DIM
            ]


def qkv_back_kernel(
    win, nx, me_ref, dq_ref, own_ref, come_ref, x_ref, mod_ref, dx1_ref, w_refs,
    grad_ref, gx_ref, sum_ref, buf, sems, pad,
):
    dkv_ref = grad_ref.at[:, D:]
    grad_ref[:, :D] = dq_ref[...]
    pieces = Pieces(w_refs, me_ref, win, buf, sems, nx)
    dkv_ref[...] = (own_ref[...].astype(f32) + come_ref[...].astype(f32)).astype(bf16)
    pad[...] = jnp.zeros(pad.shape, bf16)
    total = jnp.zeros(dx1_ref.shape, f32)
    for x in range(nx):
        pieces.wait(x)
        take(pad, win.off, [grad_ref], x * win.n, win.n)
        total = total + mm_nt(pad[...], buf[x])
    normed, inv_std = stats(x_ref[...].astype(f32))
    sum_ref[0:1, :] = column_sum(total)
    sum_ref[1:2, :] = column_sum(total * normed)
    gx_ref[...] = (
        dx1_ref[...] + stats_back(total * (1.0 + mod_ref[1:2, :]), normed, inv_std)
    ).astype(bf16)


def turn_rows(turn, at, value, me_y, ny):
    rows = turn.shape[0] // ny
    flipped = value.astype(f32).T.astype(bf16)
    for y in range(ny):
        place = pl.ds(pl.multiple_of((y ^ me_y) * rows, 16), rows)
        turn[place, at : at + value.shape[0]] = flipped[y * rows : (y + 1) * rows]


def write_blocks(outs, half, columns, block, first=0):
    some_send, rest_send, some_keep, rest_keep = outs
    rows, each = block.shape[0] // 4, some_keep.shape[1] // 2
    step = pl.program_id(0)

    def write(ref, at, y):
        start = at * each + first
        ref[0, start : start + rows, columns] = block[y * rows : (y + 1) * rows]

    @pl.when(step < half)
    def _():
        for at in range(2):
            write(some_keep, at, at)
            write(some_send, at, 2 + at)

    @pl.when(step >= half)
    def _():
        for at in range(2):
            write(rest_keep, at, 2 * at)
            write(rest_send, at, 2 * at + 1)


def block_outs(nx, depth, lanes):
    half = nx // 4
    size = (1, depth // 2, lanes)
    some = pl.BlockSpec(size, lambda t, me: (jnp.minimum(t, half - 1), 0, 0))
    rest = pl.BlockSpec(size, lambda t, me: (jnp.maximum(t - half, 0), 0, 0))
    return [shape(half, depth // 2, lanes, dtype=bf16)] * 4, [some, rest, some, rest]


def view(refs, place):
    k, first, last = place
    return refs[k].at[:, first:last]


def weight_kernel(nx, ny, lanes, count, pairs, me_ref, *refs):
    sides, outs = (refs[:count], refs[count : 2 * count]), refs[2 * count : 2 * count + 4]
    pads, turned = refs[2 * count + 4 :: 2], refs[2 * count + 5 :: 2]
    step = pl.program_id(0)
    x = me_ref[0] ^ (2 * step)
    rows = refs[0].shape[0]

    @pl.when(step == 0)
    def _():
        for (left, _), turn in zip(pairs, turned):
            for i, side in enumerate(sides):
                turn_rows(turn, i * rows, view(side, left)[...], me_ref[1], ny)

    at = 0
    for (_, right), pad, turn in zip(pairs, pads, turned):
        n = pad.shape[1]
        for i in range(nx):

            @pl.when(x == i)
            def _():
                for k, side in enumerate(sides):
                    take(pad.at[k * rows : (k + 1) * rows], 0, [view(side, right)], i * n, n)

        block = mm(turn[...], pad[...]).astype(bf16)
        write_blocks(outs, nx // 4, slice(at, at + n), block)
        at += n
    if at < lanes:
        write_blocks(outs, nx // 4, slice(at, lanes), jnp.zeros((D, lanes - at), bf16))


def weight_grads(nx, me, own, other, pairs):
    widths = [(last - first) // nx for _, (_, first, last) in pairs]
    lanes = padded(sum(widths))
    rows = own[0].shape[0]
    scratch = []
    for width in widths:
        scratch += [pltpu.VMEM((2 * rows, width), bf16), pltpu.VMEM((D, 2 * rows), bf16)]
    outs, out_specs = block_outs(nx, D, lanes)
    return pl.pallas_call(
        functools.partial(weight_kernel, nx, lax.axis_size("gy"), lanes, len(own), pairs),
        out_shape=outs,
        grid_spec=pltpu.PrefetchScalarGridSpec(
            num_scalar_prefetch=1,
            grid=(nx // 2,),
            in_specs=[vmem() for _ in range(2 * len(own))],
            out_specs=out_specs,
            scratch_shapes=scratch,
        ),
        compiler_params=pltpu.CompilerParams(vmem_limit_bytes=56 << 20),
        cost_estimate=cost(9),
    )(me, *own, *other)


def whole_kernel(nx, lanes, pairs, *refs):
    count = 1 + max(k for pair in pairs for k, _, _ in pair)
    ins, out_ref = refs[:count], refs[count]
    pads, turned = refs[count + 1 :: 2], refs[count + 2 :: 2]
    x = pl.program_id(0)

    @pl.when(x == 0)
    def _():
        for (left, _), turn in zip(pairs, turned):
            turn[...] = view(ins, left)[...].astype(f32).T.astype(bf16)

    at = 0
    for (_, right), pad, turn in zip(pairs, pads, turned):
        n = pad.shape[1]
        for i in range(nx):

            @pl.when(x == i)
            def _():
                take(pad, 0, [view(ins, right)], i * n, n)

        out_ref[0, :, at : at + n] = mm(turn[...], pad[...]).astype(bf16)
        at += n
    if at < lanes:
        out_ref[0, :, at:] = jnp.zeros((D, lanes - at), bf16)


def whole_grads(nx, arrays, pairs):
    widths = [(last - first) // nx for _, (_, first, last) in pairs]
    lanes = padded(sum(widths))
    rows = arrays[0].shape[0]
    scratch = []
    for width in widths:
        scratch += [pltpu.VMEM((rows, width), bf16), pltpu.VMEM((D, rows), bf16)]
    return pl.pallas_call(
        functools.partial(whole_kernel, nx, lanes, pairs),
        out_shape=shape(nx, D, lanes, dtype=bf16),
        grid=(nx,),
        in_specs=[vmem() for _ in arrays],
        out_specs=pl.BlockSpec((1, D, lanes), lambda x: (x, 0, 0)),
        scratch_shapes=scratch,
        compiler_params=pltpu.CompilerParams(vmem_limit_bytes=56 << 20),
        cost_estimate=cost(13),
    )(*arrays)


def up_grads(nx, me, own, other, folding):
    rows, ff = own[2].shape
    n = ff // nx
    ny = lax.axis_size("gy")
    start = padded(n)
    width = ff // ny
    fold = fold_width(width)
    each = D // nx

    def kernel(me_ref, *refs):
        sides, outs = (refs[:3], refs[3:6]), refs[6:10]
        turn, pad, down_turn, down_pad = refs[-4:]
        step = pl.program_id(0)
        x = me_ref[0] ^ (2 * step)

        @pl.when(step == 0)
        def _():
            for k, (h_ref, grad_ref, _) in enumerate(sides):
                turn_rows(turn, k * rows, h_ref[...], me_ref[1], ny)
                if folding:
                    down_turn[:, k * rows : (k + 1) * rows] = (
                        grad_ref[:, ff:].astype(f32).T.astype(bf16)
                    )

        for i in range(nx):

            @pl.when(x == i)
            def _():
                for k, (_, grad_ref, _) in enumerate(sides):
                    pad[k * rows : (k + 1) * rows] = grad_ref[:, i * n : (i + 1) * n]

        write_blocks(outs, nx // 4, slice(0, n), mm(turn[...], pad[...]).astype(bf16))
        if n < start:
            write_blocks(outs, nx // 4, slice(n, start), jnp.zeros((D, start - n), bf16))
        if not folding:
            return
        left = down_turn[pl.ds(pl.multiple_of(x * each, 16), each), :]
        for y in range(ny):
            columns = slice(y * width, (y + 1) * width)
            block = mm(left[:, :rows], sides[0][2][:, columns])
            block = (block + mm(left[:, rows:], sides[1][2][:, columns])).astype(bf16)
            top = (y ^ me_ref[1]) * 2 * each
            down_pad[pl.ds(pl.multiple_of(top, 16), each), :] = block[:, :fold]
            low = pl.multiple_of(top + each, 16)
            down_pad[pl.ds(low, each), : width - fold] = block[:, fold:]
            down_pad[pl.ds(low, each), width - fold :] = jnp.zeros((each, 2 * fold - width), bf16)
        write_blocks(outs, nx // 4, slice(0, fold), down_pad[...], D // ny)

    outs, out_specs = block_outs(nx, 2 * D if folding else D, start)
    return pl.pallas_call(
        kernel,
        out_shape=outs,
        grid_spec=pltpu.PrefetchScalarGridSpec(
            num_scalar_prefetch=1,
            grid=(nx // 2,),
            in_specs=[vmem()] * 6,
            out_specs=out_specs,
            scratch_shapes=[
                pltpu.VMEM((D, 2 * rows), bf16),
                pltpu.VMEM((2 * rows, n), bf16),
                pltpu.VMEM((D, 2 * rows), bf16),
                pltpu.VMEM((D, fold), bf16),
            ],
        ),
        compiler_params=pltpu.CompilerParams(vmem_limit_bytes=56 << 20),
        cost_estimate=cost(16),
    )(me, *own, *other)


def down_grads(dm, g):
    rows = g.shape[0]
    ny = lax.axis_size("gy")
    width = g.shape[1] // ny

    def kernel(dm_ref, g_ref, out_ref, turn):
        @pl.when(pl.program_id(0) == 0)
        def _():
            turn[...] = dm_ref[...].astype(f32).T.astype(bf16)

        out_ref[0] = mm(turn[...], g_ref[...]).astype(bf16)

    return pl.pallas_call(
        kernel,
        out_shape=shape(ny, D, width, dtype=bf16),
        grid=(ny,),
        in_specs=[vmem(), pl.BlockSpec((rows, width), lambda i: (0, i))],
        out_specs=pl.BlockSpec((1, D, width), lambda i: (i, 0, 0)),
        scratch_shapes=[pltpu.VMEM((D, rows), bf16)],
        compiler_params=pltpu.CompilerParams(vmem_limit_bytes=56 << 20),
        cost_estimate=cost(12),
    )(dm, g)


def after(value, *others):
    return lax.optimization_barrier((value, others))[0]


class Gather:
    def __init__(self, shard):
        self.line = [shard]

    def along(self, fars, *others):
        shard = after(self.line[0], *others)
        new = [swap(shard, "gx", 2 * far) for far in fars]
        self.line = self.line + new
        return new

    def first(self, *others):
        line = after(self.line, *others)
        half = len(line) // 2
        some, rest = jnp.stack(line[:half]), jnp.stack(line[half:])
        self.near = (some, rest)
        self.far = [swap(some, "gy", 1), swap(rest, "gy", 2)]
        return self.far

    def second(self, *others):
        far = after(self.far, *others)
        self.own = [jnp.stack(pair) for pair in zip(self.near, far)]
        self.new = [swap(self.own[0], "gy", 2), swap(self.own[1], "gy", 1)]
        return self.new

    def own_core(self, *others):
        self.own_other = [swap(array, "gx", 1) for array in after(self.own, *others)]
        return self.own_other

    def new_core(self, *others):
        self.new_other = [swap(array, "gx", 1) for array in after(self.new, *others)]
        return self.new_other

    def arrays(self):
        pairs = ((self.own, self.new), (self.own_other, self.new_other))
        return tuple(side[i] for own, new in pairs for i in range(2) for side in (own, new))


def gather_rows(shard):
    ny = lax.axis_size("gy")
    whole = lax.all_gather(shard, row_axes, axis=0, tiled=True)
    return whole.reshape(ny, -1, shard.shape[1])


def total(*terms):
    return sum(term.astype(f32) for term in terms).astype(bf16)


class Scatter:
    def __init__(self, some_send, rest_send, some_keep, rest_keep):
        self.sent = [some_send, rest_send]
        self.kept = [some_keep, rest_keep]
        half, depth, lanes = some_keep.shape
        self.half, self.size = half, (half, 2, depth // 2, lanes)

    def first(self, *others):
        some, rest = after(self.sent, *others)
        self.come = [swap(some, "gy", 2), swap(rest, "gy", 1)]
        return self.come

    def second(self, *others):
        kept = [array.reshape(self.size) for array in self.kept]
        come = [array.reshape(self.size) for array in after(self.come, *others)]
        self.near = list(zip(kept, come))
        self.sent = [total(mine[:, 1], theirs[:, 1]) for mine, theirs in self.near]
        self.come = [swap(self.sent[0], "gy", 1), swap(self.sent[1], "gy", 2)]
        return self.come

    def line(self, *others):
        come = after(self.come, *others)
        some, rest = [
            total(mine[:, 0], theirs[:, 0], last)
            for (mine, theirs), last in zip(self.near, come)
        ]
        self.ends = [some[i] for i in range(self.half)] + [rest[i] for i in range(self.half)]
        self.got = []

    def along(self, fars, *others):
        new = [swap(after(self.ends[far], *others), "gx", 2 * far) for far in fars]
        self.got = self.got + new
        return new

    def result(self):
        return sum([term.astype(f32) for term in self.got], self.ends[0].astype(f32))


def scatter(blocks, axes):
    flat = blocks.reshape(-1, blocks.shape[-1])
    return lax.psum_scatter(flat, axes, scatter_dimension=0, tiled=True).astype(f32)


def swap(values, axis, mask):
    return lax.ppermute(values, axis, [(i, i ^ mask) for i in range(lax.axis_size(axis))])


def reorder(values):
    devices = lax.axis_size(row_axes)
    return lax.all_to_all(
        values.reshape(devices, values.shape[0] // devices, values.shape[1]),
        row_axes,
        split_axis=0,
        concat_axis=0,
        tiled=True,
    ).reshape(values.shape)


def pad_lanes(values):
    return jnp.pad(values, ((0, 0), (0, padded(values.shape[1]) - values.shape[1])))


def condition(timesteps, pooled_text):
    half_width = D // 2
    frequency = jnp.exp(
        -math.log(10000.0) * jnp.arange(half_width).astype(jnp.float32) / half_width
    )
    angles = timesteps.astype(jnp.float32)[:, None] * frequency[None, :]
    embedded = jnp.concatenate([jnp.cos(angles), jnp.sin(angles)], axis=1)
    return jax.nn.silu(embedded + pooled_text)


def local(
    tokens,
    text_states,
    pooled_text,
    timesteps,
    frame_counts,
    still_clips,
    text_lengths,
    w_ada,
    w_sqkv,
    w_sout,
    w_cq,
    w_ckv,
    w_cout,
    w_up,
    w_down,
    w_tqkv,
    w_tout,
    grad_out,
):
    nx, ny = lax.axis_size("gx"), lax.axis_size("gy")
    gx, gy = lax.axis_index("gx"), lax.axis_index("gy")
    devices = nx * ny
    me = jnp.stack([gx, gy]).astype(jnp.int32)
    device = gy * nx + gx
    rows = tokens.shape[0]
    frame_devs = FRAME // rows
    frames = rows * devices // FRAME
    k_rows = w_ada.shape[0]
    clip_ends = jnp.cumsum(frame_counts)
    clip_here = jnp.sum((clip_ends <= device // frame_devs).astype(jnp.int32))
    clip_mark = jnp.arange(CLIPS) == clip_here
    clip_pick = clip_mark.astype(f32)
    keep_here = (1.0 - jnp.sum(clip_pick * still_clips.astype(f32))).reshape(1)
    length_here = jnp.sum(jnp.where(clip_mark, text_lengths, 0)).reshape(1)
    frame_clip = jnp.sum(
        (clip_ends[None, :] <= jnp.arange(frames)[:, None]).astype(jnp.int32), axis=1
    ).astype(f32)
    row_clip = jnp.repeat(frame_clip, rows // frames)[:, None]

    n_sqkv, n_one, n_up = w_sqkv.shape[1], w_sout.shape[1], w_up.shape[1]
    shard_a = pad_lanes(jnp.concatenate([w_sqkv, w_sout, w_cq, w_cout], axis=1))
    shard_d = pad_lanes(jnp.concatenate([w_tqkv, w_tout], axis=1))
    shard_up = pad_lanes(w_up)
    each = w_down.shape[1]
    fold = fold_width(w_down.shape[0])
    trees = each % 16 == 0 and 2 * each == k_rows and fold == padded(n_up)
    if trees:
        turned = w_down.T
        rest = jnp.pad(turned[:, fold:], ((0, 0), (0, 2 * fold - turned.shape[1])))
        shard_up = jnp.concatenate([shard_up, turned[:, :fold], rest])
    fars = range(1, nx // 2)
    get_a, get_up = Gather(shard_a), Gather(shard_up)
    get_a.along(fars)
    cond_all = condition(timesteps, pooled_text)
    cond_rows = lax.dynamic_slice_in_dim(cond_all, gy * k_rows, k_rows, axis=1)
    mod_part = jnp.dot(cond_rows, w_ada.astype(f32), precision=highest)
    mod_part = mod_part + swap(mod_part, "gy", 1)
    mod_all = (mod_part + swap(mod_part, "gy", 2))[None]
    mod_first = mod_all
    own_text = text_states.shape[0]
    text_rows = text_states.reshape(own_text // CLIPS, CLIPS, -1).transpose(1, 0, 2)
    depth = w_ckv.shape[0]
    text_rows = after(text_rows.reshape(own_text, ny, depth).transpose(1, 0, 2), mod_first)
    text_rows = lax.all_to_all(text_rows, "gy", split_axis=0, concat_axis=0, tiled=True)
    text_rows = lax.all_gather(text_rows, "gx", axis=0)
    bit = 1
    while bit < nx:
        if 2 * bit == nx:
            mod_all = after(mod_all, text_rows, *get_a.line)
        come = swap(mod_all, "gx", bit)
        mod_all = jnp.where(
            gx & bit != 0,
            jnp.concatenate([come, mod_all]),
            jnp.concatenate([mod_all, come]),
        )
        bit *= 2
    mod = lax.dynamic_index_in_dim(mod_all, clip_here, axis=1, keepdims=False).reshape(9, D)
    done = [mod_all]
    held = done
    done = get_a.first(*held) + get_up.along(fars[:2], *held)
    text_block = (
        after(text_rows, *held)
        .reshape(nx, ny, CLIPS, own_text // CLIPS, depth)
        .transpose(2, 1, 0, 3, 4)
        .reshape(own_text * devices, depth)
    )
    text_part = jnp.dot(text_block, w_ckv, preferred_element_type=f32)
    done += [text_part]
    grad_branch_d = (keep_here[0] * mod[8] * grad_out.astype(f32)).astype(bf16)
    held = done
    done = get_a.second(*held) + get_a.own_core()
    done += get_up.along(fars[2:], *held, *get_a.own_other)
    text_sum = lax.psum_scatter(
        after(text_part, *held), "gy", scatter_dimension=0, tiled=True
    )
    done += [text_sum]
    held = done
    up_far = get_up.first(*held)
    done = get_a.new_core(*held, *get_up.near)
    full_a = get_a.arrays()
    ff_width = w_down.shape[0]
    ff = ff_width * ny
    win_sqkv = Window(0, n_sqkv)
    at = n_sqkv
    win_rest = Window(at, at + 3 * n_one)
    win_sout, win_cq, win_cout = [
        Window(at + i * n_one, at + (i + 1) * n_one).inside(win_rest) for i in range(3)
    ]
    win_up = Window(0, n_up)
    win_d = Window(0, n_sqkv + n_one)
    win_tqkv = Window(0, n_sqkv)
    win_tout = Window(n_sqkv, n_sqkv + n_one)


    win = win_sqkv
    hidden_a, query_a, pair_a = run(
        functools.partial(qkv_kernel, win, nx),
        [
            shape(rows, D, dtype=bf16),
            shape(rows, D, dtype=bf16),
            shape(rows, 2 * D, dtype=bf16),
        ],
        [smem()] + [vmem(), vmem(), hbm()],
        [pltpu.VMEM((nx, D, win.width), bf16), pltpu.SemaphoreType.DMA((nx,))],
        (me, tokens, after(mod, *done), full_a),
        9,
    )
    up_near = get_up.second(*up_far, pair_a)
    up_own = get_up.own_core()
    pairs = [after(pair_a, *up_far)]
    bit = frame_devs // 2
    while bit:
        pairs = pairs + [swap(p, "gx", bit) for p in pairs]
        bit //= 2
    text_all = lax.all_gather(after(text_sum, *held).astype(bf16), row_axes, axis=0)
    full_d = lax.all_gather(after(shard_d, text_all), ("gx", "gy"), axis=0, tiled=True)
    full_d = full_d.reshape(nx, D, -1)
    slots = own_text * devices // CLIPS
    text_all = text_all.reshape(ny, nx, -1, w_ckv.shape[1]).transpose(0, 2, 1, 3)
    text_all = text_all.reshape(CLIPS, slots, 2 * D)
    text_pairs = lax.dynamic_index_in_dim(text_all, clip_here, axis=0, keepdims=False)
    done = [*pairs, *up_own]
    query_a = after(query_a, *done)
    grad_branch_moved = reorder(after(grad_branch_d, *done))
    count = len(pairs)
    keys = count * rows
    out_a, lse_a = run(
        functools.partial(spatial_kernel, count),
        [shape(rows, D, dtype=bf16), shape(HEADS, rows)],
        [vmem() for _ in range(1 + count)],
        [
            pltpu.VMEM((D, rows), f32),
            pltpu.VMEM((D, keys), f32),
            pltpu.VMEM((HEADS, keys, 128), bf16),
            pltpu.VMEM((D, rows), f32),
        ],
        (query_a, *pairs),
        18,
    )

    done = [out_a, text_pairs]
    out_a = after(out_a, *done)
    branch_a, after_a, hidden_b, query_b, out_b, after_b, hidden_c = run(
        functools.partial(text_kernel, win_rest, win_sout, win_cq, win_cout, nx),
        [
            shape(rows, D),
            shape(rows, D),
            shape(rows, D, dtype=bf16),
            shape(rows, D, dtype=bf16),
            shape(rows, D, dtype=bf16),
            shape(rows, D),
            shape(rows, D, dtype=bf16),
        ],
        [smem()] + [vmem(), vmem(), vmem(), hbm(), vmem(), smem()],
        [
            pltpu.VMEM((nx, D, win_rest.width), bf16),
            pltpu.SemaphoreType.DMA((nx,)),
            pltpu.VMEM((D, rows), f32),
            pltpu.VMEM((D, rows), f32),
            pltpu.VMEM((D, slots), f32),
        ],
        (me, tokens, out_a, mod, full_a, text_pairs, length_here),
        18,
    )

    done = [hidden_c, *up_near]
    done = get_up.new_core(*done)
    full_up = get_up.arrays()
    full_down = None if trees else gather_rows(after(w_down.T, *up_near))
    hidden_c = after(hidden_c, *done)
    pre_act, activated, branch_c, after_c, hidden_d = run(
        functools.partial(ff_kernel, win_up, nx, ny),
        [
            shape(rows, ff),
            shape(rows, ff, dtype=bf16),
            shape(rows, D),
            shape(rows, D),
            shape(rows, D, dtype=bf16),
        ],
        [smem()] + [vmem(), vmem(), vmem(), hbm(), hbm()],
        [
            pltpu.VMEM((nx, D, win_up.width), bf16),
            pltpu.VMEM((ny, D, ff_width), bf16),
            pltpu.SemaphoreType.DMA((nx,)),
            pltpu.SemaphoreType.DMA((ny,)),
        ],
        (me, hidden_c, after_b, mod, full_up, full_down),
        20,
    )

    rows_own = [hidden_a, out_a, hidden_b, out_b, hidden_c]
    rows_other = swap(after(jnp.stack(rows_own), hidden_d), "gx", 1)
    g_other = swap(after(activated, hidden_d), "gx", 1)
    moved_d = reorder(hidden_d)
    moved_d = after(moved_d, rows_other, g_other, grad_branch_moved)
    pad_width = max(win_tqkv.width, win_tout.width)
    grads_d, branch_moved, grad_hidden_moved = run(
        functools.partial(temporal_kernel, win_tqkv, win_tout, nx, frames),
        [
            shape(rows, 4 * D, dtype=bf16),
            shape(rows, D, dtype=bf16),
            shape(rows, D, dtype=bf16),
        ],
        [vmem(), vmem(), hbm(), vmem(), smem()],
        [
            pltpu.VMEM((nx, D, win_d.width), bf16),
            pltpu.SemaphoreType.DMA((nx,)),
            pltpu.VMEM((rows, pad_width), bf16),
        ]
        + [pltpu.VMEM((rows, D), f32)] * 8
        + [pltpu.VMEM((rows, 3 * D), bf16)],
        (moved_d, grad_branch_moved, full_d, row_clip, frame_clip),
        25,
    )
    grad_hidden_d = reorder(grad_hidden_moved)
    late = whole_grads(
        nx, [moved_d, grad_branch_moved, grads_d], [((0, 0, D), (2, D, 4 * D)), ((2, 0, D), (1, 0, D))]
    )
    late = scatter(after(late, grad_hidden_d), ("gx", "gy"))
    d_tqkv, d_tout = late[:, :n_sqkv], late[:, n_sqkv : n_sqkv + n_one]

    grads_c, grad_b, sums_c = run(
        functools.partial(ff_back_kernel, win_up, nx, ny),
        [
            shape(rows, ff + D, dtype=bf16),
            shape(rows, D),
            shape(8, D),
        ],
        [smem()] + [vmem()] * 7 + [hbm(), hbm()],
        [
            pltpu.VMEM((nx, D, win_up.width), bf16),
            pltpu.VMEM((ny, D, ff_width), bf16),
            pltpu.SemaphoreType.DMA((nx,)),
            pltpu.SemaphoreType.DMA((ny,)),
            pltpu.VMEM((rows, win_up.width), bf16),
        ],
        (me, grad_out, grad_hidden_d, after_c, after_b, pre_act, branch_c, mod, full_up, full_down),
        22,
    )
    branch_d = reorder(after(branch_moved, grad_hidden_d))
    grads_c = after(grads_c, branch_d)
    grads_other = swap(grads_c, "gx", 1)
    up_terms = up_grads(
        nx,
        me,
        [hidden_c, grads_c, activated],
        [rows_other[4], grads_other, g_other],
        trees,
    )
    if not trees:
        d_down = scatter(down_grads(grads_c[:, ff:], activated), row_axes).T
    up_sums = Scatter(*up_terms)
    up_first = up_sums.first()
    grad_b = after(grad_b, *up_terms)

    kv_width = w_ckv.shape[1]
    grads_b, grad_a, grad_out_a, text_terms, d_gate1 = run(
        functools.partial(text_back_kernel, win_rest, win_sout, win_cq, win_cout, nx),
        [
            shape(rows, 3 * D, dtype=bf16),
            shape(rows, D),
            shape(rows, D, dtype=bf16),
            shape(nx, slots, kv_width, dtype=bf16),
            shape(1, D),
        ],
        [smem()] + [vmem()] * 4 + [hbm(), vmem(), vmem(), smem()],
        [
            pltpu.VMEM((nx, D, win_rest.width), bf16),
            pltpu.SemaphoreType.DMA((nx,)),
            pltpu.VMEM((rows, max(w.width for w in (win_sout, win_cq, win_cout))), bf16),
            pltpu.VMEM((D, rows), f32),
            pltpu.VMEM((D, rows), f32),
            pltpu.VMEM((D, rows), f32),
            pltpu.VMEM((D, slots), f32),
            pltpu.VMEM((rows, D), bf16),
            pltpu.VMEM((slots, 2 * D), f32),
        ],
        (me, grad_b, after_a, branch_a, mod, full_a, query_b, text_pairs, length_here),
        20,
    )
    text_terms = jnp.where(clip_mark[None, :, None, None], text_terms[:, None], 0)

    done = [grad_out_a]
    grads_b_other = swap(grads_b, "gx", 1)
    text_terms = lax.psum_scatter(
        after(text_terms, late).reshape(nx, -1, kv_width), "gx", scatter_dimension=0, tiled=True
    )
    grad_out_a = after(grad_out_a, *done)

    grad_query_a, grad_pairs = run(
        functools.partial(spatial_back_kernel, count),
        [shape(rows, D, dtype=bf16), shape(count, rows, 2 * D, dtype=bf16)],
        [vmem() for _ in range(4 + count)],
        [pltpu.VMEM((D, rows), f32)] * 3
        + [pltpu.VMEM((D, keys), f32), pltpu.VMEM((D, rows), f32)]
        + [pltpu.VMEM((HEADS, rows, 128), bf16)] * 2
        + [pltpu.VMEM((HEADS, keys, 128), bf16)] * 4,
        (query_a, grad_out_a, out_a, lse_a, *pairs),
        28,
    )
    done = [grad_pairs, grads_b_other]
    grad_pairs = after(grad_pairs, *done)
    up_second = up_sums.second(*done)
    done = up_sums.sent
    bit = 1
    while bit < frame_devs // 2:
        half = grad_pairs.shape[0] // 2
        come = swap(grad_pairs[half:], "gx", bit)
        grad_pairs = (grad_pairs[:half].astype(f32) + come.astype(f32)).astype(bf16)
        bit *= 2
    come = swap(grad_pairs[1], "gx", bit)
    mixed, d_gate3 = run(
        mixed_kernel,
        [shape(rows, D, dtype=bf16), shape(1, D)],
        [vmem(), vmem(), vmem(), vmem(), smem()],
        [],
        (branch_d, after_c, grad_out, mod, keep_here),
        3,
    )

    cross = Scatter(
        *weight_grads(
            nx,
            me,
            [hidden_b, out_b, after(grads_b, grad_pairs, *done)],
            [rows_other[2], rows_other[3], grads_b_other],
            [((0, 0, D), (2, D, 2 * D)), ((1, 0, D), (2, 0, D))],
        )
    )
    done = [come, *cross.sent, *up_second]
    cross_first = cross.first(*done)
    up_sums.line(*done)
    up_done = up_sums.along(fars[2:])
    grad_query_a = after(grad_query_a, *done, *up_sums.ends)
    win = win_sqkv
    grads_a, grad_tokens, sums_a = run(
        functools.partial(qkv_back_kernel, win, nx),
        [shape(rows, 3 * D, dtype=bf16), shape(rows, D, dtype=bf16), shape(2, D)],
        [smem()] + [vmem()] * 6 + [hbm()],
        [
            pltpu.VMEM((nx, D, win.width), bf16),
            pltpu.SemaphoreType.DMA((nx,)),
            pltpu.VMEM((rows, win.width), bf16),
        ],
        (me, grad_query_a, grad_pairs[0], come, tokens, mod, grad_a, full_a),
        11,
    )
    grads_a_other = swap(grads_a, "gx", 1)
    early = Scatter(
        *weight_grads(
            nx,
            me,
            [hidden_a, out_a, grads_a, grads_b],
            [rows_other[0], rows_other[1], grads_a_other, grads_b_other],
            [((0, 0, D), (2, 0, 3 * D)), ((1, 0, D), (3, 2 * D, 3 * D))],
        )
    )
    done = [*cross_first, *early.sent]
    cross_second = cross.second(*done)
    done = [*cross_second, *up_done]
    up_done = up_done + up_sums.along(fars[:2])
    early_first = early.first(*done)
    cross.line(*done)
    cross_done = cross.along(fars, *up_done)
    done = [*early_first, *up_done]
    early_second = early.second(*done)
    early.line(*early_second)
    early_done = early.along(fars)
    grad_mod = jnp.concatenate(
        [sums_a, d_gate1, sums_c[3:5], sums_c[2:3], sums_c[0:2], d_gate3]
    ).reshape(-1)
    grad_mod = after(lax.all_gather(grad_mod, row_axes, axis=0), *early.ends)
    width = w_ada.shape[1]
    grad_mod = lax.dynamic_slice_in_dim(grad_mod, gx * width, width, axis=1)
    device_clip = jnp.sum(
        (clip_ends[None, :] <= (jnp.arange(devices) // frame_devs)[:, None]).astype(jnp.int32),
        axis=1,
    )
    device_pick = (jnp.arange(CLIPS)[:, None] == device_clip[None, :]).astype(f32)
    grad_mod = jnp.dot(device_pick, grad_mod, precision=highest)
    d_ada = lax.dot_general(
        cond_rows, grad_mod, (((0,), (0,)), ((), ())), precision=highest
    )
    text_terms = after(text_terms[0], *early_first).astype(f32)
    text_terms = text_terms + swap(text_terms.astype(bf16), "gy", 1).astype(f32)
    text_terms = text_terms + swap(text_terms.astype(bf16), "gy", 2).astype(f32)
    text_grad = text_terms.astype(bf16)
    d_ckv = jnp.einsum("rd,re->de", text_block, text_grad, preferred_element_type=f32)
    up, cross, early = up_sums.result(), cross.result(), early.result()
    d_up = up[:k_rows, :n_up]
    if trees:
        down = up[k_rows:]
        d_down = jnp.concatenate([down[:each], down[each:, : ff_width - fold]], axis=1).T
    d_cq, d_cout = cross[:, :n_one], cross[:, n_one : 2 * n_one]
    d_sqkv, d_sout = early[:, :n_sqkv], early[:, n_sqkv : n_sqkv + n_one]

    return (
        mixed,
        grad_tokens,
        d_ada,
        d_sqkv,
        d_sout,
        d_cq,
        d_ckv,
        d_cout,
        d_up,
        d_down,
        d_tqkv,
        d_tout,
    )


def solution(mesh):
    rows = P(("gy", "gx"), None)
    both = P("gy", "gx")
    return jax.shard_map(
        local,
        mesh=mesh,
        in_specs=(rows, rows, P(), P(), P(), P(), P()) + (both,) * 10 + (rows,),
        out_specs=(rows, rows) + (both,) * 10,
        check_vma=False,
    )
```
